32 devices in a mesh: gz: 8 (over y, x, core), gy: 4 (over z).
Axes of the slice: x: 2, y: 2, z: 4, core: 2. Of those that a mesh axis runs over, the one named last changes fastest.
Arguments:
- fields: bfloat16 [6, 64, 128, 256], P(None, 'gz', 'gy'), may hold values from -13 to 13
- target: bfloat16 [128, 32, 64, 128], P(None, 'gz', 'gy'), may hold values from -6 to 6
- conv_weight: bfloat16 [64, 162], replicated, may hold values from -0.5 to 0.5
- conv_bias: float32 [64], replicated, may hold values from -3 to 3
- down_weight: bfloat16 [128, 512], replicated, may hold values from -0.25 to 0.25
- down_bias: float32 [128], replicated, may hold values from -3 to 3
Outputs:
- out_field: bfloat16 [128, 32, 64, 128], P(None, 'gz', 'gy')
- sensitivity: float32 [6, 64, 128, 256], P(None, 'gz', 'gy')
- grad_conv: float32 [64, 162], replicated
- grad_conv_bias: float32 [64], replicated
- grad_down: float32 [128, 512], P('gz')
- grad_down_bias: float32 [128], replicated
- loss: float32 [], replicated
The draws below stay inside these ranges and needn't reach their ends.
All inputs are finite; a program needn't handle non-finite values.
Results may differ from the reference program's by a relative error of at most 0.0046.
Values may be sent and summed in bfloat16 or wider, within the bound.
No kernel may reach another device: no remote copies, remote signals or barrier semaphores. Data moves between devices by JAX's collectives and lax.ppermute only.
A program may use at most 192 MiB of HBM per device.

```python
import math
import jax
import jax.numpy as jnp
from jax import lax

C_IN = 6
HID = 64
OUT = 128
NX = 256
NZ = 64
NY = 128
CELLS2 = 262144


def draw_fields(key, part):
    key_base = jax.random.fold_in(key, 11)
    key_phase = jax.random.fold_in(key, 23)
    phases = jax.random.uniform(key_phase, (2,), minval=0.0, maxval=2.0 * math.pi)
    z_pos = jnp.arange(NZ, dtype=jnp.float32)[:, None]
    y_pos = jnp.arange(NY, dtype=jnp.float32)[None, :]
    waves = jnp.sin(2.0 * math.pi * z_pos / NZ + phases[0]) + jnp.sin(2.0 * math.pi * y_pos / NY + phases[1])
    base_draw = jnp.clip(jax.random.normal(key_base, (C_IN, NZ, NY, NX)), -4.0, 4.0)
    amplitude = jnp.exp(0.55 * waves)
    return (base_draw * amplitude[None, :, :, None]).astype(jnp.bfloat16)


def block_levels(stream_key, shape, cuts, least, top_value):
    level, own = 1.0, jax.random.fold_in(stream_key, 6)
    for dim, shards_of in cuts:
        draws = jnp.exp(jax.random.uniform(jax.random.fold_in(own, dim), (shards_of,), jnp.float32, least / len(cuts), top_value / len(cuts)))
        level = level * jnp.repeat(draws, shape[dim] // shards_of).reshape([-1 if axis == dim else 1 for axis in range(len(shape))])
    return level


def bell_draw(key, extent, scale, limit, cuts=(), held_as=jnp.bfloat16):
    drawn = jax.random.normal(key, extent, jnp.float32) * scale
    if len(cuts) > 0:
        drawn = block_levels(key, extent, cuts, -0.22, 0.18) * drawn
    return jnp.clip(drawn, min=-limit, max=limit).astype(held_as)


def setup_inputs(seed: int = 0) -> dict:
    seeds = jax.random.split(jax.random.key(seed), 7)
    return {
        "fields": draw_fields(jax.random.fold_in(seeds[6], 71), 0),
        "target": bell_draw(seeds[1], (OUT, NZ // 2, NY // 2, NX // 2), 1.0, 6.0, ((1, 8), (2, 4))),
        "conv_weight": bell_draw(seeds[2], (HID, C_IN * 27), (C_IN * 27) ** -0.5, 0.5),
        "conv_bias": bell_draw(seeds[3], (HID,), 0.5, 3.0, (), jnp.float32),
        "down_weight": bell_draw(seeds[4], (OUT, HID * 8), (HID * 8) ** -0.5, 0.25),
        "down_bias": bell_draw(seeds[5], (OUT,), 0.5, 3.0, (), jnp.float32),
    }


gelu_scale = 0.7978845608028654
gelu_cubic = 0.044715


def gelu_parts(inputs):
    inner_arg = gelu_scale * (inputs + gelu_cubic * inputs * inputs * inputs)
    tangent = jnp.tanh(inner_arg)
    result = 0.5 * inputs * (1.0 + tangent)
    slopes = 0.5 * (1.0 + tangent) + 0.5 * inputs * (1.0 - tangent * tangent) * gelu_scale * (1.0 + 3.0 * gelu_cubic * inputs * inputs)
    return result, slopes


def to_blocks(hidden):
    channels, planes_count, row_count, col_count = hidden.shape
    split = hidden.reshape(channels, 2, row_count // 2, 2, col_count // 2, 2)
    return split.transpose(0, 1, 3, 5, 2, 4).reshape(channels * 8, (row_count // 2) * (col_count // 2))


def from_blocks(blocks, channels, row_count, col_count):
    split = blocks.reshape(channels, 2, 2, 2, row_count // 2, col_count // 2)
    return split.transpose(0, 1, 4, 2, 5, 3).reshape(channels, 2, row_count, col_count)


def column_block(planes):
    pieces = []
    for off_z in range(3):
        for off_y in range(3):
            for off_x in range(3):
                shifted = planes[:, off_z:off_z + 2]
                shifted = jnp.roll(shifted, 1 - off_y, axis=2)
                shifted = jnp.roll(shifted, 1 - off_x, axis=3)
                pieces.append(shifted)
    stacked = jnp.stack(pieces, axis=1)
    return stacked.reshape(C_IN * 27, 2 * NY * NX)


def reference(fields, target, conv_weight, conv_bias, down_weight, down_bias):
    plane_offsets = jnp.arange(4, dtype=jnp.int32)

    def pair_step(state_tuple, pair_index):
        grad_conv, grad_cbias, grad_down, grad_dbias, square_sum, sensitivity = state_tuple
        plane_index = (2 * pair_index - 1 + plane_offsets) % NZ
        planes = jnp.take(fields, plane_index, axis=1)
        columns = column_block(planes)
        pre_act = jnp.dot(conv_weight, columns, preferred_element_type=jnp.float32) + conv_bias[:, None]
        activated, slopes = gelu_parts(pre_act)
        hidden = activated.astype(jnp.bfloat16)
        blocks = to_blocks(hidden.reshape(HID, 2, NY, NX))
        output = jnp.dot(down_weight, blocks, preferred_element_type=jnp.float32) + down_bias[:, None]
        wanted = lax.dynamic_index_in_dim(target, pair_index, 1, keepdims=False).reshape(OUT, -1).astype(jnp.float32)
        diff_value = output - wanted
        grad_out = diff_value.astype(jnp.bfloat16)
        grad_down = grad_down + jnp.dot(grad_out, blocks.T, preferred_element_type=jnp.float32)
        grad_dbias = grad_dbias + jnp.sum(diff_value, axis=1)
        back_hidden = jnp.dot(down_weight.T, grad_out, preferred_element_type=jnp.float32)
        back_hidden = from_blocks(back_hidden, HID, NY, NX).reshape(HID, 2 * NY * NX)
        grad_pre = (back_hidden * slopes).astype(jnp.bfloat16)
        grad_conv = grad_conv + jnp.dot(grad_pre, columns.T, preferred_element_type=jnp.float32)
        grad_cbias = grad_cbias + jnp.sum(grad_pre.astype(jnp.float32), axis=1)
        square_sum = square_sum + jnp.sum(diff_value * diff_value)
        spread = jnp.dot(conv_weight.T, grad_pre, preferred_element_type=jnp.float32).reshape(C_IN, 3, 3, 3, 2, NY, NX)
        window = jnp.zeros((C_IN, 4, NY, NX), jnp.float32)
        for off_z in range(3):
            for off_y in range(3):
                for off_x in range(3):
                    shifted = jnp.roll(spread[:, off_z, off_y, off_x], off_y - 1, axis=2)
                    shifted = jnp.roll(shifted, off_x - 1, axis=3)
                    window = window.at[:, off_z:off_z + 2].add(shifted)
        sensitivity = sensitivity.at[:, plane_index].add(window)
        new_state = (grad_conv, grad_cbias, grad_down, grad_dbias, square_sum, sensitivity)
        return new_state, output.astype(jnp.bfloat16).reshape(OUT, NY // 2, NX // 2)

    start_state = (jnp.zeros((HID, C_IN * 27), jnp.float32), jnp.zeros((HID,), jnp.float32),
                   jnp.zeros((OUT, HID * 8), jnp.float32), jnp.zeros((OUT,), jnp.float32),
                   jnp.zeros((), jnp.float32), jnp.zeros((C_IN, NZ, NY, NX), jnp.float32))
    final_state, outputs = lax.scan(pair_step, start_state, jnp.arange(NZ // 2, dtype=jnp.int32))
    grad_conv, grad_cbias, grad_down, grad_dbias, square_sum, sensitivity = final_state
    out_field = jnp.transpose(outputs, (1, 0, 2, 3))
    return (out_field, sensitivity, grad_conv / CELLS2, grad_cbias / CELLS2,
            grad_down / CELLS2, grad_dbias / CELLS2, square_sum / (OUT * CELLS2))
```

```python
import functools

import jax
import jax.numpy as jnp
import numpy as np
from jax import lax
from jax.experimental import pallas as pl
from jax.experimental.pallas import tpu as pltpu
from jax.sharding import PartitionSpec as P

gelu_scale = 0.7978845608028654
gelu_cubic = 0.044715
lanes = 128
bf16 = jnp.bfloat16
f32 = jnp.float32


def shifted(value, axis, by):
    count = lax.axis_size(axis)
    return lax.ppermute(value, axis, [(i, (i + by) % count) for i in range(count)])


def exchanged(value, axis, bit):
    count = lax.axis_size(axis)
    return lax.ppermute(value, axis, [(i, i ^ bit) for i in range(count)])


def column_spread(half_cols):
    spread = np.zeros((2 * half_cols, 4 * half_cols), np.float32)
    for step in range(2):
        for par in range(2):
            for col in range(half_cols):
                source = (2 * ((col + step) % half_cols) + par - 1) % (2 * half_cols)
                spread[source, (2 * step + par) * half_cols + col] = 1
    return spread


def column_merge(half_cols):
    merge = np.zeros((2 * half_cols, 2 * half_cols), np.float32)
    for par in range(2):
        for col in range(half_cols):
            merge[par * half_cols + col, (2 * col + par - 1) % (2 * half_cols)] = 1
    return merge


def row_spread(channels, pair_rows, row_pad):
    spread = np.zeros((pair_rows * 4 * channels, 2 * channels * row_pad), np.float32)
    for row in range(pair_rows):
        for par_z in range(2):
            for par_y in range(2):
                for ch in range(channels):
                    target = ((row * 2 + par_z) * 2 + par_y) * channels + ch
                    spread[target, (par_z * channels + ch) * row_pad + 2 * row + par_y] = 1
    return spread


def tap_spread(channels):
    spread = np.zeros((8, channels * 27, 64 * channels), np.float32)
    for cls in range(8):
        par_z, par_y, par_x = cls // 4, cls // 2 % 2, cls % 2
        for ch in range(channels):
            for off_z in range(3):
                for off_y in range(3):
                    for off_x in range(3):
                        at_z, at_y, at_x = par_z + off_z, par_y + off_y, par_x + off_x
                        place = (at_z // 2 * 2 + at_y // 2) * 2 + at_x // 2
                        place = ((place * 2 + at_x % 2) * 2 + at_z % 2) * 2 + at_y % 2
                        spread[cls, ch * 27 + 9 * off_z + 3 * off_y + off_x, place * channels + ch] = 1
    return spread


def dot(a, b):
    return jnp.dot(a, b, preferred_element_type=f32)


def dot_rows(a, b):
    return lax.dot_general(a, b, (((1,), (1,)), ((), ())), preferred_element_type=f32)


def split_two(value):
    high = value.astype(bf16)
    return high, (value - high.astype(f32)).astype(bf16)


def block_kernel(
    sizes,
    field_ref,
    target_ref,
    conv_ref,
    conv_t_ref,
    cbias_ref,
    down_ref,
    down_t_ref,
    dbias_ref,
    col_ref,
    merge_ref,
    row_ref,
    row_t_ref,
    tap_ref,
    out_ref,
    acc_ref,
    gdown_ref,
    small_ref,
    split_ref,
    spread_ref,
    hid_ref,
    slope_ref,
    gpre_ref,
    gconv_ref,
    gcb_ref,
    gdb_ref,
    sq_ref,
):
    channels, pairs, pair_rows, row_pad, width, hidden, tile = sizes
    group = 4 * channels
    span = 4 * group
    step_z, step_y = pl.program_id(0), pl.program_id(1)
    last = (step_z == pairs - 1) & (step_y == pl.num_programs(1) - 1)

    @pl.when((step_z == 0) & (step_y == 0))
    def _():
        gdown_ref[...] = jnp.zeros_like(gdown_ref)
        gconv_ref[...] = jnp.zeros_like(gconv_ref)
        gcb_ref[...] = jnp.zeros_like(gcb_ref)
        gdb_ref[...] = jnp.zeros_like(gdb_ref)
        sq_ref[...] = jnp.zeros_like(sq_ref)
        spread_ref[...] = jnp.zeros_like(spread_ref)

        @pl.loop(0, pairs + 1)
        def _(slot):
            planes = [field_ref[ch, 2 * slot + par] for par in range(2) for ch in range(channels)]
            rows = jnp.concatenate(planes, axis=0)
            rows = dot(rows, col_ref[...]).astype(bf16)
            rows = dot(row_ref[...], rows)
            for row in range(pair_rows):
                piece = [
                    rows[row * group : (row + 1) * group, v * lanes : (v + 1) * lanes]
                    for v in range(4)
                ]
                split_ref[slot, :, row * lanes : (row + 1) * lanes] = jnp.concatenate(
                    piece, axis=0
                ).astype(bf16)

    for part in range(width // tile):
        here = slice(part * tile, (part + 1) * tile)
        base = step_y * width + part * tile

        def cells(dy):
            return pl.ds(pl.multiple_of(base + dy * lanes, lanes), tile)

        window = jnp.concatenate(
            [split_ref[step_z + dz, :, cells(dy)] for dz in range(2) for dy in range(2)], axis=0
        )
        pre = dot(conv_ref[...], window)
        pre = pre + jnp.concatenate([cbias_ref[...]] * (tile // lanes), axis=1)
        square = pre * pre
        tangent = jnp.tanh(pre * (square * (gelu_scale * gelu_cubic) + gelu_scale))
        half = 0.5 * tangent + 0.5
        hid = (pre * half).astype(bf16)
        bend = pre * (square * (6.0 * gelu_scale * gelu_cubic) + 2.0 * gelu_scale)
        slope = half * (bend * (1.0 - half)) + half
        output = dot(down_ref[...], hid)
        output = output + jnp.concatenate([dbias_ref[...]] * (tile // lanes), axis=1)
        diff = output - target_ref[0, :, here].astype(f32)
        out_ref[0, :, here] = output.astype(bf16)
        grad_out = diff.astype(bf16)
        gdown_ref[...] += dot_rows(grad_out, hid)
        for k in range(tile // lanes):
            piece = diff[:, k * lanes : (k + 1) * lanes]
            gdb_ref[...] += piece
            sq_ref[...] += piece * piece
        back = dot(down_t_ref[...], grad_out)
        grad_pre = (back * slope).astype(bf16)
        for k in range(tile // lanes):
            gcb_ref[...] += grad_pre[:, k * lanes : (k + 1) * lanes].astype(f32)
        gconv_ref[...] += dot_rows(grad_pre, window)
        spread = dot(conv_t_ref[...], grad_pre)
        for dz in range(2):
            for dy in range(2):
                at = (2 * dz + dy) * span
                spread_ref[step_z + dz, :, cells(dy)] += spread[at : at + span]

    @pl.when(last)
    def _():
        @pl.loop(0, pairs + 1)
        def _(slot):
            rows = []
            for row in range(pair_rows):
                piece = spread_ref[slot, :, row * lanes : (row + 1) * lanes]
                rows.append(
                    jnp.concatenate(
                        [
                            piece[par * group : (par + 1) * group]
                            + pltpu.roll(piece[(2 + par) * group : (3 + par) * group], 1, 1)
                            for par in range(2)
                        ],
                        axis=1,
                    )
                )
            total = 0.0
            for value in split_two(jnp.concatenate(rows, axis=0)):
                moved = dot(row_t_ref[...], value).astype(bf16)
                total = total + dot(moved, merge_ref[...])
            for par in range(2):
                for ch in range(channels):
                    at = (par * channels + ch) * row_pad
                    acc_ref[ch, 2 * slot + par] = total[at : at + row_pad]

        taps = channels * 27
        folded = jnp.zeros((hidden, taps), f32)
        cb = jnp.zeros((hidden, lanes), f32)
        for cls in range(8):
            rows = gconv_ref[cls * hidden : (cls + 1) * hidden]
            high, rest = split_two(rows)
            low, least = split_two(rows - high.astype(f32))
            tap = tap_ref[cls]
            folded = folded + (dot_rows(high, tap) + dot_rows(low, tap) + dot_rows(least, tap))
            cb = cb + gcb_ref[cls * hidden : (cls + 1) * hidden]
        small_ref[:, :taps] = folded
        columns = [jnp.sum(cb, axis=1, keepdims=True)]
        for ref in (gdb_ref, sq_ref):
            whole = jnp.sum(ref[...], axis=1, keepdims=True)
            columns += [whole[:hidden], whole[hidden:]]
        columns.append(jnp.zeros((hidden, small_ref.shape[1] - taps - 5), f32))
        small_ref[:, taps:] = jnp.concatenate(columns, axis=1)


def on_device(fields, target, conv_weight, conv_bias, down_weight, down_bias):
    channels, depth, row_count, col_count = fields.shape
    hidden = conv_weight.shape[0]
    out_count = down_weight.shape[0]
    pairs, half_rows, half_cols = depth // 2, row_count // 2, col_count // 2
    pair_rows = half_rows + 1
    row_pad = -(-(row_count + 2) // 16) * 16
    taps = channels * 27
    big = 8 * hidden
    win = 64 * channels
    cells = half_rows * half_cols
    cell_total = pairs * cells * lax.axis_size("gz") * lax.axis_size("gy")
    width, tile = 1024, 256

    before = shifted(fields[:, :, row_count - 1 :], "gy", 1)
    after = shifted(fields[:, :, :1], "gy", -1)
    blank = jnp.zeros((channels, depth, row_pad - row_count - 2, col_count), bf16)
    rows = jnp.concatenate([before, fields, after, blank], axis=2)
    below = shifted(rows[:, depth - 1 :], "gz", 1)
    above = shifted(rows[:, :1], "gz", -1)
    padded = jnp.concatenate([below, rows, above], axis=1)

    col = jnp.asarray(column_spread(half_cols), bf16)
    merge = jnp.asarray(column_merge(half_cols), bf16)
    row_np = row_spread(channels, pair_rows, row_pad)
    row = jnp.asarray(row_np, bf16)
    row_t = jnp.asarray(row_np.T, bf16)
    tap = jnp.asarray(tap_spread(channels), bf16)
    conv_big = jnp.concatenate([dot(conv_weight, tap[cls]) for cls in range(8)], axis=0).astype(bf16)
    conv_big_t = conv_big.T
    cbias = jnp.broadcast_to(jnp.tile(conv_bias, 8)[:, None], (big, lanes))
    dbias = jnp.broadcast_to(down_bias[:, None], (out_count, lanes))
    down = down_weight.reshape(out_count, hidden, 8).transpose(0, 2, 1).reshape(out_count, big)
    down_t = down.T
    wanted = target.transpose(1, 0, 2, 3).reshape(pairs, out_count, cells)

    sizes = (channels, pairs, pair_rows, row_pad, width, hidden, tile)
    whole = lambda *shape: pl.BlockSpec(shape, lambda z, y: (0,) * len(shape))
    out, accum, grad_down, small = pl.pallas_call(
        functools.partial(block_kernel, sizes),
        grid=(pairs, cells // width),
        in_specs=[
            whole(channels, depth + 2, row_pad, col_count),
            pl.BlockSpec((1, out_count, width), lambda z, y: (z, 0, y)),
            whole(big, win),
            whole(win, big),
            whole(big, lanes),
            whole(out_count, big),
            whole(big, out_count),
            whole(out_count, lanes),
            whole(*col.shape),
            whole(*merge.shape),
            whole(*row.shape),
            whole(*row_t.shape),
            whole(*tap.shape),
        ],
        out_specs=[
            pl.BlockSpec((1, out_count, width), lambda z, y: (z, 0, y)),
            whole(channels, depth + 2, row_pad, col_count),
            whole(out_count, big),
            whole(hidden, 256),
        ],
        out_shape=[
            jax.ShapeDtypeStruct((pairs, out_count, cells), bf16),
            jax.ShapeDtypeStruct((channels, depth + 2, row_pad, col_count), f32),
            jax.ShapeDtypeStruct((out_count, big), f32),
            jax.ShapeDtypeStruct((hidden, 256), f32),
        ],
        scratch_shapes=[
            pltpu.VMEM((pairs + 1, 16 * channels, pair_rows * lanes), bf16),
            pltpu.VMEM((pairs + 1, 16 * channels, pair_rows * lanes), f32),
            pltpu.VMEM((big, width), bf16),
            pltpu.VMEM((big, width), f32),
            pltpu.VMEM((big, width), bf16),
            pltpu.VMEM((big, win), f32),
            pltpu.VMEM((big, lanes), f32),
            pltpu.VMEM((out_count, lanes), f32),
            pltpu.VMEM((out_count, lanes), f32),
        ],
        compiler_params=pltpu.CompilerParams(vmem_limit_bytes=56 * 1024 * 1024),
        name="down_block",
    )(padded, wanted, conv_big, conv_big_t, cbias, down, down_t, dbias, col, merge, row, row_t, tap)
    out_field = out.reshape(pairs, out_count, half_rows, half_cols).transpose(1, 0, 2, 3)

    from_above = shifted(accum[:, 0].astype(bf16), "gz", -1).astype(f32)
    from_below = shifted(accum[:, depth + 1].astype(bf16), "gz", 1).astype(f32)
    core = accum[:, 1 : depth + 1]
    core = core.at[:, depth - 1].add(from_above)
    core = core.at[:, 0].add(from_below)
    from_right = shifted(core[:, :, 0].astype(bf16), "gy", -1).astype(f32)
    from_left = shifted(core[:, :, row_count + 1].astype(bf16), "gy", 1).astype(f32)
    sensitivity = core[:, :, 1 : row_count + 1]
    sensitivity = sensitivity.at[:, :, row_count - 1].add(from_right)
    sensitivity = sensitivity.at[:, :, 0].add(from_left)

    def beside(value, count):
        return jnp.concatenate(jnp.split(value, value.shape[0] // count, axis=0), axis=1)

    me = lax.axis_index("gz")
    own = grad_down
    bit = lax.axis_size("gz")
    bits = []
    while bit > 1:
        bit //= 2
        bits.append(bit)
    for bit in bits:
        count = own.shape[0] // 2
        upper = (me // bit) % 2
        keep = lax.dynamic_slice_in_dim(own, upper * count, count, 0)
        give = lax.dynamic_slice_in_dim(own, (1 - upper) * count, count, 0)
        packed = jnp.concatenate([give, beside(small, count) if count < hidden else small], axis=1)
        got = exchanged(packed, "gz", bit)
        own = keep + got[:, :big]
        small = small + jnp.concatenate(
            jnp.split(got[:, big:], hidden // count, axis=1), axis=0
        )
    bit = 1
    count = own.shape[0]
    packed = jnp.concatenate([own, beside(small, count)], axis=1)
    while bit < lax.axis_size("gy"):
        packed = packed + exchanged(packed, "gy", bit)
        bit *= 2
    own = packed[:, :big]
    small = jnp.concatenate(jnp.split(packed[:, big:], hidden // count, axis=1), axis=0)
    down_rows = own.reshape(count, 8, hidden).transpose(0, 2, 1).reshape(count, big)
    return (
        out_field,
        sensitivity,
        small[:, :taps] / cell_total,
        small[:, taps] / cell_total,
        down_rows / cell_total,
        jnp.concatenate([small[:, taps + 1], small[:, taps + 2]]) / cell_total,
        jnp.sum(small[:, taps + 3 : taps + 5]) / (out_count * cell_total),
    )


def solution(mesh):
    in_specs = (P(None, "gz", "gy", None), P(None, "gz", "gy", None), P(), P(), P(), P())
    out_specs = (
        P(None, "gz", "gy", None),
        P(None, "gz", "gy", None),
        P(),
        P(),
        P("gz", None),
        P(),
        P(),
    )
    return jax.shard_map(
        on_device, mesh=mesh, in_specs=in_specs, out_specs=out_specs, check_vma=False
    )
```

```python
import functools

import jax
import jax.numpy as jnp
import numpy as np
from jax import lax
from jax.experimental import pallas as pl
from jax.experimental.pallas import tpu as pltpu
from jax.sharding import PartitionSpec as P

gelu_scale = 0.7978845608028654
gelu_cubic = 0.044715
lanes = 128
bf16 = jnp.bfloat16
f32 = jnp.float32


def shifted(value, axis, by):
    count = lax.axis_size(axis)
    return lax.ppermute(value, axis, [(i, (i + by) % count) for i in range(count)])


def exchanged(value, axis, bit):
    count = lax.axis_size(axis)
    return lax.ppermute(value, axis, [(i, i ^ bit) for i in range(count)])


def column_spread(half_cols):
    spread = np.zeros((2 * half_cols, 4 * half_cols), np.float32)
    for step in range(2):
        for par in range(2):
            for col in range(half_cols):
                source = (2 * ((col + step) % half_cols) + par - 1) % (2 * half_cols)
                spread[source, (2 * step + par) * half_cols + col] = 1
    return spread


def column_merge(half_cols):
    merge = np.zeros((2 * half_cols, 2 * half_cols), np.float32)
    for par in range(2):
        for col in range(half_cols):
            merge[par * half_cols + col, (2 * col + par - 1) % (2 * half_cols)] = 1
    return merge


def row_spread(channels, row_count):
    pair_rows = row_count // 2 + 1
    core = np.zeros((pair_rows * 4 * channels, 2 * channels * row_count), np.float32)
    edge = np.zeros((8 * channels, 32), np.float32)
    for par_z in range(2):
        for ch in range(channels):
            for at in range(1, row_count + 1):
                target = ((at // 2 * 2 + par_z) * 2 + at % 2) * channels + ch
                core[target, (par_z * channels + ch) * row_count + at - 1] = 1
            edge[(par_z * 2) * channels + ch, par_z * 16 + ch] = 1
            edge[((2 + par_z) * 2 + 1) * channels + ch, par_z * 16 + 8 + ch] = 1
    return core, edge


def tap_spread(channels):
    spread = np.zeros((8, channels * 27, 64 * channels), np.float32)
    for cls in range(8):
        par_z, par_y, par_x = cls // 4, cls // 2 % 2, cls % 2
        for ch in range(channels):
            for off_z in range(3):
                for off_y in range(3):
                    for off_x in range(3):
                        at_z, at_y, at_x = par_z + off_z, par_y + off_y, par_x + off_x
                        place = (at_z // 2 * 2 + at_y // 2) * 2 + at_x // 2
                        place = ((place * 2 + at_x % 2) * 2 + at_z % 2) * 2 + at_y % 2
                        spread[cls, ch * 27 + 9 * off_z + 3 * off_y + off_x, place * channels + ch] = 1
    return spread


def class_order(hidden):
    order = np.zeros((8 * hidden, 8 * hidden), np.float32)
    for ch in range(hidden):
        for cls in range(8):
            order[ch * 8 + cls, cls * hidden + ch] = 1
    return order


def dot(a, b):
    return jnp.dot(a, b, preferred_element_type=f32)


def dot_rows(a, b):
    return lax.dot_general(a, b, (((1,), (1,)), ((), ())), preferred_element_type=f32)


def split_two(value):
    high = value.astype(bf16)
    return high, (value - high.astype(f32)).astype(bf16)


def split_three(value):
    high = value.astype(bf16)
    return (high,) + split_two(value - high.astype(f32))


def conv_rows(conv_ref, tap_ref):
    return jnp.concatenate([dot(conv_ref[...], tap_ref[cls]) for cls in range(8)], axis=0)


def row_of(ref, count):
    return jnp.transpose(jnp.broadcast_to(ref[...], (lanes, count)))


def forward_kernel(
    sizes,
    field_ref,
    below_ref,
    above_ref,
    before_ref,
    after_ref,
    target_ref,
    conv_weight_ref,
    conv_bias_ref,
    down_weight_ref,
    down_bias_ref,
    tap_ref,
    order_ref,
    col_ref,
    row_ref,
    edge_ref,
    out_ref,
    gpre_ref,
    gdown_ref,
    small_ref,
    split_ref,
    conv_ref,
    down_ref,
    down_t_ref,
    gconv_ref,
    gcb_ref,
    gdb_ref,
    sq_ref,
):
    channels, pairs, half_rows, hidden, out_count, tile = sizes
    group = 4 * channels
    cells = half_rows * lanes
    step = pl.program_id(0)

    @pl.when(step == 0)
    def _():
        gdown_ref[...] = jnp.zeros_like(gdown_ref)
        gconv_ref[...] = jnp.zeros_like(gconv_ref)
        gcb_ref[...] = jnp.zeros_like(gcb_ref)
        gdb_ref[...] = jnp.zeros_like(gdb_ref)
        sq_ref[...] = jnp.zeros_like(sq_ref)
        conv_ref[...] = conv_rows(conv_weight_ref, tap_ref).astype(bf16)
        down = dot(down_weight_ref[...], order_ref[...])
        down_ref[...] = down.astype(bf16)
        down_t_ref[...] = jnp.transpose(down).astype(bf16)
        for slot in range(pairs + 1):
            lower = below_ref if slot == 0 else field_ref.at[:, 2 * slot - 1]
            upper = above_ref if slot == pairs else field_ref.at[:, 2 * slot]
            rows = [ref[ch] for ref in (lower, upper) for ch in range(channels)]
            rows = dot(jnp.concatenate(rows, axis=0), col_ref[...]).astype(bf16)
            rows = dot(row_ref[...], rows)
            sides = [ref[2 * slot + par].astype(f32) for par in range(2) for ref in (before_ref, after_ref)]
            sides = jnp.concatenate(sides, axis=0).astype(bf16)
            sides = dot(edge_ref[...], dot(sides, col_ref[...]).astype(bf16))
            for row in range(half_rows + 1):
                piece = rows[row * group : (row + 1) * group]
                if row == 0:
                    piece = piece + sides[:group]
                if row == half_rows:
                    piece = piece + sides[group:]
                piece = [piece[:, v * lanes : (v + 1) * lanes] for v in range(4)]
                split_ref[slot, :, row * lanes : (row + 1) * lanes] = jnp.concatenate(
                    piece, axis=0
                ).astype(bf16)

    conv_bias = row_of(conv_bias_ref, hidden)
    conv_bias = jnp.concatenate([conv_bias] * 8, axis=0)
    conv_bias = jnp.concatenate([conv_bias] * (tile // lanes), axis=1)
    down_bias = row_of(down_bias_ref, out_count)
    down_bias = jnp.concatenate([down_bias] * (tile // lanes), axis=1)
    wanted = jnp.swapaxes(target_ref[:, 0].astype(f32), 0, 1)
    outputs = []
    for part in range(cells // tile):
        here = slice(part * tile, (part + 1) * tile)
        window = jnp.concatenate(
            [
                split_ref[step + dz, :, part * tile + dy * lanes : (part + 1) * tile + dy * lanes]
                for dz in range(2)
                for dy in range(2)
            ],
            axis=0,
        )
        pre = dot(conv_ref[...], window) + conv_bias
        square = pre * pre
        tangent = jnp.tanh(pre * (square * (gelu_scale * gelu_cubic) + gelu_scale))
        half = 0.5 * tangent + 0.5
        hid = (pre * half).astype(bf16)
        bend = pre * (square * (6.0 * gelu_scale * gelu_cubic) + 2.0 * gelu_scale)
        slope = half * (bend * (1.0 - half)) + half
        output = dot(down_ref[...], hid) + down_bias
        outputs += [output[:, k * lanes : (k + 1) * lanes] for k in range(tile // lanes)]
        first = part * tile // lanes
        diff = output - jnp.concatenate([wanted[first + k] for k in range(tile // lanes)], axis=1)
        grad_out = diff.astype(bf16)
        gdown_ref[...] += dot_rows(grad_out, hid)
        for k in range(tile // lanes):
            piece = diff[:, k * lanes : (k + 1) * lanes]
            gdb_ref[...] += piece
            sq_ref[...] += piece * piece
        back = dot(down_t_ref[...], grad_out)
        grad_pre = (back * slope).astype(bf16)
        gpre_ref[0, :, here] = grad_pre
        for k in range(tile // lanes):
            gcb_ref[...] += grad_pre[:, k * lanes : (k + 1) * lanes].astype(f32)
        gconv_ref[...] += dot_rows(grad_pre, window)
    out_ref[:, 0] = jnp.swapaxes(jnp.stack(outputs, axis=0), 0, 1).astype(bf16)

    @pl.when(step == pairs - 1)
    def _():
        taps = channels * 27
        folded = jnp.zeros((hidden, taps), f32)
        cb = jnp.zeros((hidden, lanes), f32)
        for cls in range(8):
            tap = tap_ref[cls]
            for piece in split_three(gconv_ref[cls * hidden : (cls + 1) * hidden]):
                folded = folded + dot_rows(piece, tap)
            cb = cb + gcb_ref[cls * hidden : (cls + 1) * hidden]
        small_ref[:, :taps] = folded
        columns = [jnp.sum(cb, axis=1, keepdims=True)]
        for ref in (gdb_ref, sq_ref):
            whole = jnp.sum(ref[...], axis=1, keepdims=True)
            columns += [whole[:hidden], whole[hidden:]]
        columns.append(jnp.zeros((hidden, small_ref.shape[1] - taps - 5), f32))
        small_ref[:, taps:] = jnp.concatenate(columns, axis=1)


def spread_kernel(
    sizes,
    gpre_ref,
    conv_weight_ref,
    tap_ref,
    merge_ref,
    row_t_ref,
    edge_t_ref,
    sens_ref,
    below_ref,
    above_ref,
    before_ref,
    after_ref,
    spread_ref,
    conv_t_ref,
):
    channels, pairs, half_rows, tile = sizes
    group = 4 * channels
    span = 4 * group
    row_count = 2 * half_rows
    cells = half_rows * lanes
    step = pl.program_id(0)

    @pl.when(step == 0)
    def _():
        spread_ref[...] = jnp.zeros_like(spread_ref)
        conv_t_ref[...] = jnp.transpose(conv_rows(conv_weight_ref, tap_ref)).astype(bf16)

    for part in range(cells // tile):
        spread = dot(conv_t_ref[...], gpre_ref[0, :, part * tile : (part + 1) * tile])
        for dz in range(2):
            for dy in range(2):
                at = (2 * dz + dy) * span
                here = slice(part * tile + dy * lanes, (part + 1) * tile + dy * lanes)
                spread_ref[step + dz, :, here] += spread[at : at + span]

    def finish(slot, store):
        rows = []
        for row in range(half_rows + 1):
            piece = spread_ref[slot, :, row * lanes : (row + 1) * lanes]
            halves = [
                piece[par * group : (par + 1) * group]
                + pltpu.roll(piece[(2 + par) * group : (3 + par) * group], 1, 1)
                for par in range(2)
            ]
            rows.append(jnp.concatenate(halves, axis=1))
        core, sides = 0.0, 0.0
        outer = jnp.concatenate([rows[0], rows[half_rows]], axis=0)
        for value in split_two(jnp.concatenate(rows, axis=0)):
            core = core + dot(dot(row_t_ref[...], value).astype(bf16), merge_ref[...])
        for value in split_two(outer):
            sides = sides + dot(dot(edge_t_ref[...], value).astype(bf16), merge_ref[...])
        for par in range(2):
            before_ref[2 * slot + par] = sides[par * 16 : par * 16 + 8].astype(bf16)
            after_ref[2 * slot + par] = sides[par * 16 + 8 : par * 16 + 16].astype(bf16)
            for ch in range(channels):
                at = (par * channels + ch) * row_count
                store(2 * slot + par, ch, core[at : at + row_count])

    def store_first(at, ch, value):
        if at == 0:
            below_ref[ch] = value.astype(bf16)
        else:
            sens_ref[ch, at - 1] = value

    def store_middle(at, ch, value):
        sens_ref[ch, at - 1] = value

    def store_last(at, ch, value):
        if at == 2 * pairs + 1:
            above_ref[ch] = value.astype(bf16)
        else:
            sens_ref[ch, at - 1] = value

    @pl.when(step == 0)
    def _():
        finish(0, store_first)

    @pl.when(step > 0)
    def _():
        finish(step, store_middle)

    @pl.when(step == pairs - 1)
    def _():
        finish(pairs, store_last)


def join_kernel(sizes, sens_ref, below_ref, above_ref, before_ref, after_ref, out_ref):
    channels, depth, row_count = sizes
    out_ref[...] = sens_ref[...]
    for ch in range(channels):
        for z in range(depth):
            out_ref[ch, z, 0:1] += after_ref[z + 1, ch : ch + 1].astype(f32)
            out_ref[ch, z, row_count - 1 : row_count] += before_ref[z + 1, ch : ch + 1].astype(f32)
        out_ref[ch, 0] += above_ref[ch].astype(f32)
        out_ref[ch, depth - 1] += below_ref[ch].astype(f32)


def last_kernel(sizes, small_ref, down_ref, order_ref, conv_out, cbias_out, down_out, dbias_out, loss_out):
    hidden, taps, cell_total, out_count = sizes
    scale = 1.0 / cell_total
    small = small_ref[...]
    conv_out[...] = small[:, :taps] * scale
    turned = jnp.transpose(small[:, lanes : 2 * lanes])
    at = taps - lanes
    cbias_out[...] = turned[at : at + 1] * scale
    dbias_out[...] = jnp.concatenate([turned[at + 1 : at + 2], turned[at + 2 : at + 3]], axis=1) * scale
    squares = jnp.sum(turned[at + 3 : at + 4] + turned[at + 4 : at + 5], axis=1, keepdims=True)
    loss_out[...] = squares * (scale / out_count)
    rows = 0.0
    for piece in split_three(down_ref[...]):
        rows = rows + dot_rows(piece, order_ref[...])
    down_out[...] = rows * scale


def call(kernel, sizes, out_shape, *args, grid=None, in_specs=None, out_specs=None, scratch=(), flops=0, name):
    if grid is None:
        in_specs = [pl.BlockSpec(memory_space=pltpu.VMEM)] * len(args)
        out_specs = [pl.BlockSpec(memory_space=pltpu.VMEM)] * len(out_shape)
    return pl.pallas_call(
        functools.partial(kernel, sizes),
        out_shape=out_shape,
        in_specs=in_specs,
        out_specs=out_specs,
        scratch_shapes=scratch,
        compiler_params=pltpu.CompilerParams(vmem_limit_bytes=56 * 1024 * 1024),
        cost_estimate=pl.CostEstimate(
            flops=flops,
            bytes_accessed=sum(a.size * a.dtype.itemsize for a in (*args, *out_shape)),
            transcendentals=0,
        ),
        name=name,
        **({} if grid is None else {"grid": grid}),
    )(*args)


def whole(shape):
    return pl.BlockSpec(tuple(shape), lambda z: (0,) * len(shape))


def constants(channels, row_count, half_cols, hidden):
    core, edge = row_spread(channels, row_count)
    names = {
        "col": column_spread(half_cols),
        "merge": column_merge(half_cols),
        "row": core,
        "row_t": core.T,
        "edge": edge,
        "edge_t": edge.T,
        "tap": tap_spread(channels),
        "order": class_order(hidden),
    }
    return {name: jnp.asarray(value, bf16) for name, value in names.items()}


def forward(fields, below, above, before, after, target, conv_weight, conv_bias, down_weight, down_bias, fixed):
    channels, depth, row_count, col_count = fields.shape
    hidden, out_count = conv_weight.shape[0], down_weight.shape[0]
    pairs, half_rows, half_cols = depth // 2, row_count // 2, col_count // 2
    cells = half_rows * half_cols
    big, win = 8 * hidden, 64 * channels
    args = (
        fields, below, above, before, after, target,
        conv_weight, conv_bias[None], down_weight, down_bias[None],
        fixed["tap"], fixed["order"], fixed["col"], fixed["row"], fixed["edge"],
    )
    slab = pl.BlockSpec((out_count, 1, half_rows, half_cols), lambda z: (0, z, 0, 0))
    return call(
        forward_kernel,
        (channels, pairs, half_rows, hidden, out_count, forward_tile),
        [
            jax.ShapeDtypeStruct(target.shape, bf16),
            jax.ShapeDtypeStruct((pairs, big, cells), bf16),
            jax.ShapeDtypeStruct((out_count, big), f32),
            jax.ShapeDtypeStruct((hidden, 2 * lanes), f32),
        ],
        *args,
        grid=(pairs,),
        in_specs=[slab if i == 5 else whole(a.shape) for i, a in enumerate(args)],
        out_specs=[
            slab,
            pl.BlockSpec((1, big, cells), lambda z: (z, 0, 0)),
            whole((out_count, big)),
            whole((hidden, 2 * lanes)),
        ],
        scratch=[
            pltpu.VMEM((pairs + 1, 16 * channels, cells + lanes), bf16),
            pltpu.VMEM((big, win), bf16),
            pltpu.VMEM((out_count, big), bf16),
            pltpu.VMEM((big, out_count), bf16),
            pltpu.VMEM((big, win), f32),
            pltpu.VMEM((big, lanes), f32),
            pltpu.VMEM((out_count, lanes), f32),
            pltpu.VMEM((out_count, lanes), f32),
        ],
        flops=4 * pairs * cells * big * (win + out_count),
        name="forward",
    )


def backward(grad_pre, conv_weight, fixed, channels, depth, row_count, col_count):
    pairs, big, cells = grad_pre.shape
    half_rows = row_count // 2
    win = 64 * channels
    args = (grad_pre, conv_weight, fixed["tap"], fixed["merge"], fixed["row_t"], fixed["edge_t"])
    outs = [
        jax.ShapeDtypeStruct((channels, depth, row_count, col_count), f32),
        jax.ShapeDtypeStruct((channels, row_count, col_count), bf16),
        jax.ShapeDtypeStruct((channels, row_count, col_count), bf16),
        jax.ShapeDtypeStruct((depth + 2, 8, col_count), bf16),
        jax.ShapeDtypeStruct((depth + 2, 8, col_count), bf16),
    ]
    return call(
        spread_kernel,
        (channels, pairs, half_rows, spread_tile),
        outs,
        *args,
        grid=(pairs,),
        in_specs=[pl.BlockSpec((1, big, cells), lambda z: (z, 0, 0))] + [whole(a.shape) for a in args[1:]],
        out_specs=[whole(o.shape) for o in outs],
        scratch=[
            pltpu.VMEM((pairs + 1, 16 * channels, cells + lanes), f32),
            pltpu.VMEM((win, big), bf16),
        ],
        flops=2 * pairs * cells * big * win,
        name="spread",
    )


forward_tile = 1024
spread_tile = 1024


def on_device(fields, target, conv_weight, conv_bias, down_weight, down_bias):
    channels, depth, row_count, col_count = fields.shape
    hidden = conv_weight.shape[0]
    out_count = down_weight.shape[0]
    taps = channels * 27
    big = 8 * hidden
    cell_total = fields.size // channels // 8 * lax.axis_size("gz") * lax.axis_size("gy")
    fixed = constants(channels, row_count, col_count // 2, hidden)

    below = shifted(fields[:, depth - 1], "gz", 1)
    above = shifted(fields[:, 0], "gz", -1)

    def side(row):
        rows = [below[:, row][:, None], fields[:, :, row], above[:, row][:, None]]
        rows = jnp.concatenate(rows, axis=1).transpose(1, 0, 2)
        return jnp.pad(rows, ((0, 0), (0, 8 - channels), (0, 0)))

    before = shifted(side(row_count - 1), "gy", 1)
    after = shifted(side(0), "gy", -1)
    out_field, grad_pre, grad_down, small = forward(
        fields, below, above, before, after, target, conv_weight, conv_bias, down_weight, down_bias, fixed
    )

    def beside(value, count):
        return jnp.concatenate(jnp.split(value, value.shape[0] // count, axis=0), axis=1)

    me = lax.axis_index("gz")
    own = grad_down
    bit = lax.axis_size("gz")
    while bit > 1:
        bit //= 2
        count = own.shape[0] // 2
        upper = (me // bit) % 2
        keep = lax.dynamic_slice_in_dim(own, upper * count, count, 0)
        give = lax.dynamic_slice_in_dim(own, (1 - upper) * count, count, 0)
        packed = jnp.concatenate([give, beside(small, min(count, hidden))], axis=1)
        got = exchanged(packed, "gz", bit)
        own = keep + got[:, :big]
        parts = jnp.split(got[:, big:], hidden // count, axis=1)
        small = small + jnp.concatenate(parts, axis=0)
    count = own.shape[0]
    packed = jnp.concatenate([own, beside(small, count)], axis=1)
    bit = 1
    while bit < lax.axis_size("gy"):
        packed = packed + exchanged(packed, "gy", bit)
        bit *= 2
    own = packed[:, :big]
    small = jnp.concatenate(jnp.split(packed[:, big:], hidden // count, axis=1), axis=0)

    sens, to_below, to_above, to_before, to_after = backward(
        grad_pre, conv_weight, fixed, channels, depth, row_count, col_count
    )
    from_before = shifted(to_after, "gy", 1)
    from_after = shifted(to_before, "gy", -1)

    def plane(value, at):
        low = from_before[at, :channels, None].astype(f32)
        high = from_after[at, :channels, None].astype(f32)
        gap = jnp.zeros((channels, row_count - 2, col_count), f32)
        return (value.astype(f32) + jnp.concatenate([low, gap, high], axis=1)).astype(bf16)

    from_below = shifted(plane(to_above, depth + 1), "gz", 1)
    from_above = shifted(plane(to_below, 0), "gz", -1)
    (sensitivity,) = call(
        join_kernel,
        (channels, depth, row_count),
        [jax.ShapeDtypeStruct(sens.shape, f32)],
        sens, from_above, from_below, from_after, from_before,
        name="join",
    )
    conv, cbias, down, dbias, loss = call(
        last_kernel,
        (hidden, taps, cell_total, out_count),
        [
            jax.ShapeDtypeStruct((hidden, taps), f32),
            jax.ShapeDtypeStruct((1, hidden), f32),
            jax.ShapeDtypeStruct((count, big), f32),
            jax.ShapeDtypeStruct((1, out_count), f32),
            jax.ShapeDtypeStruct((1, 1), f32),
        ],
        small, own, fixed["order"],
        name="last",
    )
    return out_field, sensitivity, conv, cbias[0], down, dbias[0], loss[0, 0]


def solution(mesh):
    in_specs = (P(None, "gz", "gy", None), P(None, "gz", "gy", None), P(), P(), P(), P())
    out_specs = (
        P(None, "gz", "gy", None),
        P(None, "gz", "gy", None),
        P(),
        P(),
        P("gz", None),
        P(),
        P(),
    )
    return jax.shard_map(
        on_device, mesh=mesh, in_specs=in_specs, out_specs=out_specs, check_vma=False
    )
```

```python
import functools

import jax
import jax.numpy as jnp
import numpy as np
from jax import lax
from jax.experimental import pallas as pl
from jax.experimental.pallas import tpu as pltpu
from jax.sharding import PartitionSpec as P

gelu_scale = 0.7978845608028654
gelu_cubic = 0.044715
lanes = 128
bf16 = jnp.bfloat16
f32 = jnp.float32


def shifted(value, axis, by):
    count = lax.axis_size(axis)
    return lax.ppermute(value, axis, [(i, (i + by) % count) for i in range(count)])


def exchanged(value, axis, bit):
    count = lax.axis_size(axis)
    return lax.ppermute(value, axis, [(i, i ^ bit) for i in range(count)])


def column_merge(half_cols):
    merge = np.zeros((2 * half_cols, 2 * half_cols), np.float32)
    for par in range(2):
        for col in range(half_cols):
            merge[par * half_cols + col, (2 * col + par - 1) % (2 * half_cols)] = 1
    return merge


def row_spread(channels, row_count):
    pair_rows = row_count // 2 + 1
    core = np.zeros((pair_rows * 4 * channels, 2 * channels * row_count), np.float32)
    edge = np.zeros((8 * channels, 32), np.float32)
    for par_z in range(2):
        for ch in range(channels):
            for at in range(1, row_count + 1):
                target = ((at // 2 * 2 + par_z) * 2 + at % 2) * channels + ch
                core[target, (par_z * channels + ch) * row_count + at - 1] = 1
            edge[(par_z * 2) * channels + ch, par_z * 16 + ch] = 1
            edge[((2 + par_z) * 2 + 1) * channels + ch, par_z * 16 + 8 + ch] = 1
    return core, edge


def tap_spread(channels):
    spread = np.zeros((8, channels * 27, 64 * channels), np.float32)
    for cls in range(8):
        par_z, par_y, par_x = cls // 4, cls // 2 % 2, cls % 2
        for ch in range(channels):
            for off_z in range(3):
                for off_y in range(3):
                    for off_x in range(3):
                        at_z, at_y, at_x = par_z + off_z, par_y + off_y, par_x + off_x
                        place = (at_z // 2 * 2 + at_y // 2) * 2 + at_x // 2
                        place = ((place * 2 + at_x % 2) * 2 + at_z % 2) * 2 + at_y % 2
                        spread[cls, ch * 27 + 9 * off_z + 3 * off_y + off_x, place * channels + ch] = 1
    return spread


def class_order(hidden):
    order = np.zeros((8 * hidden, 8 * hidden), np.float32)
    for ch in range(hidden):
        for cls in range(8):
            order[ch * 8 + cls, cls * hidden + ch] = 1
    return order


def dot(a, b):
    return jnp.dot(a, b, preferred_element_type=f32)


def dot_rows(a, b):
    return lax.dot_general(a, b, (((1,), (1,)), ((), ())), preferred_element_type=f32)


def split_two(value):
    high = value.astype(bf16)
    return high, (value - high.astype(f32)).astype(bf16)


def split_three(value):
    high = value.astype(bf16)
    return (high,) + split_two(value - high.astype(f32))


def conv_rows(conv_ref, tap_ref):
    return jnp.concatenate([dot(conv_ref[...], tap_ref[cls]) for cls in range(8)], axis=0)


def row_of(ref, count):
    return jnp.transpose(jnp.broadcast_to(ref[...], (lanes, count)))


def forward_kernel(
    sizes,
    field_ref,
    below_ref,
    above_ref,
    before_ref,
    after_ref,
    target_ref,
    conv_weight_ref,
    conv_bias_ref,
    down_weight_ref,
    down_bias_ref,
    tap_ref,
    order_ref,
    col_ref,
    row_ref,
    edge_ref,
    out_ref,
    gpre_ref,
    keep_ref,
    give_ref,
    split_ref,
    conv_ref,
    down_ref,
    down_t_ref,
    gdown_t_ref,
    gconv_t_ref,
    gdb_ref,
    sq_ref,
    hid_ref,
    slope_ref,
    whole_ref,
):
    channels, pairs, half_rows, hidden, out_count, tile, cell_total = sizes
    group = 4 * channels
    cells = half_rows * lanes
    step = pl.program_id(0)

    @pl.when(step == 0)
    def _():
        gdown_t_ref[...] = jnp.zeros_like(gdown_t_ref)
        gconv_t_ref[...] = jnp.zeros_like(gconv_t_ref)
        gdb_ref[...] = jnp.zeros_like(gdb_ref)
        sq_ref[...] = jnp.zeros_like(sq_ref)
        conv_ref[:, : 16 * group] = (0.5 * conv_rows(conv_weight_ref, tap_ref)).astype(bf16)
        bias = 0.5 * row_of(conv_bias_ref, hidden)
        at = lax.broadcasted_iota(jnp.int32, bias.shape, 1)
        columns = jnp.zeros_like(bias)
        for k, piece in enumerate(split_three(bias)):
            columns = jnp.where(at == k, piece.astype(f32), columns)
        columns = jnp.concatenate([columns[:, :16]] * 8, axis=0)
        conv_ref[:, 16 * group :] = columns.astype(bf16)
        down = dot(down_weight_ref[...], order_ref[...])
        down_ref[...] = down.astype(bf16)
        down_t_ref[...] = jnp.transpose(down).astype(bf16)
        for slot in range(pairs + 1):
            lower = below_ref if slot == 0 else field_ref.at[:, 2 * slot - 1]
            upper = above_ref if slot == pairs else field_ref.at[:, 2 * slot]
            rows = [ref[ch] for ref in (lower, upper) for ch in range(channels)]
            rows = dot(row_ref[...], jnp.concatenate(rows, axis=0)).astype(bf16)
            rows = dot(rows, col_ref[...])
            sides = [ref[2 * slot + par].astype(f32) for par in range(2) for ref in (before_ref, after_ref)]
            sides = jnp.concatenate(sides, axis=0).astype(bf16)
            sides = dot(dot(edge_ref[...], sides).astype(bf16), col_ref[...])
            for row in range(half_rows + 1):
                piece = rows[row * group : (row + 1) * group]
                if row == 0:
                    piece = piece + sides[:group]
                if row == half_rows:
                    piece = piece + sides[group:]
                piece = jnp.concatenate([piece[:, :lanes], piece[:, lanes:]], axis=0)
                piece = jnp.concatenate([piece, pltpu.roll(piece, lanes - 1, 1)], axis=0)
                split_ref[slot, :, row * lanes : (row + 1) * lanes] = piece.astype(bf16)

    ones = jnp.ones((16, tile), bf16)
    down_bias = row_of(down_bias_ref, out_count)
    down_bias = jnp.concatenate([down_bias] * (tile // lanes), axis=1)
    wanted = jnp.swapaxes(target_ref[:, 0].astype(f32), 0, 1)
    parts = cells // tile
    count = tile // lanes

    def window_of(part):
        start, stop = part * tile, (part + 1) * tile
        return jnp.concatenate(
            [
                split_ref[step + dz, :, start + dy * lanes : stop + dy * lanes]
                for dz in range(2)
                for dy in range(2)
            ]
            + [ones],
            axis=0,
        )

    outputs, diffs = {}, {}

    def activate(part, rows):
        pre = dot(conv_ref[rows], window_of(part))
        square = pre * pre
        tangent = jnp.tanh(pre * (square * (8.0 * gelu_scale * gelu_cubic) + 2.0 * gelu_scale))
        above = 1.0 + tangent
        bend = pre * (square * (12.0 * gelu_scale * gelu_cubic) + gelu_scale)
        hid_ref[part % 2, rows] = (pre * above).astype(bf16)
        slope_ref[part % 2, rows] = above * ((1.0 - tangent) * bend + 0.5)

    def compare(part):
        output = dot(down_ref[...], hid_ref[part % 2]) + down_bias
        first = part * count
        diff = output - jnp.concatenate([wanted[first + k] for k in range(count)], axis=1)
        outputs[part] = [output[:, k * lanes : (k + 1) * lanes] for k in range(count)]
        for k in range(count):
            piece = diff[:, k * lanes : (k + 1) * lanes]
            gdb_ref[...] += piece
            sq_ref[...] += piece * piece
        diffs[part] = diff.astype(bf16)

    def weigh_down(part):
        gdown_t_ref[...] += dot_rows(hid_ref[part % 2], diffs[part])

    def back(part, rows):
        value = dot(down_t_ref[rows], diffs[part]) * slope_ref[part % 2, rows]
        gpre_ref[0, rows, part * tile : (part + 1) * tile] = value.astype(bf16)

    def weigh_conv(part):
        gconv_t_ref[...] += dot_rows(window_of(part), gpre_ref[0, :, part * tile : (part + 1) * tile])

    big = 8 * hidden
    blocks = [slice(0, big)]
    for part in range(parts + 1):
        first = [functools.partial(activate, part, rows) for rows in blocks] if part < parts else []
        second = []
        if part > 0:
            done = part - 1
            second = [functools.partial(compare, done), functools.partial(weigh_down, done)]
            second += [functools.partial(back, done, rows) for rows in blocks]
            second += [functools.partial(weigh_conv, done)]
        for k in range(max(len(first), len(second))):
            if k < len(second):
                second[k]()
            if k < len(first):
                first[k]()
    outputs = [value for part in range(parts) for value in outputs[part]]
    out_ref[:, 0] = jnp.swapaxes(jnp.stack(outputs, axis=0), 0, 1).astype(bf16)

    @pl.when(step == pairs - 1)
    def _():
        taps = channels * 27
        folded = 0.0
        cb = jnp.zeros((hidden, 1), f32)
        gconv = jnp.transpose(gconv_t_ref[...])
        for cls in range(8):
            rows = gconv[cls * hidden : (cls + 1) * hidden]
            cb = cb + rows[:, 16 * group : 16 * group + 1]
            rows = jnp.concatenate(split_three(rows[:, : 16 * group]), axis=0)
            folded = folded + dot_rows(rows, tap_ref[cls])
        folded = folded[:hidden] + (folded[hidden : 2 * hidden] + folded[2 * hidden :])
        columns = [folded, cb]
        for ref, share in ((gdb_ref, 1.0), (sq_ref, 1.0 / out_count)):
            total = share * jnp.sum(ref[...], axis=1, keepdims=True)
            columns += [total[:hidden], total[hidden:]]
        columns.append(jnp.zeros((hidden, 2 * lanes - taps - 5), f32))
        small = jnp.concatenate(columns, axis=1) / cell_total
        pieces = jnp.concatenate(split_three(jnp.transpose(gdown_t_ref[...])), axis=0)
        pieces = dot_rows(pieces, order_ref[...])
        grad_down = pieces[:out_count] + (pieces[out_count : 2 * out_count] + pieces[2 * out_count :])
        rows = out_count // 2
        upper = lax.axis_index("gz") // (lax.axis_size("gz") // 2)
        whole_ref[...] = grad_down / cell_total
        keep_ref[...] = whole_ref[pl.ds(pl.multiple_of(upper * rows, rows), rows)]
        give_ref[:, : 8 * hidden] = whole_ref[pl.ds(pl.multiple_of((1 - upper) * rows, rows), rows)]
        give_ref[:, 8 * hidden :] = small


def spread_kernel(sizes, *refs):
    channels, count, half_rows, tile, opening = sizes
    refs = list(refs)
    gpre_ref, conv_weight_ref, tap_ref, merge_ref, row_t_ref, edge_t_ref = refs[:6]
    if opening:
        core_ref, before_ref, after_ref, open_ref, spread_ref, conv_t_ref = refs[6:]
        at = 0
    else:
        open_ref, early_before_ref, early_after_ref = refs[6:9]
        core_ref, before_ref, after_ref, spread_ref, conv_t_ref = refs[9:]
        at = early_before_ref.shape[0]
    group = 4 * channels
    span = 4 * group
    row_count = 2 * half_rows
    cells = half_rows * lanes
    step = pl.program_id(0)

    def spread_out(pair):
        for part in range(cells // tile):
            spread = dot(conv_t_ref[...], gpre_ref[0, :, part * tile : (part + 1) * tile])
            for dz in range(2):
                for dy in range(2):
                    first = (2 * dz + dy) * span
                    here = slice(part * tile + dy * lanes, (part + 1) * tile + dy * lanes)
                    spread_ref[pair + dz, :, here] += spread[first : first + span]

    def finish(slot):
        rows = []
        for row in range(half_rows + 1):
            piece = spread_ref[slot, :, row * lanes : (row + 1) * lanes]
            halves = [
                piece[par * group : (par + 1) * group]
                + pltpu.roll(piece[(2 + par) * group : (3 + par) * group], 1, 1)
                for par in range(2)
            ]
            rows.append(jnp.concatenate(halves, axis=1))
        core, sides = 0.0, 0.0
        outer = jnp.concatenate([rows[0], rows[half_rows]], axis=0)
        for value in split_two(jnp.concatenate(rows, axis=0)):
            core = core + dot(dot(row_t_ref[...], value).astype(bf16), merge_ref[...])
        for value in split_two(outer):
            sides = sides + dot(dot(edge_t_ref[...], value).astype(bf16), merge_ref[...])
        for par in range(2):
            before_ref[at + 2 * slot + par] = sides[par * 16 : par * 16 + 8].astype(bf16)
            after_ref[at + 2 * slot + par] = sides[par * 16 + 8 : par * 16 + 16].astype(bf16)
            for ch in range(channels):
                first = (par * channels + ch) * row_count
                core_ref[2 * slot + par, ch] = core[first : first + row_count]

    for pair in range(count):

        @pl.when(step == pair)
        def _():
            if pair == 0:
                spread_ref[...] = jnp.zeros_like(spread_ref)
                conv_t_ref[...] = jnp.transpose(conv_rows(conv_weight_ref, tap_ref)).astype(bf16)
                if not opening:
                    spread_ref[0] = open_ref[...]
                    before_ref[:at] = early_before_ref[...]
                    after_ref[:at] = early_after_ref[...]
            else:
                finish(pair - 1)
            spread_out(pair)
            if pair == count - 1:
                finish(pair)
                if opening:
                    open_ref[...] = spread_ref[count]
                else:
                    finish(count)


def join_kernel(
    sizes, early_ref, late_ref, below_ref, above_ref, before_ref, after_ref, out_ref
):
    channels, depth, row_count = sizes
    early = early_ref.shape[0]
    for z in range(depth):
        plane_ref = early_ref.at[z + 1] if z + 1 < early else late_ref.at[z + 1 - early]
        for ch in range(channels):
            value = plane_ref[ch]
            if z == 0:
                value = value + above_ref[ch].astype(f32)
            if z == depth - 1:
                value = value + below_ref[ch].astype(f32)
            out_ref[ch, z] = value
            out_ref[ch, z, 0:1] += after_ref[z + 1, ch : ch + 1].astype(f32)
            out_ref[ch, z, row_count - 1 : row_count] += before_ref[z + 1, ch : ch + 1].astype(f32)


def last_kernel(sizes, mine_ref, theirs_ref, conv_out, cbias_out, down_out, dbias_out, loss_out):
    hidden, taps, big = sizes
    total = mine_ref[...] + theirs_ref[...]
    down_out[...] = total[:, :big]
    small = jnp.concatenate(
        [total[:, at : at + 2 * lanes] for at in range(big, total.shape[1], 2 * lanes)], axis=0
    )
    conv_out[...] = small[:, :taps]
    turned = jnp.transpose(small[:, lanes:])
    at = taps - lanes
    cbias_out[...] = turned[at : at + 1]
    dbias_out[...] = jnp.concatenate([turned[at + 1 : at + 2], turned[at + 2 : at + 3]], axis=1)
    loss_out[...] = jnp.sum(turned[at + 3 : at + 4] + turned[at + 4 : at + 5], axis=1, keepdims=True)


def call(kernel, sizes, out_shape, *args, grid=None, in_specs=None, out_specs=None, scratch=(), flops=0, name):
    if grid is None:
        in_specs = [pl.BlockSpec(memory_space=pltpu.VMEM)] * len(args)
        out_specs = [pl.BlockSpec(memory_space=pltpu.VMEM)] * len(out_shape)
    return pl.pallas_call(
        functools.partial(kernel, sizes),
        out_shape=out_shape,
        in_specs=in_specs,
        out_specs=out_specs,
        scratch_shapes=scratch,
        compiler_params=pltpu.CompilerParams(vmem_limit_bytes=56 * 1024 * 1024),
        cost_estimate=pl.CostEstimate(
            flops=flops,
            bytes_accessed=sum(a.size * a.dtype.itemsize for a in (*args, *out_shape)),
            transcendentals=0,
        ),
        name=name,
        **({} if grid is None else {"grid": grid}),
    )(*args)


def whole(shape):
    return pl.BlockSpec(tuple(shape), lambda z: (0,) * len(shape))


def constants(channels, row_count, half_cols, hidden):
    core, edge = row_spread(channels, row_count)
    names = {
        "col": column_merge(half_cols).T,
        "merge": column_merge(half_cols),
        "row": core,
        "row_t": core.T,
        "edge": edge,
        "edge_t": edge.T,
        "tap": tap_spread(channels),
        "order": class_order(hidden),
    }
    return {name: jnp.asarray(value, bf16) for name, value in names.items()}


def forward(fields, below, above, before, after, target, conv_weight, conv_bias, down_weight, down_bias, fixed, cell_total):
    channels, depth, row_count, col_count = fields.shape
    hidden, out_count = conv_weight.shape[0], down_weight.shape[0]
    pairs, half_rows, half_cols = depth // 2, row_count // 2, col_count // 2
    cells = half_rows * half_cols
    big, win = 8 * hidden, 64 * channels
    args = (
        fields, below, above, before, after, target,
        conv_weight, conv_bias[None], down_weight, down_bias[None],
        fixed["tap"], fixed["order"], fixed["col"], fixed["row"], fixed["edge"],
    )
    slab = pl.BlockSpec((out_count, 1, half_rows, half_cols), lambda z: (0, z, 0, 0))
    return call(
        forward_kernel,
        (channels, pairs, half_rows, hidden, out_count, forward_tile, cell_total),
        [
            jax.ShapeDtypeStruct(target.shape, bf16),
            jax.ShapeDtypeStruct((pairs, big, cells), bf16),
            jax.ShapeDtypeStruct((out_count // 2, big), f32),
            jax.ShapeDtypeStruct((out_count // 2, big + 2 * lanes), f32),
        ],
        *args,
        grid=(pairs,),
        in_specs=[slab if i == 5 else whole(a.shape) for i, a in enumerate(args)],
        out_specs=[
            slab,
            pl.BlockSpec((1, big, cells), lambda z: (z, 0, 0)),
            whole((out_count // 2, big)),
            whole((out_count // 2, big + 2 * lanes)),
        ],
        scratch=[
            pltpu.VMEM((pairs + 1, 16 * channels, cells + lanes), bf16),
            pltpu.VMEM((big, win + 16), bf16),
            pltpu.VMEM((out_count, big), bf16),
            pltpu.VMEM((big, out_count), bf16),
            pltpu.VMEM((big, out_count), f32),
            pltpu.VMEM((win + 16, big), f32),
            pltpu.VMEM((out_count, lanes), f32),
            pltpu.VMEM((out_count, lanes), f32),
            pltpu.VMEM((2, big, forward_tile), bf16),
            pltpu.VMEM((2, big, forward_tile), f32),
            pltpu.VMEM((out_count, big), f32),
        ],
        flops=4 * pairs * cells * big * (win + out_count),
        name="forward",
    )


def backward(grad_pre, first, count, conv_weight, fixed, shape, open_slot=None, early=()):
    channels, depth, row_count, col_count = shape
    _, big, cells = grad_pre.shape
    half_rows = row_count // 2
    win = 64 * channels
    opening = open_slot is None
    args = (grad_pre, conv_weight, fixed["tap"], fixed["merge"], fixed["row_t"], fixed["edge_t"])
    if not opening:
        args += (open_slot, *early)
    slots = count if opening else count + 1
    sides = jax.ShapeDtypeStruct((2 * (first + slots), 8, col_count), bf16)
    outs = [jax.ShapeDtypeStruct((2 * slots, channels, row_count, col_count), f32), sides, sides]
    if opening:
        outs.append(jax.ShapeDtypeStruct((16 * channels, cells + lanes), f32))
    return call(
        spread_kernel,
        (channels, count, half_rows, spread_tile, opening),
        outs,
        *args,
        grid=(count,),
        in_specs=[pl.BlockSpec((1, big, cells), lambda z: (first + z, 0, 0))] + [whole(a.shape) for a in args[1:]],
        out_specs=[whole(o.shape) for o in outs],
        scratch=[
            pltpu.VMEM((count + 1, 16 * channels, cells + lanes), f32),
            pltpu.VMEM((win, big), bf16),
        ],
        flops=2 * count * cells * big * win,
        name="spread",
    )


forward_tile = 1024
spread_tile = 1024


def on_device(fields, target, conv_weight, conv_bias, down_weight, down_bias):
    channels, depth, row_count, col_count = fields.shape
    hidden = conv_weight.shape[0]
    out_count = down_weight.shape[0]
    taps = channels * 27
    big = 8 * hidden
    cell_total = fields.size // channels // 8 * lax.axis_size("gz") * lax.axis_size("gy")
    fixed = constants(channels, row_count, col_count // 2, hidden)

    below = shifted(fields[:, depth - 1], "gz", 1)
    above = shifted(fields[:, 0], "gz", -1)

    def side(row):
        rows = [below[:, row][:, None], fields[:, :, row], above[:, row][:, None]]
        rows = jnp.concatenate(rows, axis=1).transpose(1, 0, 2)
        return jnp.pad(rows, ((0, 0), (0, 8 - channels), (0, 0)))

    before = shifted(side(row_count - 1), "gy", 1)
    after = shifted(side(0), "gy", -1)
    out_field, grad_pre, own, packed = forward(
        fields, below, above, before, after, target,
        conv_weight, conv_bias, down_weight, down_bias, fixed, cell_total,
    )

    def beside(value, count):
        return jnp.concatenate(jnp.split(value, value.shape[0] // count, axis=0), axis=1)

    me = lax.axis_index("gz")
    bit = lax.axis_size("gz") // 2
    small = packed[:, big:]
    parts, open_slot, early, core = 2, None, (), []
    pairs = depth // 2
    while True:
        got = exchanged(packed, "gz", bit)
        if len(core) < parts:
            count = pairs // parts
            found = backward(
                grad_pre, len(core) * count, count, conv_weight, fixed, fields.shape, open_slot, early
            )
            core.append(found[0])
            early = found[1:3]
            open_slot = found[3] if len(core) < parts else None
        count = own.shape[0]
        own = own + got[:, :big]
        pieces = jnp.split(got[:, big:], hidden // count, axis=1)
        small = small + jnp.concatenate(pieces, axis=0)
        if bit == 1:
            break
        bit //= 2
        count //= 2
        upper = (me // bit) % 2
        give = lax.dynamic_slice_in_dim(own, (1 - upper) * count, count, 0)
        own = lax.dynamic_slice_in_dim(own, upper * count, count, 0)
        packed = jnp.concatenate([give, beside(small, count)], axis=1)
        if len(core) < parts:
            packed, open_slot = lax.optimization_barrier((packed, open_slot))
    packed = jnp.concatenate([own, beside(small, own.shape[0])], axis=1)
    count = own.shape[0]
    to_before, to_after = early

    from_before = shifted(to_after, "gy", 1)
    from_after = shifted(to_before, "gy", -1)

    def plane(value, at):
        low = from_before[at, :channels, None].astype(f32)
        high = from_after[at, :channels, None].astype(f32)
        gap = jnp.zeros((channels, row_count - 2, col_count), f32)
        return (value + jnp.concatenate([low, gap, high], axis=1)).astype(bf16)

    from_below = shifted(plane(core[-1][-1], depth + 1), "gz", 1)
    from_above = shifted(plane(core[0][0], 0), "gz", -1)

    bit = 1
    while 2 * bit < lax.axis_size("gy"):
        packed = packed + exchanged(packed, "gy", bit)
        bit *= 2
    got = exchanged(packed, "gy", bit)
    (sensitivity,) = call(
        join_kernel,
        (channels, depth, row_count),
        [jax.ShapeDtypeStruct(fields.shape, f32)],
        *core, from_above, from_below, from_after, from_before,
        name="join",
    )
    conv, cbias, down, dbias, loss = call(
        last_kernel,
        (hidden, taps, big),
        [
            jax.ShapeDtypeStruct((hidden, taps), f32),
            jax.ShapeDtypeStruct((1, hidden), f32),
            jax.ShapeDtypeStruct((count, big), f32),
            jax.ShapeDtypeStruct((1, out_count), f32),
            jax.ShapeDtypeStruct((1, 1), f32),
        ],
        packed, got,
        name="last",
    )
    return out_field, sensitivity, conv, cbias[0], down, dbias[0], loss[0, 0]


def solution(mesh):
    in_specs = (P(None, "gz", "gy", None), P(None, "gz", "gy", None), P(), P(), P(), P())
    out_specs = (
        P(None, "gz", "gy", None),
        P(None, "gz", "gy", None),
        P(),
        P(),
        P("gz", None),
        P(),
        P(),
    )
    return jax.shard_map(
        on_device, mesh=mesh, in_specs=in_specs, out_specs=out_specs, check_vma=False
    )
```

```python
import functools

import jax
import jax.numpy as jnp
import numpy as np
from jax import lax
from jax.experimental import pallas as pl
from jax.experimental.pallas import tpu as pltpu
from jax.sharding import PartitionSpec as P

gelu_scale = 0.7978845608028654
gelu_cubic = 0.044715
lanes = 128
bf16 = jnp.bfloat16
f32 = jnp.float32


def shifted(value, axis, by):
    count = lax.axis_size(axis)
    return lax.ppermute(value, axis, [(i, (i + by) % count) for i in range(count)])


def exchanged(value, axis, bit):
    count = lax.axis_size(axis)
    return lax.ppermute(value, axis, [(i, i ^ bit) for i in range(count)])


def column_merge(half_cols):
    merge = np.zeros((2 * half_cols, 2 * half_cols), np.float32)
    for par in range(2):
        for col in range(half_cols):
            merge[par * half_cols + col, (2 * col + par - 1) % (2 * half_cols)] = 1
    return merge


def row_spread(channels, row_count):
    pair_rows = row_count // 2 + 1
    core = np.zeros((pair_rows * 4 * channels, 2 * channels * row_count), np.float32)
    edge = np.zeros((8 * channels, 32), np.float32)
    for par_z in range(2):
        for ch in range(channels):
            for at in range(1, row_count + 1):
                target = ((at // 2 * 2 + par_z) * 2 + at % 2) * channels + ch
                core[target, (par_z * channels + ch) * row_count + at - 1] = 1
            edge[(par_z * 2) * channels + ch, par_z * 16 + ch] = 1
            edge[((2 + par_z) * 2 + 1) * channels + ch, par_z * 16 + 8 + ch] = 1
    return core, edge


def tap_spread(channels):
    spread = np.zeros((8, channels * 27, 64 * channels), np.float32)
    for cls in range(8):
        par_z, par_y, par_x = cls // 4, cls // 2 % 2, cls % 2
        for ch in range(channels):
            for off_z in range(3):
                for off_y in range(3):
                    for off_x in range(3):
                        at_z, at_y, at_x = par_z + off_z, par_y + off_y, par_x + off_x
                        place = (at_z // 2 * 2 + at_y // 2) * 2 + at_x // 2
                        place = ((place * 2 + at_x % 2) * 2 + at_z % 2) * 2 + at_y % 2
                        spread[cls, ch * 27 + 9 * off_z + 3 * off_y + off_x, place * channels + ch] = 1
    return spread


def class_order(hidden):
    order = np.zeros((8 * hidden, 8 * hidden), np.float32)
    for ch in range(hidden):
        for cls in range(8):
            order[ch * 8 + cls, cls * hidden + ch] = 1
    return order


def dot(a, b):
    return jnp.dot(a, b, preferred_element_type=f32)


def dot_rows(a, b):
    return lax.dot_general(a, b, (((1,), (1,)), ((), ())), preferred_element_type=f32)


def split_two(value):
    high = value.astype(bf16)
    return high, (value - high.astype(f32)).astype(bf16)


def split_three(value):
    high = value.astype(bf16)
    return (high,) + split_two(value - high.astype(f32))


def conv_rows(conv_ref, tap_ref):
    return jnp.concatenate([dot(conv_ref[...], tap_ref[cls]) for cls in range(8)], axis=0)


def row_of(ref, count):
    return jnp.transpose(jnp.broadcast_to(ref[...], (lanes, count)))


def forward_kernel(
    sizes,
    field_ref,
    below_ref,
    above_ref,
    before_ref,
    after_ref,
    target_ref,
    conv_weight_ref,
    conv_bias_ref,
    down_weight_ref,
    down_bias_ref,
    tap_ref,
    order_ref,
    col_ref,
    row_ref,
    edge_ref,
    out_ref,
    gpre_ref,
    keep_ref,
    give_ref,
    split_ref,
    conv_ref,
    down_ref,
    down_t_ref,
    gdown_t_ref,
    gconv_t_ref,
    gdb_ref,
    sq_ref,
    hid_ref,
    slope_ref,
    whole_ref,
):
    channels, pairs, half_rows, hidden, out_count, tile, cell_total = sizes
    group = 4 * channels
    cells = half_rows * lanes
    step = pl.program_id(0)

    @pl.when(step == 0)
    def _():
        gdown_t_ref[...] = jnp.zeros_like(gdown_t_ref)
        gconv_t_ref[...] = jnp.zeros_like(gconv_t_ref)
        gdb_ref[...] = jnp.zeros_like(gdb_ref)
        sq_ref[...] = jnp.zeros_like(sq_ref)
        conv_ref[:, : 16 * group] = (0.5 * conv_rows(conv_weight_ref, tap_ref)).astype(bf16)
        bias = 0.5 * row_of(conv_bias_ref, hidden)
        at = lax.broadcasted_iota(jnp.int32, bias.shape, 1)
        columns = jnp.zeros_like(bias)
        for k, piece in enumerate(split_three(bias)):
            columns = jnp.where(at == k, piece.astype(f32), columns)
        columns = jnp.concatenate([columns[:, :16]] * 8, axis=0)
        conv_ref[:, 16 * group :] = columns.astype(bf16)
        down = dot(down_weight_ref[...], order_ref[...])
        down_ref[...] = down.astype(bf16)
        down_t_ref[...] = jnp.transpose(down).astype(bf16)
        for slot in range(pairs + 1):
            lower = below_ref if slot == 0 else field_ref.at[:, 2 * slot - 1]
            upper = above_ref if slot == pairs else field_ref.at[:, 2 * slot]
            rows = [ref[ch] for ref in (lower, upper) for ch in range(channels)]
            rows = dot(row_ref[...], jnp.concatenate(rows, axis=0)).astype(bf16)
            rows = dot(rows, col_ref[...])
            sides = [ref[2 * slot + par].astype(f32) for par in range(2) for ref in (before_ref, after_ref)]
            sides = jnp.concatenate(sides, axis=0).astype(bf16)
            sides = dot(dot(edge_ref[...], sides).astype(bf16), col_ref[...])
            for row in range(half_rows + 1):
                piece = rows[row * group : (row + 1) * group]
                if row == 0:
                    piece = piece + sides[:group]
                if row == half_rows:
                    piece = piece + sides[group:]
                piece = jnp.concatenate([piece[:, :lanes], piece[:, lanes:]], axis=0)
                piece = jnp.concatenate([piece, pltpu.roll(piece, lanes - 1, 1)], axis=0)
                split_ref[slot, :, row * lanes : (row + 1) * lanes] = piece.astype(bf16)

    ones = jnp.ones((16, tile), bf16)
    down_bias = row_of(down_bias_ref, out_count)
    down_bias = jnp.concatenate([down_bias] * (tile // lanes), axis=1)
    wanted = jnp.swapaxes(target_ref[:, 0].astype(f32), 0, 1)
    parts = cells // tile
    count = tile // lanes

    def window_of(part):
        start, stop = part * tile, (part + 1) * tile
        return jnp.concatenate(
            [
                split_ref[step + dz, :, start + dy * lanes : stop + dy * lanes]
                for dz in range(2)
                for dy in range(2)
            ]
            + [ones],
            axis=0,
        )

    outputs, diffs = {}, {}

    def activate(part, rows):
        pre = dot(conv_ref[rows], window_of(part))
        square = pre * pre
        tangent = jnp.tanh(pre * (square * (8.0 * gelu_scale * gelu_cubic) + 2.0 * gelu_scale))
        above = 1.0 + tangent
        bend = pre * (square * (12.0 * gelu_scale * gelu_cubic) + gelu_scale)
        hid_ref[part % 2, rows] = (pre * above).astype(bf16)
        slope_ref[part % 2, rows] = above * ((1.0 - tangent) * bend + 0.5)

    def compare(part):
        output = dot(down_ref[...], hid_ref[part % 2]) + down_bias
        first = part * count
        diff = output - jnp.concatenate([wanted[first + k] for k in range(count)], axis=1)
        outputs[part] = [output[:, k * lanes : (k + 1) * lanes] for k in range(count)]
        for k in range(count):
            piece = diff[:, k * lanes : (k + 1) * lanes]
            gdb_ref[...] += piece
            sq_ref[...] += piece * piece
        diffs[part] = diff.astype(bf16)

    def weigh_down(part):
        gdown_t_ref[...] += dot_rows(hid_ref[part % 2], diffs[part])

    def back(part, rows):
        value = dot(down_t_ref[rows], diffs[part]) * slope_ref[part % 2, rows]
        gpre_ref[0, rows, part * tile : (part + 1) * tile] = value.astype(bf16)

    def weigh_conv(part):
        gconv_t_ref[...] += dot_rows(window_of(part), gpre_ref[0, :, part * tile : (part + 1) * tile])

    big = 8 * hidden
    blocks = [slice(0, big)]
    for part in range(parts + 1):
        first = [functools.partial(activate, part, rows) for rows in blocks] if part < parts else []
        second = []
        if part > 0:
            done = part - 1
            second = [functools.partial(compare, done), functools.partial(weigh_down, done)]
            second += [functools.partial(back, done, rows) for rows in blocks]
            second += [functools.partial(weigh_conv, done)]
        for k in range(max(len(first), len(second))):
            if k < len(second):
                second[k]()
            if k < len(first):
                first[k]()
    outputs = [value for part in range(parts) for value in outputs[part]]
    out_ref[:, 0] = jnp.swapaxes(jnp.stack(outputs, axis=0), 0, 1).astype(bf16)

    @pl.when(step == pairs - 1)
    def _():
        taps = channels * 27
        folded = 0.0
        cb = jnp.zeros((hidden, 1), f32)
        gconv = jnp.transpose(gconv_t_ref[...])
        for cls in range(8):
            rows = gconv[cls * hidden : (cls + 1) * hidden]
            cb = cb + rows[:, 16 * group : 16 * group + 1]
            rows = jnp.concatenate(split_three(rows[:, : 16 * group]), axis=0)
            folded = folded + dot_rows(rows, tap_ref[cls])
        folded = folded[:hidden] + (folded[hidden : 2 * hidden] + folded[2 * hidden :])
        columns = [folded, cb]
        for ref, share in ((gdb_ref, 1.0), (sq_ref, 1.0 / out_count)):
            total = share * jnp.sum(ref[...], axis=1, keepdims=True)
            columns += [total[:hidden], total[hidden:]]
        columns.append(jnp.zeros((hidden, 2 * lanes - taps - 5), f32))
        small = jnp.concatenate(columns, axis=1) / cell_total
        pieces = jnp.concatenate(split_three(jnp.transpose(gdown_t_ref[...])), axis=0)
        pieces = dot_rows(pieces, order_ref[...])
        grad_down = pieces[:out_count] + (pieces[out_count : 2 * out_count] + pieces[2 * out_count :])
        rows = out_count // 2
        upper = lax.axis_index("gz") // (lax.axis_size("gz") // 2)
        whole_ref[...] = grad_down / cell_total
        keep_ref[...] = whole_ref[pl.ds(pl.multiple_of(upper * rows, rows), rows)]
        give_ref[:, : 8 * hidden] = whole_ref[pl.ds(pl.multiple_of((1 - upper) * rows, rows), rows)]
        give_ref[:, 8 * hidden :] = small


def spread_kernel(sizes, *refs):
    channels, count, half_rows, tile, opening = sizes
    refs = list(refs)
    gpre_ref, conv_weight_ref, tap_ref, merge_ref, row_t_ref, edge_t_ref = refs[:6]
    if opening:
        core_ref, before_ref, after_ref, open_ref, spread_ref, conv_t_ref = refs[6:]
        at = 0
    else:
        open_ref, early_before_ref, early_after_ref = refs[6:9]
        core_ref, before_ref, after_ref, spread_ref, conv_t_ref = refs[9:]
        at = early_before_ref.shape[0]
    group = 4 * channels
    span = 4 * group
    row_count = 2 * half_rows
    cells = half_rows * lanes
    step = pl.program_id(0)

    def spread_out(pair):
        for part in range(cells // tile):
            spread = dot(conv_t_ref[...], gpre_ref[0, :, part * tile : (part + 1) * tile])
            for dz in range(2):
                for dy in range(2):
                    first = (2 * dz + dy) * span
                    here = slice(part * tile + dy * lanes, (part + 1) * tile + dy * lanes)
                    spread_ref[pair + dz, :, here] += spread[first : first + span]

    def finish(slot):
        rows = []
        for row in range(half_rows + 1):
            piece = spread_ref[slot, :, row * lanes : (row + 1) * lanes]
            halves = [
                piece[par * group : (par + 1) * group]
                + pltpu.roll(piece[(2 + par) * group : (3 + par) * group], 1, 1)
                for par in range(2)
            ]
            rows.append(jnp.concatenate(halves, axis=1))
        core, sides = 0.0, 0.0
        outer = jnp.concatenate([rows[0], rows[half_rows]], axis=0)
        for value in split_two(jnp.concatenate(rows, axis=0)):
            core = core + dot(dot(row_t_ref[...], value).astype(bf16), merge_ref[...])
        for value in split_two(outer):
            sides = sides + dot(dot(edge_t_ref[...], value).astype(bf16), merge_ref[...])
        for par in range(2):
            before_ref[at + 2 * slot + par] = sides[par * 16 : par * 16 + 8].astype(bf16)
            after_ref[at + 2 * slot + par] = sides[par * 16 + 8 : par * 16 + 16].astype(bf16)
            for ch in range(channels):
                first = (par * channels + ch) * row_count
                core_ref[2 * slot + par, ch] = core[first : first + row_count]

    for pair in range(count):

        @pl.when(step == pair)
        def _():
            if pair == 0:
                spread_ref[...] = jnp.zeros_like(spread_ref)
                conv_t_ref[...] = jnp.transpose(conv_rows(conv_weight_ref, tap_ref)).astype(bf16)
                if not opening:
                    spread_ref[0] = open_ref[...]
                    before_ref[:at] = early_before_ref[...]
                    after_ref[:at] = early_after_ref[...]
            else:
                finish(pair - 1)
            spread_out(pair)
            if pair == count - 1:
                finish(pair)
                if opening:
                    open_ref[...] = spread_ref[count]
                else:
                    finish(count)


def join_kernel(
    sizes, early_ref, late_ref, below_ref, above_ref, before_ref, after_ref, out_ref
):
    channels, depth, row_count = sizes
    early = early_ref.shape[0]
    for z in range(depth):
        plane_ref = early_ref.at[z + 1] if z + 1 < early else late_ref.at[z + 1 - early]
        for ch in range(channels):
            value = plane_ref[ch]
            if z == 0:
                value = value + above_ref[ch].astype(f32)
            if z == depth - 1:
                value = value + below_ref[ch].astype(f32)
            out_ref[ch, z] = value
            out_ref[ch, z, 0:1] += after_ref[z + 1, ch : ch + 1].astype(f32)
            out_ref[ch, z, row_count - 1 : row_count] += before_ref[z + 1, ch : ch + 1].astype(f32)


def last_kernel(sizes, mine_ref, theirs_ref, conv_out, cbias_out, down_out, dbias_out, loss_out):
    hidden, taps, big = sizes
    total = mine_ref[...] + theirs_ref[...]
    down_out[...] = total[:, :big]
    small = jnp.concatenate(
        [total[:, at : at + 2 * lanes] for at in range(big, total.shape[1], 2 * lanes)], axis=0
    )
    conv_out[...] = small[:, :taps]
    turned = jnp.transpose(small[:, lanes:])
    at = taps - lanes
    cbias_out[...] = turned[at : at + 1]
    dbias_out[...] = jnp.concatenate([turned[at + 1 : at + 2], turned[at + 2 : at + 3]], axis=1)
    loss_out[...] = jnp.sum(turned[at + 3 : at + 4] + turned[at + 4 : at + 5], axis=1, keepdims=True)


def call(kernel, sizes, out_shape, *args, grid=None, in_specs=None, out_specs=None, scratch=(), flops=0, name):
    if grid is None:
        in_specs = [pl.BlockSpec(memory_space=pltpu.VMEM)] * len(args)
        out_specs = [pl.BlockSpec(memory_space=pltpu.VMEM)] * len(out_shape)
    return pl.pallas_call(
        functools.partial(kernel, sizes),
        out_shape=out_shape,
        in_specs=in_specs,
        out_specs=out_specs,
        scratch_shapes=scratch,
        compiler_params=pltpu.CompilerParams(vmem_limit_bytes=56 * 1024 * 1024),
        cost_estimate=pl.CostEstimate(
            flops=flops,
            bytes_accessed=sum(a.size * a.dtype.itemsize for a in (*args, *out_shape)),
            transcendentals=0,
        ),
        name=name,
        **({} if grid is None else {"grid": grid}),
    )(*args)


def whole(shape):
    return pl.BlockSpec(tuple(shape), lambda z: (0,) * len(shape))


def constants(channels, row_count, half_cols, hidden):
    core, edge = row_spread(channels, row_count)
    names = {
        "col": column_merge(half_cols).T,
        "merge": column_merge(half_cols),
        "row": core,
        "row_t": core.T,
        "edge": edge,
        "edge_t": edge.T,
        "tap": tap_spread(channels),
        "order": class_order(hidden),
    }
    return {name: jnp.asarray(value, bf16) for name, value in names.items()}


def forward(fields, below, above, before, after, target, conv_weight, conv_bias, down_weight, down_bias, fixed, cell_total):
    channels, depth, row_count, col_count = fields.shape
    hidden, out_count = conv_weight.shape[0], down_weight.shape[0]
    pairs, half_rows, half_cols = depth // 2, row_count // 2, col_count // 2
    cells = half_rows * half_cols
    big, win = 8 * hidden, 64 * channels
    args = (
        fields, below, above, before, after, target,
        conv_weight, conv_bias[None], down_weight, down_bias[None],
        fixed["tap"], fixed["order"], fixed["col"], fixed["row"], fixed["edge"],
    )
    slab = pl.BlockSpec((out_count, 1, half_rows, half_cols), lambda z: (0, z, 0, 0))
    return call(
        forward_kernel,
        (channels, pairs, half_rows, hidden, out_count, forward_tile, cell_total),
        [
            jax.ShapeDtypeStruct(target.shape, bf16),
            jax.ShapeDtypeStruct((pairs, big, cells), bf16),
            jax.ShapeDtypeStruct((out_count // 2, big), f32),
            jax.ShapeDtypeStruct((out_count // 2, big + 2 * lanes), f32),
        ],
        *args,
        grid=(pairs,),
        in_specs=[slab if i == 5 else whole(a.shape) for i, a in enumerate(args)],
        out_specs=[
            slab,
            pl.BlockSpec((1, big, cells), lambda z: (z, 0, 0)),
            whole((out_count // 2, big)),
            whole((out_count // 2, big + 2 * lanes)),
        ],
        scratch=[
            pltpu.VMEM((pairs + 1, 16 * channels, cells + lanes), bf16),
            pltpu.VMEM((big, win + 16), bf16),
            pltpu.VMEM((out_count, big), bf16),
            pltpu.VMEM((big, out_count), bf16),
            pltpu.VMEM((big, out_count), f32),
            pltpu.VMEM((win + 16, big), f32),
            pltpu.VMEM((out_count, lanes), f32),
            pltpu.VMEM((out_count, lanes), f32),
            pltpu.VMEM((2, big, forward_tile), bf16),
            pltpu.VMEM((2, big, forward_tile), f32),
            pltpu.VMEM((out_count, big), f32),
        ],
        flops=4 * pairs * cells * big * (win + out_count),
        name="forward",
    )


def backward(grad_pre, first, count, conv_weight, fixed, shape, open_slot=None, early=()):
    channels, depth, row_count, col_count = shape
    _, big, cells = grad_pre.shape
    half_rows = row_count // 2
    win = 64 * channels
    opening = open_slot is None
    args = (grad_pre, conv_weight, fixed["tap"], fixed["merge"], fixed["row_t"], fixed["edge_t"])
    if not opening:
        args += (open_slot, *early)
    slots = count if opening else count + 1
    sides = jax.ShapeDtypeStruct((2 * (first + slots), 8, col_count), bf16)
    outs = [jax.ShapeDtypeStruct((2 * slots, channels, row_count, col_count), f32), sides, sides]
    if opening:
        outs.append(jax.ShapeDtypeStruct((16 * channels, cells + lanes), f32))
    return call(
        spread_kernel,
        (channels, count, half_rows, spread_tile, opening),
        outs,
        *args,
        grid=(count,),
        in_specs=[pl.BlockSpec((1, big, cells), lambda z: (first + z, 0, 0))] + [whole(a.shape) for a in args[1:]],
        out_specs=[whole(o.shape) for o in outs],
        scratch=[
            pltpu.VMEM((count + 1, 16 * channels, cells + lanes), f32),
            pltpu.VMEM((win, big), bf16),
        ],
        flops=2 * count * cells * big * win,
        name="spread",
    )


forward_tile = 1024
spread_tile = 1024


def on_device(fields, target, conv_weight, conv_bias, down_weight, down_bias):
    channels, depth, row_count, col_count = fields.shape
    hidden = conv_weight.shape[0]
    out_count = down_weight.shape[0]
    taps = channels * 27
    big = 8 * hidden
    cell_total = fields.size // channels // 8 * lax.axis_size("gz") * lax.axis_size("gy")
    fixed = constants(channels, row_count, col_count // 2, hidden)

    below = shifted(fields[:, depth - 1], "gz", 1)
    above = shifted(fields[:, 0], "gz", -1)

    def side(row):
        rows = [below[:, row][:, None], fields[:, :, row], above[:, row][:, None]]
        rows = jnp.concatenate(rows, axis=1).transpose(1, 0, 2)
        return jnp.pad(rows, ((0, 0), (0, 8 - channels), (0, 0)))

    before = shifted(side(row_count - 1), "gy", 1)
    after = shifted(side(0), "gy", -1)
    out_field, grad_pre, own, packed = forward(
        fields, below, above, before, after, target,
        conv_weight, conv_bias, down_weight, down_bias, fixed, cell_total,
    )

    def beside(value, count):
        return jnp.concatenate(jnp.split(value, value.shape[0] // count, axis=0), axis=1)

    me = lax.axis_index("gz")
    bit = lax.axis_size("gz") // 2
    small = packed[:, big:]
    parts, open_slot, early, core = 2, None, (), []
    pairs = depth // 2
    while True:
        got = exchanged(packed, "gz", bit)
        if len(core) < parts:
            count = pairs // parts
            found = backward(
                grad_pre, len(core) * count, count, conv_weight, fixed, fields.shape, open_slot, early
            )
            core.append(found[0])
            early = found[1:3]
            open_slot = found[3] if len(core) < parts else None
        count = own.shape[0]
        own = own + got[:, :big]
        pieces = jnp.split(got[:, big:], hidden // count, axis=1)
        small = small + jnp.concatenate(pieces, axis=0)
        if len(core) == parts and early:
            own, small, to_before, to_after = lax.optimization_barrier((own, small, *early))
            early = ()
        if bit == 1:
            break
        bit //= 2
        count //= 2
        upper = (me // bit) % 2
        give = lax.dynamic_slice_in_dim(own, (1 - upper) * count, count, 0)
        own = lax.dynamic_slice_in_dim(own, upper * count, count, 0)
        packed = jnp.concatenate([give, beside(small, count)], axis=1)
        if len(core) < parts:
            packed, open_slot = lax.optimization_barrier((packed, open_slot))
    packed = jnp.concatenate([own, beside(small, own.shape[0])], axis=1)
    count = own.shape[0]

    from_before = shifted(to_after, "gy", 1)
    from_after = shifted(to_before, "gy", -1)

    def plane(value, at):
        low = from_before[at, :channels, None].astype(f32)
        high = from_after[at, :channels, None].astype(f32)
        gap = jnp.zeros((channels, row_count - 2, col_count), f32)
        return (value + jnp.concatenate([low, gap, high], axis=1)).astype(bf16)

    from_below = shifted(plane(core[-1][-1], depth + 1), "gz", 1)
    from_above = shifted(plane(core[0][0], 0), "gz", -1)

    bit = 1
    while 2 * bit < lax.axis_size("gy"):
        packed = packed + exchanged(packed, "gy", bit)
        bit *= 2
    got = exchanged(packed, "gy", bit)
    (sensitivity,) = call(
        join_kernel,
        (channels, depth, row_count),
        [jax.ShapeDtypeStruct(fields.shape, f32)],
        *core, from_above, from_below, from_after, from_before,
        name="join",
    )
    conv, cbias, down, dbias, loss = call(
        last_kernel,
        (hidden, taps, big),
        [
            jax.ShapeDtypeStruct((hidden, taps), f32),
            jax.ShapeDtypeStruct((1, hidden), f32),
            jax.ShapeDtypeStruct((count, big), f32),
            jax.ShapeDtypeStruct((1, out_count), f32),
            jax.ShapeDtypeStruct((1, 1), f32),
        ],
        packed, got,
        name="last",
    )
    return out_field, sensitivity, conv, cbias[0], down, dbias[0], loss[0, 0]


def solution(mesh):
    in_specs = (P(None, "gz", "gy", None), P(None, "gz", "gy", None), P(), P(), P(), P())
    out_specs = (
        P(None, "gz", "gy", None),
        P(None, "gz", "gy", None),
        P(),
        P(),
        P("gz", None),
        P(),
        P(),
    )
    return jax.shard_map(
        on_device, mesh=mesh, in_specs=in_specs, out_specs=out_specs, check_vma=False
    )
```

```python
import functools

import jax
import jax.numpy as jnp
import numpy as np
from jax import lax
from jax.experimental import pallas as pl
from jax.experimental.pallas import tpu as pltpu
from jax.sharding import PartitionSpec as P

gelu_scale = 0.7978845608028654
gelu_cubic = 0.044715
lanes = 128
bf16 = jnp.bfloat16
f32 = jnp.float32


def shifted(value, axis, by):
    count = lax.axis_size(axis)
    return lax.ppermute(value, axis, [(i, (i + by) % count) for i in range(count)])


def exchanged(value, axis, bit):
    count = lax.axis_size(axis)
    return lax.ppermute(value, axis, [(i, i ^ bit) for i in range(count)])


def column_merge(half_cols):
    merge = np.zeros((2 * half_cols, 2 * half_cols), np.float32)
    for par in range(2):
        for col in range(half_cols):
            merge[par * half_cols + col, (2 * col + par - 1) % (2 * half_cols)] = 1
    return merge


def row_spread(channels, row_count):
    pair_rows = row_count // 2 + 1
    core = np.zeros((pair_rows * 4 * channels, 2 * channels * row_count), np.float32)
    edge = np.zeros((8 * channels, 32), np.float32)
    for par_z in range(2):
        for ch in range(channels):
            for at in range(1, row_count + 1):
                target = ((at // 2 * 2 + par_z) * 2 + at % 2) * channels + ch
                core[target, (par_z * channels + ch) * row_count + at - 1] = 1
            edge[(par_z * 2) * channels + ch, par_z * 16 + ch] = 1
            edge[((2 + par_z) * 2 + 1) * channels + ch, par_z * 16 + 8 + ch] = 1
    return core, edge


def tap_spread(channels):
    spread = np.zeros((8, channels * 27, 64 * channels), np.float32)
    for cls in range(8):
        par_z, par_y, par_x = cls // 4, cls // 2 % 2, cls % 2
        for ch in range(channels):
            for off_z in range(3):
                for off_y in range(3):
                    for off_x in range(3):
                        at_z, at_y, at_x = par_z + off_z, par_y + off_y, par_x + off_x
                        place = (at_z // 2 * 2 + at_y // 2) * 2 + at_x // 2
                        place = ((place * 2 + at_x % 2) * 2 + at_z % 2) * 2 + at_y % 2
                        spread[cls, ch * 27 + 9 * off_z + 3 * off_y + off_x, place * channels + ch] = 1
    return spread


def class_order(hidden):
    order = np.zeros((8 * hidden, 8 * hidden), np.float32)
    for ch in range(hidden):
        for cls in range(8):
            order[ch * 8 + cls, cls * hidden + ch] = 1
    return order


def dot(a, b):
    return jnp.dot(a, b, preferred_element_type=f32)


def dot_rows(a, b):
    return lax.dot_general(a, b, (((1,), (1,)), ((), ())), preferred_element_type=f32)


def split_two(value):
    high = value.astype(bf16)
    return high, (value - high.astype(f32)).astype(bf16)


def split_three(value):
    high = value.astype(bf16)
    return (high,) + split_two(value - high.astype(f32))


def conv_rows(conv_ref, tap_ref):
    return jnp.concatenate([dot(conv_ref[...], tap_ref[cls]) for cls in range(8)], axis=0)


def row_of(ref, count):
    return jnp.transpose(jnp.broadcast_to(ref[...], (lanes, count)))


def forward_kernel(
    sizes,
    field_ref,
    below_ref,
    above_ref,
    before_ref,
    after_ref,
    target_ref,
    conv_weight_ref,
    conv_bias_ref,
    down_weight_ref,
    down_bias_ref,
    tap_ref,
    order_ref,
    col_ref,
    row_ref,
    edge_ref,
    out_ref,
    gpre_ref,
    keep_ref,
    give_ref,
    conv_t_ref,
    split_ref,
    conv_ref,
    down_ref,
    down_t_ref,
    gdown_t_ref,
    gconv_t_ref,
    gdb_ref,
    sq_ref,
    hid_ref,
    slope_ref,
    whole_ref,
):
    channels, pairs, half_rows, hidden, out_count, tile, cell_total = sizes
    group = 4 * channels
    cells = half_rows * lanes
    step = pl.program_id(0)

    @pl.when(step == 0)
    def _():
        gdown_t_ref[...] = jnp.zeros_like(gdown_t_ref)
        gconv_t_ref[...] = jnp.zeros_like(gconv_t_ref)
        gdb_ref[...] = jnp.zeros_like(gdb_ref)
        sq_ref[...] = jnp.zeros_like(sq_ref)
        conv = conv_rows(conv_weight_ref, tap_ref)
        conv_t_ref[...] = jnp.transpose(conv).astype(bf16)
        conv_ref[:, : 16 * group] = (0.5 * conv).astype(bf16)
        bias = 0.5 * row_of(conv_bias_ref, hidden)
        at = lax.broadcasted_iota(jnp.int32, bias.shape, 1)
        columns = jnp.zeros_like(bias)
        for k, piece in enumerate(split_three(bias)):
            columns = jnp.where(at == k, piece.astype(f32), columns)
        columns = jnp.concatenate([columns[:, :16]] * 8, axis=0)
        conv_ref[:, 16 * group :] = columns.astype(bf16)
        down = dot(down_weight_ref[...], order_ref[...])
        down_ref[...] = down.astype(bf16)
        down_t_ref[...] = jnp.transpose(down).astype(bf16)
        for slot in range(pairs + 1):
            lower = below_ref if slot == 0 else field_ref.at[:, 2 * slot - 1]
            upper = above_ref if slot == pairs else field_ref.at[:, 2 * slot]
            rows = [ref[ch] for ref in (lower, upper) for ch in range(channels)]
            rows = dot(row_ref[...], jnp.concatenate(rows, axis=0)).astype(bf16)
            rows = dot(rows, col_ref[...])
            sides = [ref[2 * slot + par].astype(f32) for par in range(2) for ref in (before_ref, after_ref)]
            sides = jnp.concatenate(sides, axis=0).astype(bf16)
            sides = dot(dot(edge_ref[...], sides).astype(bf16), col_ref[...])
            for row in range(half_rows + 1):
                piece = rows[row * group : (row + 1) * group]
                if row == 0:
                    piece = piece + sides[:group]
                if row == half_rows:
                    piece = piece + sides[group:]
                piece = jnp.concatenate([piece[:, :lanes], piece[:, lanes:]], axis=0)
                piece = jnp.concatenate([piece, pltpu.roll(piece, lanes - 1, 1)], axis=0)
                split_ref[slot, :, row * lanes : (row + 1) * lanes] = piece.astype(bf16)

    ones = jnp.ones((16, tile), bf16)
    down_bias = row_of(down_bias_ref, out_count)
    down_bias = jnp.concatenate([down_bias] * (tile // lanes), axis=1)
    wanted = jnp.swapaxes(target_ref[:, 0].astype(f32), 0, 1)
    parts = cells // tile
    count = tile // lanes

    def window_of(part):
        start, stop = part * tile, (part + 1) * tile
        return jnp.concatenate(
            [
                split_ref[step + dz, :, start + dy * lanes : stop + dy * lanes]
                for dz in range(2)
                for dy in range(2)
            ]
            + [ones],
            axis=0,
        )

    outputs, diffs = {}, {}

    def activate(part, rows):
        pre = dot(conv_ref[rows], window_of(part))
        square = pre * pre
        tangent = jnp.tanh(pre * (square * (8.0 * gelu_scale * gelu_cubic) + 2.0 * gelu_scale))
        above = 1.0 + tangent
        bend = pre * (square * (12.0 * gelu_scale * gelu_cubic) + gelu_scale)
        hid_ref[part % 2, rows] = (pre * above).astype(bf16)
        slope_ref[part % 2, rows] = above * ((1.0 - tangent) * bend + 0.5)

    def compare(part):
        output = dot(down_ref[...], hid_ref[part % 2]) + down_bias
        first = part * count
        diff = output - jnp.concatenate([wanted[first + k] for k in range(count)], axis=1)
        outputs[part] = [output[:, k * lanes : (k + 1) * lanes] for k in range(count)]
        for k in range(count):
            piece = diff[:, k * lanes : (k + 1) * lanes]
            gdb_ref[...] += piece
            sq_ref[...] += piece * piece
        diffs[part] = diff.astype(bf16)

    def weigh_down(part):
        gdown_t_ref[...] += dot_rows(hid_ref[part % 2], diffs[part])

    def back(part, rows):
        value = dot(down_t_ref[rows], diffs[part]) * slope_ref[part % 2, rows]
        gpre_ref[0, rows, part * tile : (part + 1) * tile] = value.astype(bf16)

    def weigh_conv(part):
        gconv_t_ref[...] += dot_rows(window_of(part), gpre_ref[0, :, part * tile : (part + 1) * tile])

    big = 8 * hidden
    blocks = [slice(0, big)]
    for part in range(parts + 1):
        first = [functools.partial(activate, part, rows) for rows in blocks] if part < parts else []
        second = []
        if part > 0:
            done = part - 1
            second = [functools.partial(compare, done), functools.partial(weigh_down, done)]
            second += [functools.partial(back, done, rows) for rows in blocks]
            second += [functools.partial(weigh_conv, done)]
        for k in range(max(len(first), len(second))):
            if k < len(second):
                second[k]()
            if k < len(first):
                first[k]()
    outputs = [value for part in range(parts) for value in outputs[part]]
    out_ref[:, 0] = jnp.swapaxes(jnp.stack(outputs, axis=0), 0, 1).astype(bf16)

    @pl.when(step == pairs - 1)
    def _():
        taps = channels * 27
        folded = 0.0
        cb = jnp.zeros((hidden, 1), f32)
        gconv = jnp.transpose(gconv_t_ref[...])
        for cls in range(8):
            rows = gconv[cls * hidden : (cls + 1) * hidden]
            cb = cb + rows[:, 16 * group : 16 * group + 1]
            rows = jnp.concatenate(split_three(rows[:, : 16 * group]), axis=0)
            folded = folded + dot_rows(rows, tap_ref[cls])
        folded = folded[:hidden] + (folded[hidden : 2 * hidden] + folded[2 * hidden :])
        columns = [folded, cb]
        for ref, share in ((gdb_ref, 1.0), (sq_ref, 1.0 / out_count)):
            total = share * jnp.sum(ref[...], axis=1, keepdims=True)
            columns += [total[:hidden], total[hidden:]]
        columns.append(jnp.zeros((hidden, 2 * lanes - taps - 5), f32))
        small = jnp.concatenate(columns, axis=1) / cell_total
        pieces = jnp.concatenate(split_three(jnp.transpose(gdown_t_ref[...])), axis=0)
        pieces = dot_rows(pieces, order_ref[...])
        grad_down = pieces[:out_count] + (pieces[out_count : 2 * out_count] + pieces[2 * out_count :])
        rows = out_count // 2
        upper = lax.axis_index("gz") // (lax.axis_size("gz") // 2)
        whole_ref[...] = grad_down / cell_total
        keep_ref[...] = whole_ref[pl.ds(pl.multiple_of(upper * rows, rows), rows)]
        give_ref[:, : 8 * hidden] = whole_ref[pl.ds(pl.multiple_of((1 - upper) * rows, rows), rows)]
        give_ref[:, 8 * hidden :] = small


def merged(piece, group):
    halves = [
        piece[par * group : (par + 1) * group]
        + pltpu.roll(piece[(2 + par) * group : (3 + par) * group], 1, 1)
        for par in range(2)
    ]
    return jnp.concatenate(halves, axis=1)


def sides_kernel(sizes, first_ref, last_ref, conv_t_ref, merge_ref, edge_t_ref, before_ref, after_ref):
    channels, pairs = sizes
    group = 4 * channels
    span = 4 * group
    found = []
    for ref, dy in ((first_ref, 0), (last_ref, 1)):
        weights = jnp.concatenate([conv_t_ref[(2 * dz + dy) * span : (2 * dz + dy + 1) * span] for dz in range(2)], axis=0)
        found.append(dot(weights, jnp.concatenate([ref[pair] for pair in range(pairs)], axis=1)))
    rows = []
    for slot in range(pairs + 1):
        outer = []
        for value in found:
            total = 0.0
            for dz in range(2):
                pair = slot - dz
                if 0 <= pair < pairs:
                    total = total + value[dz * span : (dz + 1) * span, pair * lanes : (pair + 1) * lanes]
            outer.append(merged(total, group))
        rows.append(jnp.concatenate(outer, axis=0))
    for slot in range(pairs + 1):
        sides = 0.0
        for value in split_two(rows[slot]):
            sides = sides + dot(dot(edge_t_ref[...], value).astype(bf16), merge_ref[...])
        for par in range(2):
            before_ref[2 * slot + par] = sides[par * 16 : par * 16 + 8].astype(bf16)
            after_ref[2 * slot + par] = sides[par * 16 + 8 : par * 16 + 16].astype(bf16)


def spread_kernel(sizes, *refs):
    channels, half_rows, tile, plan = sizes
    pairs, slots, taken, done, given = plan
    refs = list(refs)
    gpre_ref, conv_t_ref, merge_ref, row_t_ref = refs[:4]
    taken_refs = refs[4 : 4 + len(taken)]
    core_ref = refs[4 + len(taken)]
    given_refs = refs[5 + len(taken) : -1]
    spread_ref = refs[-1]
    group = 4 * channels
    span = 4 * group
    row_count = 2 * half_rows
    cells = half_rows * lanes
    step = pl.program_id(0)

    def spread_out(pair):
        for part in range(cells // tile):
            spread = dot(conv_t_ref[...], gpre_ref[0, :, part * tile : (part + 1) * tile])
            for dz in range(2):
                for dy in range(2):
                    first = (2 * dz + dy) * span
                    here = slice(part * tile + dy * lanes, (part + 1) * tile + dy * lanes)
                    spread_ref[slots.index(pair + dz), :, here] += spread[first : first + span]

    def finish(slot):
        rows = [
            merged(spread_ref[slots.index(slot), :, row * lanes : (row + 1) * lanes], group)
            for row in range(half_rows + 1)
        ]
        core = 0.0
        for value in split_two(jnp.concatenate(rows, axis=0)):
            core = core + dot(dot(row_t_ref[...], value).astype(bf16), merge_ref[...])
        for par in range(2):
            for ch in range(channels):
                first = (par * channels + ch) * row_count
                core_ref[2 * done.index(slot) + par, ch] = core[first : first + row_count]

    for k, pair in enumerate(pairs):

        @pl.when(step == k)
        def _():
            if k == 0:
                spread_ref[...] = jnp.zeros_like(spread_ref)
                for slot, ref in zip(taken, taken_refs, strict=True):
                    spread_ref[slots.index(slot)] = ref[...]
            for slot in done:
                if all(later not in (slot - 1, slot) for later in pairs[k:]) and slot - 1 != pairs[-1]:
                    if any(before in (slot - 1, slot) for before in pairs[k - 1 : k]):
                        finish(slot)
            spread_out(pair)
            if k == len(pairs) - 1:
                for slot in done:
                    if pair in (slot - 1, slot):
                        finish(slot)
                for slot, ref in zip(given, given_refs, strict=True):
                    ref[...] = spread_ref[slots.index(slot)]


def join_kernel(sizes, *refs):
    channels, depth, row_count, places = sizes
    below_ref, above_ref, before_ref, after_ref, out_ref = refs[-5:]
    for z in range(depth):
        which, at = places[z]
        for ch in range(channels):
            value = refs[which][at, ch]
            if z == 0:
                value = value + above_ref[ch].astype(f32)
            if z == depth - 1:
                value = value + below_ref[ch].astype(f32)
            out_ref[ch, z] = value
            out_ref[ch, z, 0:1] += after_ref[z + 1, ch : ch + 1].astype(f32)
            out_ref[ch, z, row_count - 1 : row_count] += before_ref[z + 1, ch : ch + 1].astype(f32)


def last_kernel(sizes, mine_ref, theirs_ref, conv_out, cbias_out, down_out, dbias_out, loss_out):
    hidden, taps, big = sizes
    total = mine_ref[...] + theirs_ref[...]
    down_out[...] = total[:, :big]
    small = jnp.concatenate(
        [total[:, at : at + 2 * lanes] for at in range(big, total.shape[1], 2 * lanes)], axis=0
    )
    conv_out[...] = small[:, :taps]
    turned = jnp.transpose(small[:, lanes:])
    at = taps - lanes
    cbias_out[...] = turned[at : at + 1]
    dbias_out[...] = jnp.concatenate([turned[at + 1 : at + 2], turned[at + 2 : at + 3]], axis=1)
    loss_out[...] = jnp.sum(turned[at + 3 : at + 4] + turned[at + 4 : at + 5], axis=1, keepdims=True)


def call(kernel, sizes, out_shape, *args, grid=None, in_specs=None, out_specs=None, scratch=(), flops=0, name):
    if grid is None:
        grid = (1,)
        in_specs = [whole(a.shape) for a in args]
        out_specs = [whole(o.shape) for o in out_shape]
    return pl.pallas_call(
        functools.partial(kernel, sizes),
        out_shape=out_shape,
        in_specs=in_specs,
        out_specs=out_specs,
        scratch_shapes=scratch,
        compiler_params=pltpu.CompilerParams(vmem_limit_bytes=56 * 1024 * 1024),
        cost_estimate=pl.CostEstimate(
            flops=flops,
            bytes_accessed=sum(a.size * a.dtype.itemsize for a in (*args, *out_shape)),
            transcendentals=0,
        ),
        name=name,
        grid=grid,
    )(*args)


def whole(shape):
    return pl.BlockSpec(tuple(shape), lambda z: (0,) * len(shape))


def constants(channels, row_count, half_cols, hidden):
    core, edge = row_spread(channels, row_count)
    names = {
        "col": column_merge(half_cols).T,
        "merge": column_merge(half_cols),
        "row": core,
        "row_t": core.T,
        "edge": edge,
        "edge_t": edge.T,
        "tap": tap_spread(channels),
        "order": class_order(hidden),
    }
    return {name: jnp.asarray(value, bf16) for name, value in names.items()}


def forward(fields, below, above, before, after, target, conv_weight, conv_bias, down_weight, down_bias, fixed, cell_total):
    channels, depth, row_count, col_count = fields.shape
    hidden, out_count = conv_weight.shape[0], down_weight.shape[0]
    pairs, half_rows, half_cols = depth // 2, row_count // 2, col_count // 2
    cells = half_rows * half_cols
    big, win = 8 * hidden, 64 * channels
    args = (
        fields, below, above, before, after, target,
        conv_weight, conv_bias[None], down_weight, down_bias[None],
        fixed["tap"], fixed["order"], fixed["col"], fixed["row"], fixed["edge"],
    )
    slab = pl.BlockSpec((out_count, 1, half_rows, half_cols), lambda z: (0, z, 0, 0))
    return call(
        forward_kernel,
        (channels, pairs, half_rows, hidden, out_count, forward_tile, cell_total),
        [
            jax.ShapeDtypeStruct(target.shape, bf16),
            jax.ShapeDtypeStruct((pairs, big, cells), bf16),
            jax.ShapeDtypeStruct((out_count // 2, big), f32),
            jax.ShapeDtypeStruct((out_count // 2, big + 2 * lanes), f32),
            jax.ShapeDtypeStruct((win, big), bf16),
        ],
        *args,
        grid=(pairs,),
        in_specs=[slab if i == 5 else whole(a.shape) for i, a in enumerate(args)],
        out_specs=[
            slab,
            pl.BlockSpec((1, big, cells), lambda z: (z, 0, 0)),
            whole((out_count // 2, big)),
            whole((out_count // 2, big + 2 * lanes)),
            whole((win, big)),
        ],
        scratch=[
            pltpu.VMEM((pairs + 1, 16 * channels, cells + lanes), bf16),
            pltpu.VMEM((big, win + 16), bf16),
            pltpu.VMEM((out_count, big), bf16),
            pltpu.VMEM((big, out_count), bf16),
            pltpu.VMEM((big, out_count), f32),
            pltpu.VMEM((win + 16, big), f32),
            pltpu.VMEM((out_count, lanes), f32),
            pltpu.VMEM((out_count, lanes), f32),
            pltpu.VMEM((2, big, forward_tile), bf16),
            pltpu.VMEM((2, big, forward_tile), f32),
            pltpu.VMEM((out_count, big), f32),
        ],
        flops=4 * pairs * cells * big * (win + out_count),
        name="forward",
    )


def sides(grad_pre, conv_t, fixed, shape):
    channels, depth, _, col_count = shape
    pairs, big, cells = grad_pre.shape
    args = (grad_pre, grad_pre, conv_t, fixed["merge"], fixed["edge_t"])
    out = jax.ShapeDtypeStruct((depth + 2, 8, col_count), bf16)
    outer = [
        pl.BlockSpec((pairs, big, lanes), lambda z: (0, 0, 0)),
        pl.BlockSpec((pairs, big, lanes), lambda z: (0, 0, cells // lanes - 1)),
    ]
    return call(
        sides_kernel,
        (channels, pairs),
        [out, out],
        *args,
        grid=(1,),
        in_specs=outer + [whole(a.shape) for a in args[2:]],
        out_specs=[whole(out.shape)] * 2,
        flops=4 * pairs * big * lanes * conv_t.shape[0],
        name="sides",
    )


def spread(grad_pre, conv_t, fixed, shape, plan, *taken):
    channels, _, row_count, col_count = shape
    _, big, cells = grad_pre.shape
    pairs, slots, _, done, given = plan
    open_shape = (16 * channels, cells + lanes)
    args = (grad_pre, conv_t, fixed["merge"], fixed["row_t"], *taken)
    outs = [jax.ShapeDtypeStruct((2 * len(done), channels, row_count, col_count), f32)]
    outs += [jax.ShapeDtypeStruct(open_shape, f32)] * len(given)
    first = pairs[0]
    stride = pairs[1] - first if len(pairs) > 1 else 1
    return call(
        spread_kernel,
        (channels, row_count // 2, spread_tile, plan),
        outs,
        *args,
        grid=(len(pairs),),
        in_specs=[pl.BlockSpec((1, big, cells), lambda z: (first + stride * z, 0, 0))]
        + [whole(a.shape) for a in args[1:]],
        out_specs=[whole(o.shape) for o in outs],
        scratch=[pltpu.VMEM((len(slots), *open_shape), f32)],
        flops=2 * len(pairs) * cells * big * conv_t.shape[0],
        name="spread",
    )


forward_tile = 1024
spread_tile = 1024


def on_device(fields, target, conv_weight, conv_bias, down_weight, down_bias):
    channels, depth, row_count, col_count = fields.shape
    hidden = conv_weight.shape[0]
    out_count = down_weight.shape[0]
    taps = channels * 27
    big = 8 * hidden
    cell_total = fields.size // channels // 8 * lax.axis_size("gz") * lax.axis_size("gy")
    fixed = constants(channels, row_count, col_count // 2, hidden)

    below = shifted(fields[:, depth - 1], "gz", 1)
    above = shifted(fields[:, 0], "gz", -1)

    def side(row):
        rows = [below[:, row][:, None], fields[:, :, row], above[:, row][:, None]]
        rows = jnp.concatenate(rows, axis=1).transpose(1, 0, 2)
        return jnp.pad(rows, ((0, 0), (0, 8 - channels), (0, 0)))

    before = shifted(side(row_count - 1), "gy", 1)
    after = shifted(side(0), "gy", -1)
    out_field, grad_pre, own, packed, conv_t = forward(
        fields, below, above, before, after, target,
        conv_weight, conv_bias, down_weight, down_bias, fixed, cell_total,
    )
    pairs = depth // 2
    shape = fields.shape

    def beside(value, count):
        return jnp.concatenate(jnp.split(value, value.shape[0] // count, axis=0), axis=1)

    me = lax.axis_index("gz")
    small = packed[:, big:]

    def added(own, small, got):
        pieces = jnp.split(got[:, big:], hidden // own.shape[0], axis=1)
        return own + got[:, :big], small + jnp.concatenate(pieces, axis=0)

    def halved(own, small, bit):
        count = own.shape[0] // 2
        upper = (me // bit) % 2
        give = lax.dynamic_slice_in_dim(own, (1 - upper) * count, count, 0)
        own = lax.dynamic_slice_in_dim(own, upper * count, count, 0)
        return own, jnp.concatenate([give, beside(small, count)], axis=1)

    bit = lax.axis_size("gz") // 2
    got = exchanged(packed, "gz", bit)
    to_before, to_after = sides(grad_pre, conv_t, fixed, shape)
    from_before = shifted(to_after, "gy", 1)
    from_after = shifted(to_before, "gy", -1)
    outer = ((0, pairs - 1), (0, 1, pairs - 1, pairs), (), (0, pairs), (1, pairs - 1))
    outer_core, low_open, high_open = spread(grad_pre, conv_t, fixed, shape, outer)
    own, small = added(own, small, got)
    bit //= 2
    own, packed = halved(own, small, bit)
    packed, low_open = lax.optimization_barrier((packed, low_open))

    def plane(value, at):
        low = from_before[at, :channels, None].astype(f32)
        high = from_after[at, :channels, None].astype(f32)
        gap = jnp.zeros((channels, row_count - 2, col_count), f32)
        return (value + jnp.concatenate([low, gap, high], axis=1)).astype(bf16)

    got = exchanged(packed, "gz", bit)
    from_below = shifted(plane(outer_core[3], depth + 1), "gz", 1)
    from_above = shifted(plane(outer_core[0], 0), "gz", -1)
    middle = pairs // 2
    lower = (tuple(range(1, middle)), tuple(range(1, middle + 1)), (1,), tuple(range(1, middle)), (middle,))
    lower_core, middle_open = spread(grad_pre, conv_t, fixed, shape, lower, low_open)
    own, small = added(own, small, got)
    while bit > 1:
        bit //= 2
        own, packed = halved(own, small, bit)
        own, small = added(own, small, exchanged(packed, "gz", bit))
    packed = jnp.concatenate([own, beside(small, own.shape[0])], axis=1)
    count = own.shape[0]
    packed, middle_open = lax.optimization_barrier((packed, middle_open))

    bit = 1
    got = exchanged(packed, "gy", bit)
    slots = tuple(range(middle, pairs))
    upper = (tuple(range(middle, pairs - 1)), slots, (middle, pairs - 1), slots, ())
    (upper_core,) = spread(grad_pre, conv_t, fixed, shape, upper, middle_open, high_open)
    while 2 * bit < lax.axis_size("gy"):
        packed = packed + got
        bit *= 2
        got = exchanged(packed, "gy", bit)
    places = [(0, 1)] + [(1, at) for at in range(2 * middle - 2)]
    places += [(2, at) for at in range(2 * (pairs - middle))] + [(0, 2)]
    (sensitivity,) = call(
        join_kernel,
        (channels, depth, row_count, tuple(places)),
        [jax.ShapeDtypeStruct(shape, f32)],
        outer_core, lower_core, upper_core, from_above, from_below, from_after, from_before,
        name="join",
    )
    conv, cbias, down, dbias, loss = call(
        last_kernel,
        (hidden, taps, big),
        [
            jax.ShapeDtypeStruct((hidden, taps), f32),
            jax.ShapeDtypeStruct((1, hidden), f32),
            jax.ShapeDtypeStruct((count, big), f32),
            jax.ShapeDtypeStruct((1, out_count), f32),
            jax.ShapeDtypeStruct((1, 1), f32),
        ],
        packed, got,
        name="last",
    )
    return out_field, sensitivity, conv, cbias[0], down, dbias[0], loss[0, 0]


def solution(mesh):
    in_specs = (P(None, "gz", "gy", None), P(None, "gz", "gy", None), P(), P(), P(), P())
    out_specs = (
        P(None, "gz", "gy", None),
        P(None, "gz", "gy", None),
        P(),
        P(),
        P("gz", None),
        P(),
        P(),
    )
    return jax.shard_map(
        on_device, mesh=mesh, in_specs=in_specs, out_specs=out_specs, check_vma=False
    )
```

```python
import functools

import jax
import jax.numpy as jnp
import numpy as np
from jax import lax
from jax.experimental import pallas as pl
from jax.experimental.pallas import tpu as pltpu
from jax.sharding import PartitionSpec as P

gelu_scale = 0.7978845608028654
gelu_cubic = 0.044715
lanes = 128
bf16 = jnp.bfloat16
f32 = jnp.float32


def shifted(value, axis, by):
    count = lax.axis_size(axis)
    return lax.ppermute(value, axis, [(i, (i + by) % count) for i in range(count)])


def exchanged(value, axis, bit):
    count = lax.axis_size(axis)
    return lax.ppermute(value, axis, [(i, i ^ bit) for i in range(count)])


def column_merge(half_cols):
    merge = np.zeros((2 * half_cols, 2 * half_cols), np.float32)
    for par in range(2):
        for col in range(half_cols):
            merge[par * half_cols + col, (2 * col + par - 1) % (2 * half_cols)] = 1
    return merge


def row_spread(channels, row_count):
    pair_rows = row_count // 2 + 1
    core = np.zeros((pair_rows * 4 * channels, 2 * channels * row_count), np.float32)
    edge = np.zeros((8 * channels, 32), np.float32)
    for par_z in range(2):
        for ch in range(channels):
            for at in range(1, row_count + 1):
                target = ((at // 2 * 2 + par_z) * 2 + at % 2) * channels + ch
                core[target, (par_z * channels + ch) * row_count + at - 1] = 1
            edge[(par_z * 2) * channels + ch, par_z * 16 + ch] = 1
            edge[((2 + par_z) * 2 + 1) * channels + ch, par_z * 16 + 8 + ch] = 1
    return core, edge


def tap_spread(channels):
    spread = np.zeros((8, channels * 27, 64 * channels), np.float32)
    for cls in range(8):
        par_z, par_y, par_x = cls // 4, cls // 2 % 2, cls % 2
        for ch in range(channels):
            for off_z in range(3):
                for off_y in range(3):
                    for off_x in range(3):
                        at_z, at_y, at_x = par_z + off_z, par_y + off_y, par_x + off_x
                        place = (at_z // 2 * 2 + at_y // 2) * 2 + at_x // 2
                        place = ((place * 2 + at_x % 2) * 2 + at_z % 2) * 2 + at_y % 2
                        spread[cls, ch * 27 + 9 * off_z + 3 * off_y + off_x, place * channels + ch] = 1
    return spread


def class_order(hidden):
    order = np.zeros((8 * hidden, 8 * hidden), np.float32)
    for ch in range(hidden):
        for cls in range(8):
            order[ch * 8 + cls, cls * hidden + ch] = 1
    return order


def dot(a, b):
    return jnp.dot(a, b, preferred_element_type=f32)


def dot_rows(a, b):
    return lax.dot_general(a, b, (((1,), (1,)), ((), ())), preferred_element_type=f32)


def split_two(value):
    high = value.astype(bf16)
    return high, (value - high.astype(f32)).astype(bf16)


def split_three(value):
    high = value.astype(bf16)
    return (high,) + split_two(value - high.astype(f32))


def conv_rows(conv_ref, tap_ref):
    return jnp.concatenate([dot(conv_ref[...], tap_ref[cls]) for cls in range(8)], axis=0)


def row_of(ref, count):
    return jnp.transpose(jnp.broadcast_to(ref[...], (lanes, count)))


def prepare_kernel(
    sizes,
    field_ref,
    below_ref,
    above_ref,
    conv_weight_ref,
    conv_bias_ref,
    down_weight_ref,
    tap_ref,
    order_ref,
    col_ref,
    row_ref,
    split_ref,
    conv_ref,
    conv_t_ref,
    down_ref,
    down_t_ref,
):
    channels, pairs, half_rows, hidden = sizes
    group = 4 * channels
    conv = conv_rows(conv_weight_ref, tap_ref)
    conv_t_ref[...] = jnp.transpose(conv).astype(bf16)
    conv_ref[:, : 16 * group] = (0.5 * conv).astype(bf16)
    bias = 0.5 * row_of(conv_bias_ref, hidden)
    at = lax.broadcasted_iota(jnp.int32, bias.shape, 1)
    columns = jnp.zeros_like(bias)
    for k, piece in enumerate(split_three(bias)):
        columns = jnp.where(at == k, piece.astype(f32), columns)
    columns = jnp.concatenate([columns[:, :16]] * 8, axis=0)
    conv_ref[:, 16 * group :] = columns.astype(bf16)
    down = dot(down_weight_ref[...], order_ref[...])
    down_ref[...] = down.astype(bf16)
    down_t_ref[...] = jnp.transpose(down).astype(bf16)
    for slot in range(pairs + 1):
        lower = below_ref if slot == 0 else field_ref.at[:, 2 * slot - 1]
        upper = above_ref if slot == pairs else field_ref.at[:, 2 * slot]
        rows = [ref[ch] for ref in (lower, upper) for ch in range(channels)]
        rows = dot(row_ref[...], jnp.concatenate(rows, axis=0)).astype(bf16)
        rows = dot(rows, col_ref[...])
        for row in range(half_rows + 1):
            piece = rows[row * group : (row + 1) * group]
            split_ref[slot, :, row * lanes : (row + 1) * lanes] = shifts_of(piece).astype(bf16)


def shifts_of(piece):
    piece = jnp.concatenate([piece[:, :lanes], piece[:, lanes:]], axis=0)
    return jnp.concatenate([piece, pltpu.roll(piece, lanes - 1, 1)], axis=0)


def forward_kernel(
    sizes,
    early_ref,
    before_ref,
    after_ref,
    target_ref,
    conv_ref,
    conv_t_ref,
    down_ref,
    down_t_ref,
    down_bias_ref,
    tap_ref,
    order_ref,
    col_ref,
    edge_ref,
    merge_ref,
    edge_t_ref,
    out_ref,
    gpre_ref,
    keep_ref,
    give_ref,
    to_before_ref,
    to_after_ref,
    split_ref,
    gdown_t_ref,
    gconv_t_ref,
    gdb_ref,
    sq_ref,
    hid_ref,
    slope_ref,
    whole_ref,
    outer_ref,
    sem,
):
    channels, pairs, half_rows, hidden, out_count, tile, cell_total = sizes
    group = 4 * channels
    cells = half_rows * lanes
    step = pl.program_id(0)

    @pl.when(step == 0)
    def _():
        copy = pltpu.make_async_copy(early_ref, split_ref, sem)
        copy.start()
        gdown_t_ref[...] = jnp.zeros_like(gdown_t_ref)
        gconv_t_ref[...] = jnp.zeros_like(gconv_t_ref)
        gdb_ref[...] = jnp.zeros_like(gdb_ref)
        sq_ref[...] = jnp.zeros_like(sq_ref)
        pieces = []
        for slot in range(pairs + 1):
            sides = [ref[2 * slot + par].astype(f32) for par in range(2) for ref in (before_ref, after_ref)]
            sides = jnp.concatenate(sides, axis=0).astype(bf16)
            sides = dot(dot(edge_ref[...], sides).astype(bf16), col_ref[...])
            pieces.append((shifts_of(sides[:group]), shifts_of(sides[group:])))
        copy.wait()
        for slot in range(pairs + 1):
            for piece, row in zip(pieces[slot], (0, half_rows), strict=True):
                here = slice(row * lanes, (row + 1) * lanes)
                split_ref[slot, :, here] = (split_ref[slot, :, here].astype(f32) + piece).astype(bf16)

    ones = jnp.ones((16, tile), bf16)
    down_bias = row_of(down_bias_ref, out_count)
    down_bias = jnp.concatenate([down_bias] * (tile // lanes), axis=1)
    wanted = jnp.swapaxes(target_ref[:, 0].astype(f32), 0, 1)
    parts = cells // tile
    count = tile // lanes

    def window_of(part):
        start, stop = part * tile, (part + 1) * tile
        return jnp.concatenate(
            [
                split_ref[step + dz, :, start + dy * lanes : stop + dy * lanes]
                for dz in range(2)
                for dy in range(2)
            ]
            + [ones],
            axis=0,
        )

    outputs, diffs = {}, {}

    def activate(part, rows):
        pre = dot(conv_ref[rows], window_of(part))
        square = pre * pre
        tangent = jnp.tanh(pre * (square * (8.0 * gelu_scale * gelu_cubic) + 2.0 * gelu_scale))
        above = 1.0 + tangent
        bend = pre * (square * (12.0 * gelu_scale * gelu_cubic) + gelu_scale)
        hid_ref[part % 2, rows] = (pre * above).astype(bf16)
        slope_ref[part % 2, rows] = above * ((1.0 - tangent) * bend + 0.5)

    def compare(part):
        output = dot(down_ref[...], hid_ref[part % 2]) + down_bias
        first = part * count
        diff = output - jnp.concatenate([wanted[first + k] for k in range(count)], axis=1)
        outputs[part] = [output[:, k * lanes : (k + 1) * lanes] for k in range(count)]
        for k in range(count):
            piece = diff[:, k * lanes : (k + 1) * lanes]
            gdb_ref[...] += piece
            sq_ref[...] += piece * piece
        diffs[part] = diff.astype(bf16)

    def weigh_down(part):
        gdown_t_ref[...] += dot_rows(hid_ref[part % 2], diffs[part])

    def back(part, rows):
        value = dot(down_t_ref[rows], diffs[part]) * slope_ref[part % 2, rows]
        gpre_ref[0, rows, part * tile : (part + 1) * tile] = value.astype(bf16)

    def weigh_conv(part):
        gconv_t_ref[...] += dot_rows(window_of(part), gpre_ref[0, :, part * tile : (part + 1) * tile])

    big = 8 * hidden
    blocks = [slice(0, big)]
    for part in range(parts + 1):
        first = [functools.partial(activate, part, rows) for rows in blocks] if part < parts else []
        second = []
        if part > 0:
            done = part - 1
            second = [functools.partial(compare, done), functools.partial(weigh_down, done)]
            second += [functools.partial(back, done, rows) for rows in blocks]
            second += [functools.partial(weigh_conv, done)]
        for k in range(max(len(first), len(second))):
            if k < len(second):
                second[k]()
            if k < len(first):
                first[k]()
    for side, at in enumerate((0, cells - lanes)):
        outer_ref[side, step] = gpre_ref[0, :, at : at + lanes]
    outputs = [value for part in range(parts) for value in outputs[part]]
    out_ref[:, 0] = jnp.swapaxes(jnp.stack(outputs, axis=0), 0, 1).astype(bf16)

    @pl.when(step == pairs - 1)
    def _():
        taps = channels * 27
        folded = 0.0
        cb = jnp.zeros((hidden, 1), f32)
        gconv = jnp.transpose(gconv_t_ref[...])
        for cls in range(8):
            rows = gconv[cls * hidden : (cls + 1) * hidden]
            cb = cb + rows[:, 16 * group : 16 * group + 1]
            rows = jnp.concatenate(split_three(rows[:, : 16 * group]), axis=0)
            folded = folded + dot_rows(rows, tap_ref[cls])
        folded = folded[:hidden] + (folded[hidden : 2 * hidden] + folded[2 * hidden :])
        columns = [folded, cb]
        for ref, share in ((gdb_ref, 1.0), (sq_ref, 1.0 / out_count)):
            total = share * jnp.sum(ref[...], axis=1, keepdims=True)
            columns += [total[:hidden], total[hidden:]]
        columns.append(jnp.zeros((hidden, 2 * lanes - taps - 5), f32))
        small = jnp.concatenate(columns, axis=1) / cell_total
        pieces = jnp.concatenate(split_three(jnp.transpose(gdown_t_ref[...])), axis=0)
        pieces = dot_rows(pieces, order_ref[...])
        grad_down = pieces[:out_count] + (pieces[out_count : 2 * out_count] + pieces[2 * out_count :])
        rows = out_count // 2
        upper = lax.axis_index("gz") // (lax.axis_size("gz") // 2)
        whole_ref[...] = grad_down / cell_total
        keep_ref[...] = whole_ref[pl.ds(pl.multiple_of(upper * rows, rows), rows)]
        give_ref[:, : 8 * hidden] = whole_ref[pl.ds(pl.multiple_of((1 - upper) * rows, rows), rows)]
        give_ref[:, 8 * hidden :] = small
        sides_of(channels, pairs, outer_ref, conv_t_ref, merge_ref, edge_t_ref, to_before_ref, to_after_ref)


def merged(piece, group):
    halves = [
        piece[par * group : (par + 1) * group]
        + pltpu.roll(piece[(2 + par) * group : (3 + par) * group], 1, 1)
        for par in range(2)
    ]
    return jnp.concatenate(halves, axis=1)


def sides_of(channels, pairs, outer_ref, conv_t_ref, merge_ref, edge_t_ref, before_ref, after_ref):
    group = 4 * channels
    span = 4 * group
    found = []
    for dy in range(2):
        weights = [conv_t_ref[(2 * dz + dy) * span : (2 * dz + dy + 1) * span] for dz in range(2)]
        values = [outer_ref[dy, pair] for pair in range(pairs)]
        found.append(dot(jnp.concatenate(weights, axis=0), jnp.concatenate(values, axis=1)))
    rows = []
    for slot in range(pairs + 1):
        outer = []
        for value in found:
            total = 0.0
            for dz in range(2):
                pair = slot - dz
                if 0 <= pair < pairs:
                    total = total + value[dz * span : (dz + 1) * span, pair * lanes : (pair + 1) * lanes]
            outer.append(merged(total, group))
        rows.append(jnp.concatenate(outer, axis=0))
    for slot in range(pairs + 1):
        sides = 0.0
        for value in split_two(rows[slot]):
            sides = sides + dot(dot(edge_t_ref[...], value).astype(bf16), merge_ref[...])
        for par in range(2):
            before_ref[2 * slot + par] = sides[par * 16 : par * 16 + 8].astype(bf16)
            after_ref[2 * slot + par] = sides[par * 16 + 8 : par * 16 + 16].astype(bf16)


def spread_kernel(sizes, *refs):
    channels, half_rows, tile, plan = sizes
    pairs, slots, taken, done, given = plan
    refs = list(refs)
    gpre_ref, conv_t_ref, merge_ref, row_t_ref = refs[:4]
    taken_refs = refs[4 : 4 + len(taken)]
    core_ref = refs[4 + len(taken)]
    given_refs = refs[5 + len(taken) : -1]
    spread_ref = refs[-1]
    group = 4 * channels
    span = 4 * group
    row_count = 2 * half_rows
    cells = half_rows * lanes
    step = pl.program_id(0)

    def spread_out(pair):
        for part in range(cells // tile):
            spread = dot(conv_t_ref[...], gpre_ref[0, :, part * tile : (part + 1) * tile])
            for dz in range(2):
                for dy in range(2):
                    first = (2 * dz + dy) * span
                    here = slice(part * tile + dy * lanes, (part + 1) * tile + dy * lanes)
                    spread_ref[slots.index(pair + dz), :, here] += spread[first : first + span]

    def finish(slot):
        rows = [
            merged(spread_ref[slots.index(slot), :, row * lanes : (row + 1) * lanes], group)
            for row in range(half_rows + 1)
        ]
        core = 0.0
        for value in split_two(jnp.concatenate(rows, axis=0)):
            core = core + dot(dot(row_t_ref[...], value).astype(bf16), merge_ref[...])
        for par in range(2):
            for ch in range(channels):
                first = (par * channels + ch) * row_count
                core_ref[2 * done.index(slot) + par, ch] = core[first : first + row_count]

    for k, pair in enumerate(pairs):

        @pl.when(step == k)
        def _():
            if k == 0:
                spread_ref[...] = jnp.zeros_like(spread_ref)
                for slot, ref in zip(taken, taken_refs, strict=True):
                    spread_ref[slots.index(slot)] = ref[...]
            for slot in done:
                if all(later not in (slot - 1, slot) for later in pairs[k:]) and slot - 1 != pairs[-1]:
                    if any(before in (slot - 1, slot) for before in pairs[k - 1 : k]):
                        finish(slot)
            spread_out(pair)
            if k == len(pairs) - 1:
                for slot in done:
                    if pair in (slot - 1, slot):
                        finish(slot)
                for slot, ref in zip(given, given_refs, strict=True):
                    ref[...] = spread_ref[slots.index(slot)]


def join_kernel(sizes, *refs):
    channels, depth, row_count, places = sizes
    below_ref, above_ref, before_ref, after_ref, out_ref = refs[-5:]
    for z in range(depth):
        which, at = places[z]
        for ch in range(channels):
            value = refs[which][at, ch]
            if z == 0:
                value = value + above_ref[ch].astype(f32)
            if z == depth - 1:
                value = value + below_ref[ch].astype(f32)
            out_ref[ch, z] = value
            out_ref[ch, z, 0:1] += after_ref[z + 1, ch : ch + 1].astype(f32)
            out_ref[ch, z, row_count - 1 : row_count] += before_ref[z + 1, ch : ch + 1].astype(f32)


def last_kernel(sizes, mine_ref, theirs_ref, conv_out, cbias_out, down_out, dbias_out, loss_out):
    hidden, taps, big = sizes
    total = mine_ref[...] + theirs_ref[...]
    down_out[...] = total[:, :big]
    small = jnp.concatenate(
        [total[:, at : at + 2 * lanes] for at in range(big, total.shape[1], 2 * lanes)], axis=0
    )
    conv_out[...] = small[:, :taps]
    turned = jnp.transpose(small[:, lanes:])
    at = taps - lanes
    cbias_out[...] = turned[at : at + 1]
    dbias_out[...] = jnp.concatenate([turned[at + 1 : at + 2], turned[at + 2 : at + 3]], axis=1)
    loss_out[...] = jnp.sum(turned[at + 3 : at + 4] + turned[at + 4 : at + 5], axis=1, keepdims=True)


def call(kernel, sizes, out_shape, *args, grid=None, in_specs=None, out_specs=None, scratch=(), flops=0, name):
    if grid is None:
        grid = (1,)
        in_specs = [whole(a.shape) for a in args]
        out_specs = [whole(o.shape) for o in out_shape]
    return pl.pallas_call(
        functools.partial(kernel, sizes),
        out_shape=out_shape,
        in_specs=in_specs,
        out_specs=out_specs,
        scratch_shapes=scratch,
        compiler_params=pltpu.CompilerParams(vmem_limit_bytes=56 * 1024 * 1024),
        cost_estimate=pl.CostEstimate(
            flops=flops,
            bytes_accessed=sum(a.size * a.dtype.itemsize for a in (*args, *out_shape)),
            transcendentals=0,
        ),
        name=name,
        grid=grid,
    )(*args)


def whole(shape):
    return pl.BlockSpec(tuple(shape), lambda z: (0,) * len(shape))


def constants(channels, row_count, half_cols, hidden):
    core, edge = row_spread(channels, row_count)
    names = {
        "col": column_merge(half_cols).T,
        "merge": column_merge(half_cols),
        "row": core,
        "row_t": core.T,
        "edge": edge,
        "edge_t": edge.T,
        "tap": tap_spread(channels),
        "order": class_order(hidden),
    }
    return {name: jnp.asarray(value, bf16) for name, value in names.items()}


def prepare(fields, below, above, conv_weight, conv_bias, down_weight, fixed):
    channels, depth, row_count, _ = fields.shape
    hidden, out_count = conv_weight.shape[0], down_weight.shape[0]
    pairs, half_rows = depth // 2, row_count // 2
    big, win = 8 * hidden, 64 * channels
    return call(
        prepare_kernel,
        (channels, pairs, half_rows, hidden),
        [
            jax.ShapeDtypeStruct((pairs + 1, 16 * channels, (half_rows + 1) * lanes), bf16),
            jax.ShapeDtypeStruct((big, win + 16), bf16),
            jax.ShapeDtypeStruct((win, big), bf16),
            jax.ShapeDtypeStruct((out_count, big), bf16),
            jax.ShapeDtypeStruct((big, out_count), bf16),
        ],
        fields, below, above, conv_weight, conv_bias[None], down_weight,
        fixed["tap"], fixed["order"], fixed["col"], fixed["row"],
        flops=2 * fields.size * row_count * channels * 4,
        name="prepare",
    )


def forward(early, before, after, target, conv, conv_t, down, down_t, down_bias, fixed, channels, cell_total):
    out_count, pairs, half_rows, half_cols = target.shape
    win, big = conv_t.shape
    hidden = big // 8
    cells = half_rows * half_cols
    args = (
        early, before, after, target, conv, conv_t, down, down_t, down_bias[None],
        fixed["tap"], fixed["order"], fixed["col"], fixed["edge"], fixed["merge"], fixed["edge_t"],
    )
    slab = pl.BlockSpec((out_count, 1, half_rows, half_cols), lambda z: (0, z, 0, 0))
    in_specs = [whole(a.shape) for a in args]
    in_specs[0] = pl.BlockSpec(memory_space=pl.ANY)
    in_specs[3] = slab
    return call(
        forward_kernel,
        (channels, pairs, half_rows, hidden, out_count, forward_tile, cell_total),
        [
            jax.ShapeDtypeStruct(target.shape, bf16),
            jax.ShapeDtypeStruct((pairs, big, cells), bf16),
            jax.ShapeDtypeStruct((out_count // 2, big), f32),
            jax.ShapeDtypeStruct((out_count // 2, big + 2 * lanes), f32),
            jax.ShapeDtypeStruct(before.shape, bf16),
            jax.ShapeDtypeStruct(after.shape, bf16),
        ],
        *args,
        grid=(pairs,),
        in_specs=in_specs,
        out_specs=[
            slab,
            pl.BlockSpec((1, big, cells), lambda z: (z, 0, 0)),
            whole((out_count // 2, big)),
            whole((out_count // 2, big + 2 * lanes)),
            whole(before.shape),
            whole(after.shape),
        ],
        scratch=[
            pltpu.VMEM(early.shape, bf16),
            pltpu.VMEM((big, out_count), f32),
            pltpu.VMEM((win + 16, big), f32),
            pltpu.VMEM((out_count, lanes), f32),
            pltpu.VMEM((out_count, lanes), f32),
            pltpu.VMEM((2, big, forward_tile), bf16),
            pltpu.VMEM((2, big, forward_tile), f32),
            pltpu.VMEM((out_count, big), f32),
            pltpu.VMEM((2, pairs, big, lanes), bf16),
            pltpu.SemaphoreType.DMA,
        ],
        flops=4 * pairs * cells * big * (win + out_count),
        name="forward",
    )


def spread(grad_pre, conv_t, fixed, shape, plan, *taken):
    channels, _, row_count, col_count = shape
    _, big, cells = grad_pre.shape
    pairs, slots, _, done, given = plan
    open_shape = (16 * channels, cells + lanes)
    args = (grad_pre, conv_t, fixed["merge"], fixed["row_t"], *taken)
    outs = [jax.ShapeDtypeStruct((2 * len(done), channels, row_count, col_count), f32)]
    outs += [jax.ShapeDtypeStruct(open_shape, f32)] * len(given)
    first = pairs[0]
    stride = pairs[1] - first if len(pairs) > 1 else 1
    return call(
        spread_kernel,
        (channels, row_count // 2, spread_tile, plan),
        outs,
        *args,
        grid=(len(pairs),),
        in_specs=[pl.BlockSpec((1, big, cells), lambda z: (first + stride * z, 0, 0))]
        + [whole(a.shape) for a in args[1:]],
        out_specs=[whole(o.shape) for o in outs],
        scratch=[pltpu.VMEM((len(slots), *open_shape), f32)],
        flops=2 * len(pairs) * cells * big * conv_t.shape[0],
        name="spread",
    )


forward_tile = 1024
spread_tile = 1024


def on_device(fields, target, conv_weight, conv_bias, down_weight, down_bias):
    channels, depth, row_count, col_count = fields.shape
    hidden = conv_weight.shape[0]
    out_count = down_weight.shape[0]
    taps = channels * 27
    big = 8 * hidden
    cell_total = fields.size // channels // 8 * lax.axis_size("gz") * lax.axis_size("gy")
    fixed = constants(channels, row_count, col_count // 2, hidden)

    below = shifted(fields[:, depth - 1], "gz", 1)
    above = shifted(fields[:, 0], "gz", -1)

    def side(row):
        rows = [below[:, row][:, None], fields[:, :, row], above[:, row][:, None]]
        rows = jnp.concatenate(rows, axis=1).transpose(1, 0, 2)
        return jnp.pad(rows, ((0, 0), (0, 8 - channels), (0, 0)))

    before = shifted(side(row_count - 1), "gy", 1)
    after = shifted(side(0), "gy", -1)
    early, conv_big, conv_t, down_big, down_t = prepare(
        fields, below, above, conv_weight, conv_bias, down_weight, fixed
    )
    out_field, grad_pre, own, packed, to_before, to_after = forward(
        early, before, after, target, conv_big, conv_t, down_big, down_t, down_bias, fixed, channels, cell_total
    )
    pairs = depth // 2
    shape = fields.shape

    def beside(value, count):
        return jnp.concatenate(jnp.split(value, value.shape[0] // count, axis=0), axis=1)

    me = lax.axis_index("gz")
    small = packed[:, big:]

    def added(own, small, got):
        pieces = jnp.split(got[:, big:], hidden // own.shape[0], axis=1)
        return own + got[:, :big], small + jnp.concatenate(pieces, axis=0)

    def halved(own, small, bit):
        count = own.shape[0] // 2
        upper = (me // bit) % 2
        give = lax.dynamic_slice_in_dim(own, (1 - upper) * count, count, 0)
        own = lax.dynamic_slice_in_dim(own, upper * count, count, 0)
        return own, jnp.concatenate([give, beside(small, count)], axis=1)

    bit = lax.axis_size("gz") // 2
    got = exchanged(packed, "gz", bit)
    from_before = shifted(to_after, "gy", 1)
    from_after = shifted(to_before, "gy", -1)
    outer = ((0, pairs - 1), (0, 1, pairs - 1, pairs), (), (0, pairs), (1, pairs - 1))
    outer_core, low_open, high_open = spread(grad_pre, conv_t, fixed, shape, outer)
    own, small = added(own, small, got)
    bit //= 2
    own, packed = halved(own, small, bit)
    packed, low_open = lax.optimization_barrier((packed, low_open))

    def plane(value, at):
        low = from_before[at, :channels, None].astype(f32)
        high = from_after[at, :channels, None].astype(f32)
        gap = jnp.zeros((channels, row_count - 2, col_count), f32)
        return (value + jnp.concatenate([low, gap, high], axis=1)).astype(bf16)

    got = exchanged(packed, "gz", bit)
    from_below = shifted(plane(outer_core[3], depth + 1), "gz", 1)
    from_above = shifted(plane(outer_core[0], 0), "gz", -1)
    middle = pairs // 2
    lower = (tuple(range(1, middle)), tuple(range(1, middle + 1)), (1,), tuple(range(1, middle)), (middle,))
    lower_core, middle_open = spread(grad_pre, conv_t, fixed, shape, lower, low_open)
    own, small = added(own, small, got)
    own, small, middle_open = lax.optimization_barrier((own, small, middle_open))
    while bit > 1:
        bit //= 2
        own, packed = halved(own, small, bit)
        own, small = added(own, small, exchanged(packed, "gz", bit))
    packed = jnp.concatenate([own, beside(small, own.shape[0])], axis=1)
    count = own.shape[0]
    packed, middle_open = lax.optimization_barrier((packed, middle_open))

    bit = 1
    got = exchanged(packed, "gy", bit)
    slots = tuple(range(middle, pairs))
    upper = (tuple(range(middle, pairs - 1)), slots, (middle, pairs - 1), slots, ())
    (upper_core,) = spread(grad_pre, conv_t, fixed, shape, upper, middle_open, high_open)
    while 2 * bit < lax.axis_size("gy"):
        packed = packed + got
        bit *= 2
        got = exchanged(packed, "gy", bit)
    places = [(0, 1)] + [(1, at) for at in range(2 * middle - 2)]
    places += [(2, at) for at in range(2 * (pairs - middle))] + [(0, 2)]
    (sensitivity,) = call(
        join_kernel,
        (channels, depth, row_count, tuple(places)),
        [jax.ShapeDtypeStruct(shape, f32)],
        outer_core, lower_core, upper_core, from_above, from_below, from_after, from_before,
        name="join",
    )
    conv, cbias, down, dbias, loss = call(
        last_kernel,
        (hidden, taps, big),
        [
            jax.ShapeDtypeStruct((hidden, taps), f32),
            jax.ShapeDtypeStruct((1, hidden), f32),
            jax.ShapeDtypeStruct((count, big), f32),
            jax.ShapeDtypeStruct((1, out_count), f32),
            jax.ShapeDtypeStruct((1, 1), f32),
        ],
        packed, got,
        name="last",
    )
    return out_field, sensitivity, conv, cbias[0], down, dbias[0], loss[0, 0]


def solution(mesh):
    in_specs = (P(None, "gz", "gy", None), P(None, "gz", "gy", None), P(), P(), P(), P())
    out_specs = (
        P(None, "gz", "gy", None),
        P(None, "gz", "gy", None),
        P(),
        P(),
        P("gz", None),
        P(),
        P(),
    )
    return jax.shard_map(
        on_device, mesh=mesh, in_specs=in_specs, out_specs=out_specs, check_vma=False
    )
```

```python
import functools

import jax
import jax.numpy as jnp
import numpy as np
from jax import lax
from jax.experimental import pallas as pl
from jax.experimental.pallas import tpu as pltpu
from jax.sharding import PartitionSpec as P

gelu_scale = 0.7978845608028654
gelu_cubic = 0.044715
lanes = 128
bf16 = jnp.bfloat16
f32 = jnp.float32


def shifted(value, axis, by):
    count = lax.axis_size(axis)
    return lax.ppermute(value, axis, [(i, (i + by) % count) for i in range(count)])


def exchanged(value, axis, bit):
    count = lax.axis_size(axis)
    return lax.ppermute(value, axis, [(i, i ^ bit) for i in range(count)])


def column_merge(half_cols):
    merge = np.zeros((2 * half_cols, 2 * half_cols), np.float32)
    for par in range(2):
        for col in range(half_cols):
            merge[par * half_cols + col, (2 * col + par - 1) % (2 * half_cols)] = 1
    return merge


def row_spread(channels, row_count):
    pair_rows = row_count // 2 + 1
    core = np.zeros((pair_rows * 4 * channels, 2 * channels * row_count), np.float32)
    edge = np.zeros((8 * channels, 32), np.float32)
    for par_z in range(2):
        for ch in range(channels):
            for at in range(1, row_count + 1):
                target = ((at // 2 * 2 + par_z) * 2 + at % 2) * channels + ch
                core[target, (par_z * channels + ch) * row_count + at - 1] = 1
            edge[(par_z * 2) * channels + ch, par_z * 16 + ch] = 1
            edge[((2 + par_z) * 2 + 1) * channels + ch, par_z * 16 + 8 + ch] = 1
    return core, edge


def tap_spread(channels):
    spread = np.zeros((8, channels * 27, 64 * channels), np.float32)
    for cls in range(8):
        par_z, par_y, par_x = cls // 4, cls // 2 % 2, cls % 2
        for ch in range(channels):
            for off_z in range(3):
                for off_y in range(3):
                    for off_x in range(3):
                        at_z, at_y, at_x = par_z + off_z, par_y + off_y, par_x + off_x
                        place = (at_z // 2 * 2 + at_y // 2) * 2 + at_x // 2
                        place = ((place * 2 + at_x % 2) * 2 + at_z % 2) * 2 + at_y % 2
                        spread[cls, ch * 27 + 9 * off_z + 3 * off_y + off_x, place * channels + ch] = 1
    return spread


def class_order(hidden):
    order = np.zeros((8 * hidden, 8 * hidden), np.float32)
    for ch in range(hidden):
        for cls in range(8):
            order[ch * 8 + cls, cls * hidden + ch] = 1
    return order


def dot(a, b):
    return jnp.dot(a, b, preferred_element_type=f32)


def dot_rows(a, b):
    return lax.dot_general(a, b, (((1,), (1,)), ((), ())), preferred_element_type=f32)


def split_two(value):
    high = value.astype(bf16)
    return high, (value - high.astype(f32)).astype(bf16)


def split_three(value):
    high = value.astype(bf16)
    return (high,) + split_two(value - high.astype(f32))


def conv_rows(conv_ref, tap_ref):
    return jnp.concatenate([dot(conv_ref[...], tap_ref[cls]) for cls in range(8)], axis=0)


def row_of(ref, count):
    return jnp.transpose(jnp.broadcast_to(ref[...], (lanes, count)))


def weights_kernel(
    sizes,
    conv_weight_ref,
    conv_bias_ref,
    down_weight_ref,
    tap_ref,
    order_ref,
    conv_ref,
    conv_t_ref,
    down_ref,
    down_t_ref,
):
    hidden, win = sizes
    conv = conv_rows(conv_weight_ref, tap_ref)
    conv_t_ref[...] = jnp.transpose(conv).astype(bf16)
    conv_ref[:, :win] = (0.5 * conv).astype(bf16)
    bias = 0.5 * row_of(conv_bias_ref, hidden)
    at = lax.broadcasted_iota(jnp.int32, bias.shape, 1)
    columns = jnp.zeros_like(bias)
    for k, piece in enumerate(split_three(bias)):
        columns = jnp.where(at == k, piece.astype(f32), columns)
    columns = jnp.concatenate([columns[:, :16]] * 8, axis=0)
    conv_ref[:, win:] = columns.astype(bf16)
    down = dot(down_weight_ref[...], order_ref[...])
    down_ref[...] = down.astype(bf16)
    down_t_ref[...] = jnp.transpose(down).astype(bf16)


def cells_kernel(sizes, field_ref, below_ref, above_ref, col_ref, row_ref, split_ref):
    channels, pairs, half_rows = sizes
    group = 4 * channels
    for slot in range(pairs + 1):
        lower = below_ref if slot == 0 else field_ref.at[:, 2 * slot - 1]
        upper = above_ref if slot == pairs else field_ref.at[:, 2 * slot]
        rows = [ref[ch] for ref in (lower, upper) for ch in range(channels)]
        rows = dot(row_ref[...], jnp.concatenate(rows, axis=0)).astype(bf16)
        rows = dot(rows, col_ref[...])
        for row in range(half_rows + 1):
            piece = rows[row * group : (row + 1) * group]
            split_ref[slot, :, row * lanes : (row + 1) * lanes] = shifts_of(piece).astype(bf16)


def shifts_of(piece):
    piece = jnp.concatenate([piece[:, :lanes], piece[:, lanes:]], axis=0)
    return jnp.concatenate([piece, pltpu.roll(piece, lanes - 1, 1)], axis=0)


def forward_kernel(
    sizes,
    early_ref,
    before_ref,
    after_ref,
    target_ref,
    conv_ref,
    conv_t_ref,
    down_ref,
    down_t_ref,
    down_bias_ref,
    far_tap_ref,
    far_order_ref,
    col_ref,
    edge_ref,
    merge_ref,
    edge_t_ref,
    out_ref,
    gpre_ref,
    keep_ref,
    give_ref,
    to_before_ref,
    to_after_ref,
    split_ref,
    gdown_t_ref,
    gconv_t_ref,
    gdb_ref,
    sq_ref,
    hid_ref,
    slope_ref,
    whole_ref,
    outer_ref,
    tap_ref,
    order_ref,
    sides_ref,
    split_sem,
    late_sem,
):
    channels, pairs, half_rows, hidden, out_count, tile, cell_total = sizes
    group = 4 * channels
    cells = half_rows * lanes
    step = pl.program_id(0)

    def arrival(slot):
        return pltpu.make_async_copy(early_ref.at[slot], split_ref.at[slot], split_sem.at[slot])

    late = [
        pltpu.make_async_copy(far_tap_ref, tap_ref, late_sem.at[0]),
        pltpu.make_async_copy(far_order_ref, order_ref, late_sem.at[1]),
    ]

    def complete(slot):
        arrival(slot).wait()
        for side, row in enumerate((0, half_rows)):
            here = slice(row * lanes, (row + 1) * lanes)
            value = split_ref[slot, :, here].astype(f32) + sides_ref[slot, side]
            split_ref[slot, :, here] = value.astype(bf16)

    @pl.when(step == 0)
    def _():
        for slot in range(pairs + 1):
            arrival(slot).start()
        for copy in late:
            copy.start()
        gdown_t_ref[...] = jnp.zeros_like(gdown_t_ref)
        gconv_t_ref[...] = jnp.zeros_like(gconv_t_ref)
        gdb_ref[...] = jnp.zeros_like(gdb_ref)
        sq_ref[...] = jnp.zeros_like(sq_ref)
        width = 2 * lanes
        rows = []
        for slot in range(pairs + 1):
            sides = [ref[2 * slot + par].astype(f32) for par in range(2) for ref in (before_ref, after_ref)]
            rows.append(jnp.concatenate(sides, axis=0).astype(bf16))
        rows = dot(edge_ref[...], jnp.concatenate(rows, axis=1)).astype(bf16)
        rows = [rows[:, slot * width : (slot + 1) * width] for slot in range(pairs + 1)]
        rows = dot(jnp.concatenate(rows, axis=0), col_ref[...])
        for slot in range(pairs + 1):
            for side in range(2):
                first = (2 * slot + side) * group
                sides_ref[slot, side] = shifts_of(rows[first : first + group])
        complete(0)

    complete(step + 1)

    ones = jnp.ones((16, tile), bf16)
    down_bias = row_of(down_bias_ref, out_count)
    down_bias = jnp.concatenate([down_bias] * (tile // lanes), axis=1)
    wanted = jnp.swapaxes(target_ref[:, 0].astype(f32), 0, 1)
    parts = cells // tile
    count = tile // lanes

    def window_of(part):
        start, stop = part * tile, (part + 1) * tile
        return jnp.concatenate(
            [
                split_ref[step + dz, :, start + dy * lanes : stop + dy * lanes]
                for dz in range(2)
                for dy in range(2)
            ]
            + [ones],
            axis=0,
        )

    outputs, diffs = {}, {}

    def activate(part, rows):
        pre = dot(conv_ref[rows], window_of(part))
        square = pre * pre
        tangent = jnp.tanh(pre * (square * (8.0 * gelu_scale * gelu_cubic) + 2.0 * gelu_scale))
        above = 1.0 + tangent
        bend = pre * (square * (12.0 * gelu_scale * gelu_cubic) + gelu_scale)
        hid_ref[part % 2, rows] = (pre * above).astype(bf16)
        slope_ref[part % 2, rows] = above * ((1.0 - tangent) * bend + 0.5)

    def compare(part):
        output = dot(down_ref[...], hid_ref[part % 2]) + down_bias
        first = part * count
        diff = output - jnp.concatenate([wanted[first + k] for k in range(count)], axis=1)
        outputs[part] = [output[:, k * lanes : (k + 1) * lanes] for k in range(count)]
        for k in range(count):
            piece = diff[:, k * lanes : (k + 1) * lanes]
            gdb_ref[...] += piece
            sq_ref[...] += piece * piece
        diffs[part] = diff.astype(bf16)

    def weigh_down(part):
        gdown_t_ref[...] += dot_rows(hid_ref[part % 2], diffs[part])

    def back(part, rows):
        value = dot(down_t_ref[rows], diffs[part]) * slope_ref[part % 2, rows]
        gpre_ref[0, rows, part * tile : (part + 1) * tile] = value.astype(bf16)

    def weigh_conv(part):
        gconv_t_ref[...] += dot_rows(window_of(part), gpre_ref[0, :, part * tile : (part + 1) * tile])

    big = 8 * hidden
    blocks = [slice(0, big)]
    for part in range(parts + 1):
        first = [functools.partial(activate, part, rows) for rows in blocks] if part < parts else []
        second = []
        if part > 0:
            done = part - 1
            second = [functools.partial(compare, done), functools.partial(weigh_down, done)]
            second += [functools.partial(back, done, rows) for rows in blocks]
            second += [functools.partial(weigh_conv, done)]
        for k in range(max(len(first), len(second))):
            if k < len(second):
                second[k]()
            if k < len(first):
                first[k]()
    for side, at in enumerate((0, cells - lanes)):
        outer_ref[side, step] = gpre_ref[0, :, at : at + lanes]
    outputs = [value for part in range(parts) for value in outputs[part]]
    out_ref[:, 0] = jnp.swapaxes(jnp.stack(outputs, axis=0), 0, 1).astype(bf16)

    @pl.when(step == pairs - 1)
    def _():
        taps = channels * 27
        for copy in late:
            copy.wait()
        folded = 0.0
        cb = jnp.zeros((hidden, 1), f32)
        gconv = jnp.transpose(gconv_t_ref[...])
        for cls in range(8):
            rows = gconv[cls * hidden : (cls + 1) * hidden]
            cb = cb + rows[:, 16 * group : 16 * group + 1]
            rows = jnp.concatenate(split_three(rows[:, : 16 * group]), axis=0)
            folded = folded + dot_rows(rows, tap_ref[cls])
        folded = folded[:hidden] + (folded[hidden : 2 * hidden] + folded[2 * hidden :])
        columns = [folded, cb]
        for ref, share in ((gdb_ref, 1.0), (sq_ref, 1.0 / out_count)):
            total = share * jnp.sum(ref[...], axis=1, keepdims=True)
            columns += [total[:hidden], total[hidden:]]
        columns.append(jnp.zeros((hidden, 2 * lanes - taps - 5), f32))
        small = jnp.concatenate(columns, axis=1) / cell_total
        pieces = jnp.concatenate(split_three(jnp.transpose(gdown_t_ref[...])), axis=0)
        pieces = dot_rows(pieces, order_ref[...])
        grad_down = pieces[:out_count] + (pieces[out_count : 2 * out_count] + pieces[2 * out_count :])
        rows = out_count // 2
        upper = lax.axis_index("gz") // (lax.axis_size("gz") // 2)
        whole_ref[...] = grad_down / cell_total
        keep_ref[...] = whole_ref[pl.ds(pl.multiple_of(upper * rows, rows), rows)]
        give_ref[:, : 8 * hidden] = whole_ref[pl.ds(pl.multiple_of((1 - upper) * rows, rows), rows)]
        give_ref[:, 8 * hidden :] = small
        sides_of(channels, pairs, outer_ref, conv_t_ref, merge_ref, edge_t_ref, to_before_ref, to_after_ref)


def merged(piece, group):
    halves = [
        piece[par * group : (par + 1) * group]
        + pltpu.roll(piece[(2 + par) * group : (3 + par) * group], 1, 1)
        for par in range(2)
    ]
    return jnp.concatenate(halves, axis=1)


def sides_of(channels, pairs, outer_ref, conv_t_ref, merge_ref, edge_t_ref, before_ref, after_ref):
    group = 4 * channels
    span = 4 * group
    found = []
    for dy in range(2):
        weights = [conv_t_ref[(2 * dz + dy) * span : (2 * dz + dy + 1) * span] for dz in range(2)]
        values = [outer_ref[dy, pair] for pair in range(pairs)]
        found.append(dot(jnp.concatenate(weights, axis=0), jnp.concatenate(values, axis=1)))
    rows = []
    for slot in range(pairs + 1):
        outer = []
        for value in found:
            total = 0.0
            for dz in range(2):
                pair = slot - dz
                if 0 <= pair < pairs:
                    total = total + value[dz * span : (dz + 1) * span, pair * lanes : (pair + 1) * lanes]
            outer.append(merged(total, group))
        rows.append(jnp.concatenate(outer, axis=0))
    width = 2 * lanes
    sides = 0.0
    for value in split_two(jnp.concatenate(rows, axis=1)):
        value = dot(edge_t_ref[...], value).astype(bf16)
        value = [value[:, slot * width : (slot + 1) * width] for slot in range(pairs + 1)]
        sides = sides + dot(jnp.concatenate(value, axis=0), merge_ref[...])
    for at in range(2 * pairs + 2):
        before_ref[at] = sides[at * 16 : at * 16 + 8].astype(bf16)
        after_ref[at] = sides[at * 16 + 8 : at * 16 + 16].astype(bf16)


def spread_kernel(sizes, *refs):
    channels, depth, half_rows, tile, plan = sizes
    pairs, slots, taken, done, given = plan
    gpre_ref, conv_t_ref, merge_ref, row_t_ref = refs[:4]
    rest = refs[4:-1]
    spread_ref = refs[-1]
    if taken:
        taken_refs = rest[: len(taken)]
        outer_ref, below_ref, above_ref, before_ref, after_ref, out_ref = rest[len(taken) :]
    else:
        core_ref, *given_refs = rest
    group = 4 * channels
    span = 4 * group
    row_count = 2 * half_rows
    cells = half_rows * lanes
    step = pl.program_id(0)

    def spread_out(pair):
        for part in range(cells // tile):
            spread = dot(conv_t_ref[...], gpre_ref[0, :, part * tile : (part + 1) * tile])
            for dz in range(2):
                for dy in range(2):
                    first = (2 * dz + dy) * span
                    here = slice(part * tile + dy * lanes, (part + 1) * tile + dy * lanes)
                    spread_ref[slots.index(pair + dz), :, here] += spread[first : first + span]

    def lay_out(at, ch, value):
        z = at - 1
        out_ref[ch, z] = value
        out_ref[ch, z, 0:1] += after_ref[at, ch : ch + 1].astype(f32)
        out_ref[ch, z, row_count - 1 : row_count] += before_ref[at, ch : ch + 1].astype(f32)

    def finish(slot):
        rows = [
            merged(spread_ref[slots.index(slot), :, row * lanes : (row + 1) * lanes], group)
            for row in range(half_rows + 1)
        ]
        core = 0.0
        for value in split_two(jnp.concatenate(rows, axis=0)):
            core = core + dot(dot(row_t_ref[...], value).astype(bf16), merge_ref[...])
        for par in range(2):
            for ch in range(channels):
                first = (par * channels + ch) * row_count
                value = core[first : first + row_count]
                if taken:
                    lay_out(2 * slot + par, ch, value)
                else:
                    core_ref[2 * done.index(slot) + par, ch] = value

    for k, pair in enumerate(pairs):

        @pl.when(step == k)
        def _():
            if k == 0:
                for slot in slots:
                    if slot in taken:
                        spread_ref[slots.index(slot)] = taken_refs[taken.index(slot)][...]
                    else:
                        spread_ref[slots.index(slot)] = jnp.zeros(spread_ref.shape[1:], f32)
            if k == 0 and taken:
                for ch in range(channels):
                    lay_out(1, ch, outer_ref[1, ch] + above_ref[ch].astype(f32))
                    lay_out(depth, ch, outer_ref[2, ch] + below_ref[ch].astype(f32))
            for slot in done:
                if k > 0 and pairs[k - 1] in (slot - 1, slot) and not set(pairs[k:]) & {slot - 1, slot}:
                    finish(slot)
            spread_out(pair)
            if k == len(pairs) - 1:
                for slot in done:
                    if pair in (slot - 1, slot):
                        finish(slot)
                if not taken:
                    for slot, ref in zip(given, given_refs, strict=True):
                        ref[...] = spread_ref[slots.index(slot)]


def last_kernel(sizes, mine_ref, theirs_ref, conv_out, cbias_out, down_out, dbias_out, loss_out):
    hidden, taps, big = sizes
    total = mine_ref[...] + theirs_ref[...]
    down_out[...] = total[:, :big]
    small = jnp.concatenate(
        [total[:, at : at + 2 * lanes] for at in range(big, total.shape[1], 2 * lanes)], axis=0
    )
    conv_out[...] = small[:, :taps]
    turned = jnp.transpose(small[:, lanes:])
    at = taps - lanes
    cbias_out[...] = turned[at : at + 1]
    dbias_out[...] = jnp.concatenate([turned[at + 1 : at + 2], turned[at + 2 : at + 3]], axis=1)
    loss_out[...] = jnp.sum(turned[at + 3 : at + 4] + turned[at + 4 : at + 5], axis=1, keepdims=True)


def call(kernel, sizes, out_shape, *args, grid=None, in_specs=None, out_specs=None, scratch=(), flops=0, name):
    if grid is None:
        grid = (1,)
        in_specs = [whole(a.shape) for a in args]
        out_specs = [whole(o.shape) for o in out_shape]
    return pl.pallas_call(
        functools.partial(kernel, sizes),
        out_shape=out_shape,
        in_specs=in_specs,
        out_specs=out_specs,
        scratch_shapes=scratch,
        compiler_params=pltpu.CompilerParams(vmem_limit_bytes=56 * 1024 * 1024),
        cost_estimate=pl.CostEstimate(
            flops=flops,
            bytes_accessed=sum(a.size * a.dtype.itemsize for a in (*args, *out_shape)),
            transcendentals=0,
        ),
        name=name,
        grid=grid,
    )(*args)


def whole(shape):
    return pl.BlockSpec(tuple(shape), lambda z: (0,) * len(shape))


def constants(channels, row_count, half_cols, hidden):
    core, edge = row_spread(channels, row_count)
    names = {
        "col": column_merge(half_cols).T,
        "merge": column_merge(half_cols),
        "row": core,
        "row_t": core.T,
        "edge": edge,
        "edge_t": edge.T,
        "tap": tap_spread(channels),
        "order": class_order(hidden),
    }
    return {name: jnp.asarray(value, bf16) for name, value in names.items()}


def weights(conv_weight, conv_bias, down_weight, fixed):
    hidden, out_count = conv_weight.shape[0], down_weight.shape[0]
    big, win = 8 * hidden, fixed["tap"].shape[2]
    return call(
        weights_kernel,
        (hidden, win),
        [
            jax.ShapeDtypeStruct((big, win + 16), bf16),
            jax.ShapeDtypeStruct((win, big), bf16),
            jax.ShapeDtypeStruct((out_count, big), bf16),
            jax.ShapeDtypeStruct((big, out_count), bf16),
        ],
        conv_weight, conv_bias[None], down_weight, fixed["tap"], fixed["order"],
        flops=2 * big * win * conv_weight.shape[1],
        name="weights",
    )


def parity_cells(fields, below, above, fixed):
    channels, depth, row_count, _ = fields.shape
    pairs, half_rows = depth // 2, row_count // 2
    (early,) = call(
        cells_kernel,
        (channels, pairs, half_rows),
        [jax.ShapeDtypeStruct((pairs + 1, 16 * channels, (half_rows + 1) * lanes), bf16)],
        fields, below, above, fixed["col"], fixed["row"],
        flops=2 * fields.size * row_count * channels * 4,
        name="cells",
    )
    return early


def forward(early, before, after, target, conv, conv_t, down, down_t, down_bias, fixed, channels, cell_total):
    out_count, pairs, half_rows, half_cols = target.shape
    win, big = conv_t.shape
    hidden = big // 8
    cells = half_rows * half_cols
    args = (
        early, before, after, target, conv, conv_t, down, down_t, down_bias[None],
        fixed["tap"], fixed["order"], fixed["col"], fixed["edge"], fixed["merge"], fixed["edge_t"],
    )
    slab = pl.BlockSpec((out_count, 1, half_rows, half_cols), lambda z: (0, z, 0, 0))
    in_specs = [whole(a.shape) for a in args]
    for i in (0, 9, 10):
        in_specs[i] = pl.BlockSpec(memory_space=pl.ANY)
    in_specs[3] = slab
    return call(
        forward_kernel,
        (channels, pairs, half_rows, hidden, out_count, forward_tile, cell_total),
        [
            jax.ShapeDtypeStruct(target.shape, bf16),
            jax.ShapeDtypeStruct((pairs, big, cells), bf16),
            jax.ShapeDtypeStruct((out_count // 2, big), f32),
            jax.ShapeDtypeStruct((out_count // 2, big + 2 * lanes), f32),
            jax.ShapeDtypeStruct(before.shape, bf16),
            jax.ShapeDtypeStruct(after.shape, bf16),
        ],
        *args,
        grid=(pairs,),
        in_specs=in_specs,
        out_specs=[
            slab,
            pl.BlockSpec((1, big, cells), lambda z: (z, 0, 0)),
            whole((out_count // 2, big)),
            whole((out_count // 2, big + 2 * lanes)),
            whole(before.shape),
            whole(after.shape),
        ],
        scratch=[
            pltpu.VMEM(early.shape, bf16),
            pltpu.VMEM((big, out_count), f32),
            pltpu.VMEM((win + 16, big), f32),
            pltpu.VMEM((out_count, lanes), f32),
            pltpu.VMEM((out_count, lanes), f32),
            pltpu.VMEM((2, big, forward_tile), bf16),
            pltpu.VMEM((2, big, forward_tile), f32),
            pltpu.VMEM((out_count, big), f32),
            pltpu.VMEM((2, pairs, big, lanes), bf16),
            pltpu.VMEM(fixed["tap"].shape, bf16),
            pltpu.VMEM(fixed["order"].shape, bf16),
            pltpu.VMEM((pairs + 1, 2, 16 * channels, lanes), f32),
            pltpu.SemaphoreType.DMA((pairs + 1,)),
            pltpu.SemaphoreType.DMA((2,)),
        ],
        flops=4 * pairs * cells * big * (win + out_count),
        name="forward",
    )


def spread(grad_pre, conv_t, fixed, shape, plan, taken=(), beside=()):
    channels, depth, row_count, col_count = shape
    _, big, cells = grad_pre.shape
    pairs, slots, _, done, given = plan
    open_shape = (16 * channels, cells + lanes)
    args = (grad_pre, conv_t, fixed["merge"], fixed["row_t"], *taken, *beside)
    if taken:
        outs = [jax.ShapeDtypeStruct(shape, f32)]
    else:
        outs = [jax.ShapeDtypeStruct((2 * len(done), channels, row_count, col_count), f32)]
    outs += [jax.ShapeDtypeStruct(open_shape, f32)] * len(given)
    first = pairs[0]
    stride = pairs[1] - first if len(pairs) > 1 else 1
    return call(
        spread_kernel,
        (channels, depth, row_count // 2, spread_tile, plan),
        outs,
        *args,
        grid=(len(pairs),),
        in_specs=[pl.BlockSpec((1, big, cells), lambda z: (first + stride * z, 0, 0))]
        + [whole(a.shape) for a in args[1:]],
        out_specs=[whole(o.shape) for o in outs],
        scratch=[pltpu.VMEM((len(slots), *open_shape), f32)],
        flops=2 * len(pairs) * cells * big * conv_t.shape[0],
        name="spread",
    )


forward_tile = 1024
spread_tile = 1024


def on_device(fields, target, conv_weight, conv_bias, down_weight, down_bias):
    channels, depth, row_count, col_count = fields.shape
    hidden = conv_weight.shape[0]
    out_count = down_weight.shape[0]
    taps = channels * 27
    big = 8 * hidden
    cell_total = fields.size // channels // 8 * lax.axis_size("gz") * lax.axis_size("gy")
    fixed = constants(channels, row_count, col_count // 2, hidden)

    below = shifted(fields[:, depth - 1], "gz", 1)
    above = shifted(fields[:, 0], "gz", -1)

    def side(row):
        rows = [below[:, row][:, None], fields[:, :, row], above[:, row][:, None]]
        rows = jnp.concatenate(rows, axis=1).transpose(1, 0, 2)
        return jnp.pad(rows, ((0, 0), (0, 8 - channels), (0, 0)))

    before = shifted(side(row_count - 1), "gy", 1)
    after = shifted(side(0), "gy", -1)
    conv_big, conv_t, down_big, down_t = weights(conv_weight, conv_bias, down_weight, fixed)
    early = parity_cells(fields, below, above, fixed)
    out_field, grad_pre, own, packed, to_before, to_after = forward(
        early, before, after, target, conv_big, conv_t, down_big, down_t, down_bias, fixed, channels, cell_total
    )
    pairs = depth // 2
    shape = fields.shape

    def beside(value, count):
        return jnp.concatenate(jnp.split(value, value.shape[0] // count, axis=0), axis=1)

    me = lax.axis_index("gz")
    small = packed[:, big:]

    def added(own, small, got):
        pieces = jnp.split(got[:, big:], hidden // own.shape[0], axis=1)
        return own + got[:, :big], small + jnp.concatenate(pieces, axis=0)

    def halved(own, small, bit):
        count = own.shape[0] // 2
        upper = (me // bit) % 2
        give = lax.dynamic_slice_in_dim(own, (1 - upper) * count, count, 0)
        own = lax.dynamic_slice_in_dim(own, upper * count, count, 0)
        return own, jnp.concatenate([give, beside(small, count)], axis=1)

    bit = lax.axis_size("gz") // 2
    got = exchanged(packed, "gz", bit)
    from_before = shifted(to_after, "gy", 1)
    from_after = shifted(to_before, "gy", -1)
    outer = ((0, pairs - 1), (0, 1, pairs - 1, pairs), (), (0, pairs), (1, pairs - 1))
    outer_core, low_open, high_open = spread(grad_pre, conv_t, fixed, shape, outer)
    own, small = added(own, small, got)
    bit //= 2
    own, packed = halved(own, small, bit)

    def plane(value, at):
        low = from_before[at, :channels, None].astype(f32)
        high = from_after[at, :channels, None].astype(f32)
        gap = jnp.zeros((channels, row_count - 2, col_count), f32)
        return (value + jnp.concatenate([low, gap, high], axis=1)).astype(bf16)

    got = exchanged(packed, "gz", bit)
    from_below = shifted(plane(outer_core[3], depth + 1), "gz", 1)
    from_above = shifted(plane(outer_core[0], 0), "gz", -1)
    own, small = added(own, small, got)
    while bit > 1:
        bit //= 2
        own, packed = halved(own, small, bit)
        own, small = added(own, small, exchanged(packed, "gz", bit))
    packed = jnp.concatenate([own, beside(small, own.shape[0])], axis=1)
    count = own.shape[0]

    bit = 1
    while 2 * bit < lax.axis_size("gy"):
        packed = packed + exchanged(packed, "gy", bit)
        bit *= 2
    packed, low_open = lax.optimization_barrier((packed, low_open))
    got = exchanged(packed, "gy", bit)
    inner = tuple(range(1, pairs - 1)), tuple(range(1, pairs)), (1, pairs - 1), tuple(range(1, pairs)), ()
    (sensitivity,) = spread(
        grad_pre, conv_t, fixed, shape, inner, (low_open, high_open),
        (outer_core, from_above, from_below, from_after, from_before),
    )
    conv, cbias, down, dbias, loss = call(
        last_kernel,
        (hidden, taps, big),
        [
            jax.ShapeDtypeStruct((hidden, taps), f32),
            jax.ShapeDtypeStruct((1, hidden), f32),
            jax.ShapeDtypeStruct((count, big), f32),
            jax.ShapeDtypeStruct((1, out_count), f32),
            jax.ShapeDtypeStruct((1, 1), f32),
        ],
        packed, got,
        name="last",
    )
    return out_field, sensitivity, conv, cbias[0], down, dbias[0], loss[0, 0]


def solution(mesh):
    in_specs = (P(None, "gz", "gy", None), P(None, "gz", "gy", None), P(), P(), P(), P())
    out_specs = (
        P(None, "gz", "gy", None),
        P(None, "gz", "gy", None),
        P(),
        P(),
        P("gz", None),
        P(),
        P(),
    )
    return jax.shard_map(
        on_device, mesh=mesh, in_specs=in_specs, out_specs=out_specs, check_vma=False
    )
```

```python
import functools

import jax
import jax.numpy as jnp
import numpy as np
from jax import lax
from jax.experimental import pallas as pl
from jax.experimental.pallas import tpu as pltpu
from jax.sharding import PartitionSpec as P

gelu_scale = 0.7978845608028654
gelu_cubic = 0.044715
lanes = 128
bf16 = jnp.bfloat16
f32 = jnp.float32


def shifted(value, axis, by):
    count = lax.axis_size(axis)
    return lax.ppermute(value, axis, [(i, (i + by) % count) for i in range(count)])


def exchanged(value, axis, bit):
    count = lax.axis_size(axis)
    return lax.ppermute(value, axis, [(i, i ^ bit) for i in range(count)])


def column_merge(half_cols):
    merge = np.zeros((2 * half_cols, 2 * half_cols), np.float32)
    for par in range(2):
        for col in range(half_cols):
            merge[par * half_cols + col, (2 * col + par - 1) % (2 * half_cols)] = 1
    return merge


def row_spread(channels, row_count):
    pair_rows = row_count // 2 + 1
    core = np.zeros((pair_rows * 4 * channels, 2 * channels * row_count), np.float32)
    edge = np.zeros((8 * channels, 32), np.float32)
    for par_z in range(2):
        for ch in range(channels):
            for at in range(1, row_count + 1):
                target = ((at // 2 * 2 + par_z) * 2 + at % 2) * channels + ch
                core[target, (par_z * channels + ch) * row_count + at - 1] = 1
            edge[(par_z * 2) * channels + ch, par_z * 16 + ch] = 1
            edge[((2 + par_z) * 2 + 1) * channels + ch, par_z * 16 + 8 + ch] = 1
    return core, edge


def tap_spread(channels):
    spread = np.zeros((8, channels * 27, 64 * channels), np.float32)
    for cls in range(8):
        par_z, par_y, par_x = cls // 4, cls // 2 % 2, cls % 2
        for ch in range(channels):
            for off_z in range(3):
                for off_y in range(3):
                    for off_x in range(3):
                        at_z, at_y, at_x = par_z + off_z, par_y + off_y, par_x + off_x
                        place = (at_z // 2 * 2 + at_y // 2) * 2 + at_x // 2
                        place = ((place * 2 + at_x % 2) * 2 + at_z % 2) * 2 + at_y % 2
                        spread[cls, ch * 27 + 9 * off_z + 3 * off_y + off_x, place * channels + ch] = 1
    return spread


def class_order(hidden):
    order = np.zeros((8 * hidden, 8 * hidden), np.float32)
    for ch in range(hidden):
        for cls in range(8):
            order[ch * 8 + cls, cls * hidden + ch] = 1
    return order


def dot(a, b):
    return jnp.dot(a, b, preferred_element_type=f32)


def dot_rows(a, b):
    return lax.dot_general(a, b, (((1,), (1,)), ((), ())), preferred_element_type=f32)


def split_two(value):
    high = value.astype(bf16)
    return high, (value - high.astype(f32)).astype(bf16)


def split_three(value):
    high = value.astype(bf16)
    return (high,) + split_two(value - high.astype(f32))


def beside(value, count):
    while value.shape[0] > count:
        value = jnp.concatenate(jnp.split(value, 2, axis=0), axis=1)
    return value


def conv_rows(conv_ref, tap_ref):
    return jnp.concatenate([dot(conv_ref[...], tap_ref[cls]) for cls in range(8)], axis=0)


def row_of(ref, count):
    return jnp.transpose(jnp.broadcast_to(ref[...], (lanes, count)))


def planes_kernel(sizes, first_ref, last_ref, first_out, last_out):
    first_out[...] = first_ref[:, 0]
    last_out[...] = last_ref[:, 0]


def prepare_kernel(
    sizes,
    field_ref,
    below_ref,
    above_ref,
    conv_weight_ref,
    conv_bias_ref,
    down_weight_ref,
    tap_ref,
    order_ref,
    col_ref,
    row_ref,
    split_ref,
    conv_ref,
    conv_t_ref,
    down_ref,
    down_t_ref,
):
    channels, pairs, half_rows, hidden = sizes
    group = 4 * channels
    conv = conv_rows(conv_weight_ref, tap_ref)
    conv_t_ref[...] = jnp.transpose(conv).astype(bf16)
    conv_ref[:, : 16 * group] = (0.5 * conv).astype(bf16)
    bias = 0.5 * row_of(conv_bias_ref, hidden)
    at = lax.broadcasted_iota(jnp.int32, bias.shape, 1)
    columns = jnp.zeros_like(bias)
    for k, piece in enumerate(split_three(bias)):
        columns = jnp.where(at == k, piece.astype(f32), columns)
    columns = jnp.concatenate([columns[:, :16]] * 8, axis=0)
    conv_ref[:, 16 * group :] = columns.astype(bf16)
    down = dot(down_weight_ref[...], order_ref[...])
    down_ref[...] = down.astype(bf16)
    down_t_ref[...] = jnp.transpose(down).astype(bf16)
    for slot in range(pairs + 1):
        lower = below_ref if slot == 0 else field_ref.at[:, 2 * slot - 1]
        upper = above_ref if slot == pairs else field_ref.at[:, 2 * slot]
        rows = [ref[ch] for ref in (lower, upper) for ch in range(channels)]
        rows = dot(row_ref[...], jnp.concatenate(rows, axis=0)).astype(bf16)
        rows = dot(rows, col_ref[...])
        for row in range(half_rows + 1):
            piece = rows[row * group : (row + 1) * group]
            split_ref[slot, :, row * lanes : (row + 1) * lanes] = shifts_of(piece).astype(bf16)


def shifts_of(piece):
    piece = jnp.concatenate([piece[:, :lanes], piece[:, lanes:]], axis=0)
    return jnp.concatenate([piece, pltpu.roll(piece, lanes - 1, 1)], axis=0)


def forward_kernel(
    sizes,
    early_ref,
    before_ref,
    after_ref,
    target_ref,
    conv_ref,
    conv_t_ref,
    down_ref,
    down_t_ref,
    down_bias_ref,
    far_tap_ref,
    far_order_ref,
    col_ref,
    edge_ref,
    merge_ref,
    edge_t_ref,
    out_ref,
    gpre_ref,
    to_before_ref,
    to_after_ref,
    *rest,
):
    channels, pairs, half_rows, hidden, out_count, tile, cell_total, groups = sizes
    message_refs = rest[:groups]
    (
    split_ref,
    gdown_t_ref,
    gconv_t_ref,
    gdb_ref,
    sq_ref,
    hid_ref,
    slope_ref,
    whole_ref,
    outer_ref,
    tap_ref,
    order_ref,
    sides_ref,
    split_sem,
    late_sem,
    ) = rest[groups:]
    group = 4 * channels
    cells = half_rows * lanes
    step = pl.program_id(0)

    def arrival(slot):
        return pltpu.make_async_copy(early_ref.at[slot], split_ref.at[slot], split_sem.at[slot])

    late = [
        pltpu.make_async_copy(far_tap_ref, tap_ref, late_sem.at[0]),
        pltpu.make_async_copy(far_order_ref, order_ref, late_sem.at[1]),
    ]

    def complete(slot):
        arrival(slot).wait()
        for side, row in enumerate((0, half_rows)):
            here = slice(row * lanes, (row + 1) * lanes)
            value = split_ref[slot, :, here].astype(f32) + sides_ref[slot, side]
            split_ref[slot, :, here] = value.astype(bf16)

    @pl.when(step == 0)
    def _():
        for slot in range(pairs + 1):
            arrival(slot).start()
        for copy in late:
            copy.start()
        gdown_t_ref[...] = jnp.zeros_like(gdown_t_ref)
        gconv_t_ref[...] = jnp.zeros_like(gconv_t_ref)
        gdb_ref[...] = jnp.zeros_like(gdb_ref)
        sq_ref[...] = jnp.zeros_like(sq_ref)
        width = 2 * lanes
        rows = []
        for slot in range(pairs + 1):
            sides = [ref[2 * slot + par].astype(f32) for par in range(2) for ref in (before_ref, after_ref)]
            rows.append(jnp.concatenate(sides, axis=0).astype(bf16))
        rows = dot(edge_ref[...], jnp.concatenate(rows, axis=1)).astype(bf16)
        rows = [rows[:, slot * width : (slot + 1) * width] for slot in range(pairs + 1)]
        rows = dot(jnp.concatenate(rows, axis=0), col_ref[...])
        for slot in range(pairs + 1):
            for side in range(2):
                first = (2 * slot + side) * group
                sides_ref[slot, side] = shifts_of(rows[first : first + group])
        complete(0)

    complete(step + 1)

    ones = jnp.ones((16, tile), bf16)
    down_bias = row_of(down_bias_ref, out_count)
    down_bias = jnp.concatenate([down_bias] * (tile // lanes), axis=1)
    wanted = jnp.swapaxes(target_ref[:, 0].astype(f32), 0, 1)
    parts = cells // tile
    count = tile // lanes

    def window_of(part):
        start, stop = part * tile, (part + 1) * tile
        return jnp.concatenate(
            [
                split_ref[step + dz, :, start + dy * lanes : stop + dy * lanes]
                for dz in range(2)
                for dy in range(2)
            ]
            + [ones],
            axis=0,
        )

    outputs, diffs = {}, {}

    def activate(part, rows):
        pre = dot(conv_ref[rows], window_of(part))
        square = pre * pre
        tangent = jnp.tanh(pre * (square * (8.0 * gelu_scale * gelu_cubic) + 2.0 * gelu_scale))
        above = 1.0 + tangent
        bend = pre * (square * (12.0 * gelu_scale * gelu_cubic) + gelu_scale)
        hid_ref[part % 2, rows] = (pre * above).astype(bf16)
        slope_ref[part % 2, rows] = above * ((1.0 - tangent) * bend + 0.5)

    def compare(part):
        output = dot(down_ref[...], hid_ref[part % 2]) + down_bias
        first = part * count
        diff = output - jnp.concatenate([wanted[first + k] for k in range(count)], axis=1)
        outputs[part] = [output[:, k * lanes : (k + 1) * lanes] for k in range(count)]
        for k in range(count):
            piece = diff[:, k * lanes : (k + 1) * lanes]
            gdb_ref[...] += piece
            sq_ref[...] += piece * piece
        diffs[part] = diff.astype(bf16)

    def weigh_down(part):
        gdown_t_ref[...] += dot_rows(hid_ref[part % 2], diffs[part])

    def back(part, rows):
        value = dot(down_t_ref[rows], diffs[part]) * slope_ref[part % 2, rows]
        gpre_ref[0, rows, part * tile : (part + 1) * tile] = value.astype(bf16)

    def weigh_conv(part):
        gconv_t_ref[...] += dot_rows(window_of(part), gpre_ref[0, :, part * tile : (part + 1) * tile])

    big = 8 * hidden
    blocks = [slice(0, big)]
    for part in range(parts + 1):
        first = [functools.partial(activate, part, rows) for rows in blocks] if part < parts else []
        second = []
        if part > 0:
            done = part - 1
            second = [functools.partial(compare, done), functools.partial(weigh_down, done)]
            second += [functools.partial(back, done, rows) for rows in blocks]
            second += [functools.partial(weigh_conv, done)]
        for k in range(max(len(first), len(second))):
            if k < len(second):
                second[k]()
            if k < len(first):
                first[k]()
    for side, at in enumerate((0, cells - lanes)):
        outer_ref[side, step] = gpre_ref[0, :, at : at + lanes]
    outputs = [value for part in range(parts) for value in outputs[part]]
    out_ref[:, 0] = jnp.swapaxes(jnp.stack(outputs, axis=0), 0, 1).astype(bf16)

    @pl.when(step == pairs - 1)
    def _():
        taps = channels * 27
        for copy in late:
            copy.wait()
        folded = 0.0
        cb = jnp.zeros((hidden, 1), f32)
        gconv = jnp.transpose(gconv_t_ref[...])
        for cls in range(8):
            rows = gconv[cls * hidden : (cls + 1) * hidden]
            cb = cb + rows[:, 16 * group : 16 * group + 1]
            rows = jnp.concatenate(split_three(rows[:, : 16 * group]), axis=0)
            folded = folded + dot_rows(rows, tap_ref[cls])
        folded = folded[:hidden] + (folded[hidden : 2 * hidden] + folded[2 * hidden :])
        columns = [folded, cb]
        for ref, share in ((gdb_ref, 1.0), (sq_ref, 1.0 / out_count)):
            total = share * jnp.sum(ref[...], axis=1, keepdims=True)
            columns += [total[:hidden], total[hidden:]]
        columns.append(jnp.zeros((hidden, 2 * lanes - taps - 5), f32))
        small = jnp.concatenate(columns, axis=1) / cell_total
        pieces = jnp.concatenate(split_three(jnp.transpose(gdown_t_ref[...])), axis=0)
        pieces = dot_rows(pieces, order_ref[...])
        grad_down = pieces[:out_count] + (pieces[out_count : 2 * out_count] + pieces[2 * out_count :])
        rows = out_count // len(message_refs)
        small = beside(small, rows)
        here = lax.axis_index("gz") // 2
        whole_ref[...] = grad_down / cell_total
        for far, ref in enumerate(message_refs):
            first = pl.multiple_of((here ^ far) * rows, rows)
            ref[:, : 8 * hidden] = whole_ref[pl.ds(first, rows)]
            ref[:, 8 * hidden :] = small
        sides_of(channels, pairs, outer_ref, conv_t_ref, merge_ref, edge_t_ref, to_before_ref, to_after_ref)


def merged(piece, group):
    halves = [
        piece[par * group : (par + 1) * group]
        + pltpu.roll(piece[(2 + par) * group : (3 + par) * group], 1, 1)
        for par in range(2)
    ]
    return jnp.concatenate(halves, axis=1)


def sides_of(channels, pairs, outer_ref, conv_t_ref, merge_ref, edge_t_ref, before_ref, after_ref):
    group = 4 * channels
    span = 4 * group
    found = []
    for dy in range(2):
        weights = [conv_t_ref[(2 * dz + dy) * span : (2 * dz + dy + 1) * span] for dz in range(2)]
        values = [outer_ref[dy, pair] for pair in range(pairs)]
        found.append(dot(jnp.concatenate(weights, axis=0), jnp.concatenate(values, axis=1)))
    rows = []
    for slot in range(pairs + 1):
        outer = []
        for value in found:
            total = 0.0
            for dz in range(2):
                pair = slot - dz
                if 0 <= pair < pairs:
                    total = total + value[dz * span : (dz + 1) * span, pair * lanes : (pair + 1) * lanes]
            outer.append(merged(total, group))
        rows.append(jnp.concatenate(outer, axis=0))
    width = 2 * lanes
    sides = 0.0
    for value in split_two(jnp.concatenate(rows, axis=1)):
        value = dot(edge_t_ref[...], value).astype(bf16)
        value = [value[:, slot * width : (slot + 1) * width] for slot in range(pairs + 1)]
        sides = sides + dot(jnp.concatenate(value, axis=0), merge_ref[...])
    for at in range(2 * pairs + 2):
        before_ref[at] = sides[at * 16 : at * 16 + 8].astype(bf16)
        after_ref[at] = sides[at * 16 + 8 : at * 16 + 16].astype(bf16)


def spread_kernel(sizes, *refs):
    channels, depth, half_rows, tile, plan = sizes
    pairs, slots, taken, done, given = plan
    gpre_ref, conv_t_ref, merge_ref, row_t_ref = refs[:4]
    rest = refs[4:-1]
    spread_ref = refs[-1]
    if taken:
        taken_refs = rest[: len(taken)]
        outer_ref, below_ref, above_ref, before_ref, after_ref, out_ref = rest[len(taken) :]
    else:
        core_ref, *given_refs = rest
    group = 4 * channels
    span = 4 * group
    row_count = 2 * half_rows
    cells = half_rows * lanes
    step = pl.program_id(0)

    def spread_out(pair):
        for part in range(cells // tile):
            spread = dot(conv_t_ref[...], gpre_ref[0, :, part * tile : (part + 1) * tile])
            for dz in range(2):
                for dy in range(2):
                    first = (2 * dz + dy) * span
                    here = slice(part * tile + dy * lanes, (part + 1) * tile + dy * lanes)
                    spread_ref[slots.index(pair + dz), :, here] += spread[first : first + span]

    def lay_out(at, ch, value):
        z = at - 1
        out_ref[ch, z] = value
        out_ref[ch, z, 0:1] += after_ref[at, ch : ch + 1].astype(f32)
        out_ref[ch, z, row_count - 1 : row_count] += before_ref[at, ch : ch + 1].astype(f32)

    def finish(slot):
        rows = [
            merged(spread_ref[slots.index(slot), :, row * lanes : (row + 1) * lanes], group)
            for row in range(half_rows + 1)
        ]
        core = 0.0
        for value in split_two(jnp.concatenate(rows, axis=0)):
            core = core + dot(dot(row_t_ref[...], value).astype(bf16), merge_ref[...])
        for par in range(2):
            for ch in range(channels):
                first = (par * channels + ch) * row_count
                value = core[first : first + row_count]
                if taken:
                    lay_out(2 * slot + par, ch, value)
                else:
                    core_ref[2 * done.index(slot) + par, ch] = value

    for k, pair in enumerate(pairs):

        @pl.when(step == k)
        def _():
            if k == 0:
                for slot in slots:
                    if slot in taken:
                        spread_ref[slots.index(slot)] = taken_refs[taken.index(slot)][...]
                    else:
                        spread_ref[slots.index(slot)] = jnp.zeros(spread_ref.shape[1:], f32)
            if k == 0 and taken:
                for ch in range(channels):
                    lay_out(1, ch, outer_ref[1, ch] + above_ref[ch].astype(f32))
                    lay_out(depth, ch, outer_ref[2, ch] + below_ref[ch].astype(f32))
            for slot in done:
                if k > 0 and pairs[k - 1] in (slot - 1, slot) and not set(pairs[k:]) & {slot - 1, slot}:
                    finish(slot)
            spread_out(pair)
            if k == len(pairs) - 1:
                for slot in done:
                    if pair in (slot - 1, slot):
                        finish(slot)
                if not taken:
                    for slot, ref in zip(given, given_refs, strict=True):
                        ref[...] = spread_ref[slots.index(slot)]


def last_kernel(sizes, *refs):
    hidden, taps, big = sizes
    conv_out, cbias_out, down_out, dbias_out, loss_out = refs[-5:]
    total = refs[0][...]
    for ref in refs[1:-5]:
        total = total + ref[...]
    down_out[...] = total[:, :big]
    small = total[:, big:]
    while small.shape[0] < hidden:
        small = jnp.concatenate(jnp.split(small, 2, axis=1), axis=0)
    conv_out[...] = small[:, :taps]
    turned = jnp.transpose(small[:, lanes:])
    at = taps - lanes
    cbias_out[...] = turned[at : at + 1]
    dbias_out[...] = jnp.concatenate([turned[at + 1 : at + 2], turned[at + 2 : at + 3]], axis=1)
    loss_out[...] = jnp.sum(turned[at + 3 : at + 4] + turned[at + 4 : at + 5], axis=1, keepdims=True)


def call(kernel, sizes, out_shape, *args, grid=None, in_specs=None, out_specs=None, scratch=(), flops=0, name):
    if grid is None:
        grid = (1,)
        in_specs = [whole(a.shape) for a in args]
        out_specs = [whole(o.shape) for o in out_shape]
    return pl.pallas_call(
        functools.partial(kernel, sizes),
        out_shape=out_shape,
        in_specs=in_specs,
        out_specs=out_specs,
        scratch_shapes=scratch,
        compiler_params=pltpu.CompilerParams(vmem_limit_bytes=56 * 1024 * 1024),
        cost_estimate=pl.CostEstimate(
            flops=flops,
            bytes_accessed=sum(a.size * a.dtype.itemsize for a in (*args, *out_shape)),
            transcendentals=0,
        ),
        name=name,
        grid=grid,
    )(*args)


def whole(shape):
    return pl.BlockSpec(tuple(shape), lambda z: (0,) * len(shape))


def constants(channels, row_count, half_cols, hidden):
    core, edge = row_spread(channels, row_count)
    names = {
        "col": column_merge(half_cols).T,
        "merge": column_merge(half_cols),
        "row": core,
        "row_t": core.T,
        "edge": edge,
        "edge_t": edge.T,
        "tap": tap_spread(channels),
        "order": class_order(hidden),
    }
    return {name: jnp.asarray(value, bf16) for name, value in names.items()}


def outer_planes(fields):
    channels, depth, row_count, col_count = fields.shape
    out = jax.ShapeDtypeStruct((channels, row_count, col_count), fields.dtype)
    block = (channels, 1, row_count, col_count)
    return call(
        planes_kernel,
        (),
        [out, out],
        fields, fields,
        grid=(1,),
        in_specs=[pl.BlockSpec(block, lambda z: (0, 0, 0, 0)), pl.BlockSpec(block, lambda z: (0, depth - 1, 0, 0))],
        out_specs=[whole(out.shape)] * 2,
        name="planes",
    )


def prepare(fields, below, above, conv_weight, conv_bias, down_weight, fixed):
    channels, depth, row_count, _ = fields.shape
    hidden, out_count = conv_weight.shape[0], down_weight.shape[0]
    pairs, half_rows = depth // 2, row_count // 2
    big, win = 8 * hidden, 64 * channels
    return call(
        prepare_kernel,
        (channels, pairs, half_rows, hidden),
        [
            jax.ShapeDtypeStruct((pairs + 1, 16 * channels, (half_rows + 1) * lanes), bf16),
            jax.ShapeDtypeStruct((big, win + 16), bf16),
            jax.ShapeDtypeStruct((win, big), bf16),
            jax.ShapeDtypeStruct((out_count, big), bf16),
            jax.ShapeDtypeStruct((big, out_count), bf16),
        ],
        fields, below, above, conv_weight, conv_bias[None], down_weight,
        fixed["tap"], fixed["order"], fixed["col"], fixed["row"],
        flops=2 * fields.size * row_count * channels * 4,
        name="prepare",
    )


def forward(early, before, after, target, conv, conv_t, down, down_t, down_bias, fixed, channels, cell_total, groups):
    out_count, pairs, half_rows, half_cols = target.shape
    win, big = conv_t.shape
    hidden = big // 8
    cells = half_rows * half_cols
    args = (
        early, before, after, target, conv, conv_t, down, down_t, down_bias[None],
        fixed["tap"], fixed["order"], fixed["col"], fixed["edge"], fixed["merge"], fixed["edge_t"],
    )
    slab = pl.BlockSpec((out_count, 1, half_rows, half_cols), lambda z: (0, z, 0, 0))
    rows = out_count // groups
    message = jax.ShapeDtypeStruct((rows, big + 2 * lanes * hidden // rows), f32)
    in_specs = [whole(a.shape) for a in args]
    for i in (0, 9, 10):
        in_specs[i] = pl.BlockSpec(memory_space=pl.ANY)
    in_specs[3] = slab
    return call(
        forward_kernel,
        (channels, pairs, half_rows, hidden, out_count, forward_tile, cell_total, groups),
        [
            jax.ShapeDtypeStruct(target.shape, bf16),
            jax.ShapeDtypeStruct((pairs, big, cells), bf16),
            jax.ShapeDtypeStruct(before.shape, bf16),
            jax.ShapeDtypeStruct(after.shape, bf16),
        ]
        + [message] * groups,
        *args,
        grid=(pairs,),
        in_specs=in_specs,
        out_specs=[
            slab,
            pl.BlockSpec((1, big, cells), lambda z: (z, 0, 0)),
            whole(before.shape),
            whole(after.shape),
        ]
        + [whole(message.shape)] * groups,
        scratch=[
            pltpu.VMEM(early.shape, bf16),
            pltpu.VMEM((big, out_count), f32),
            pltpu.VMEM((win + 16, big), f32),
            pltpu.VMEM((out_count, lanes), f32),
            pltpu.VMEM((out_count, lanes), f32),
            pltpu.VMEM((2, big, forward_tile), bf16),
            pltpu.VMEM((2, big, forward_tile), f32),
            pltpu.VMEM((out_count, big), f32),
            pltpu.VMEM((2, pairs, big, lanes), bf16),
            pltpu.VMEM(fixed["tap"].shape, bf16),
            pltpu.VMEM(fixed["order"].shape, bf16),
            pltpu.VMEM((pairs + 1, 2, 16 * channels, lanes), f32),
            pltpu.SemaphoreType.DMA((pairs + 1,)),
            pltpu.SemaphoreType.DMA((2,)),
        ],
        flops=4 * pairs * cells * big * (win + out_count),
        name="forward",
    )


def spread(grad_pre, conv_t, fixed, shape, plan, taken=(), beside=()):
    channels, depth, row_count, col_count = shape
    _, big, cells = grad_pre.shape
    pairs, slots, _, done, given = plan
    open_shape = (16 * channels, cells + lanes)
    args = (grad_pre, conv_t, fixed["merge"], fixed["row_t"], *taken, *beside)
    if taken:
        outs = [jax.ShapeDtypeStruct(shape, f32)]
    else:
        outs = [jax.ShapeDtypeStruct((2 * len(done), channels, row_count, col_count), f32)]
    outs += [jax.ShapeDtypeStruct(open_shape, f32)] * len(given)
    first = pairs[0]
    stride = pairs[1] - first if len(pairs) > 1 else 1
    return call(
        spread_kernel,
        (channels, depth, row_count // 2, spread_tile, plan),
        outs,
        *args,
        grid=(len(pairs),),
        in_specs=[pl.BlockSpec((1, big, cells), lambda z: (first + stride * z, 0, 0))]
        + [whole(a.shape) for a in args[1:]],
        out_specs=[whole(o.shape) for o in outs],
        scratch=[pltpu.VMEM((len(slots), *open_shape), f32)],
        flops=2 * len(pairs) * cells * big * conv_t.shape[0],
        name="spread",
    )


forward_tile = 1024
spread_tile = 1024


def on_device(fields, target, conv_weight, conv_bias, down_weight, down_bias):
    channels, depth, row_count, col_count = fields.shape
    hidden = conv_weight.shape[0]
    out_count = down_weight.shape[0]
    taps = channels * 27
    big = 8 * hidden
    cell_total = fields.size // channels // 8 * lax.axis_size("gz") * lax.axis_size("gy")
    fixed = constants(channels, row_count, col_count // 2, hidden)

    first_plane, last_plane = outer_planes(fields)
    below = shifted(last_plane, "gz", 1)
    above = shifted(first_plane, "gz", -1)

    def side(row):
        rows = [below[:, row][:, None], fields[:, :, row], above[:, row][:, None]]
        rows = jnp.concatenate(rows, axis=1).transpose(1, 0, 2)
        return jnp.pad(rows, ((0, 0), (0, 8 - channels), (0, 0)))

    before = shifted(side(row_count - 1), "gy", 1)
    after = shifted(side(0), "gy", -1)
    early, conv_big, conv_t, down_big, down_t = prepare(
        fields, below, above, conv_weight, conv_bias, down_weight, fixed
    )
    groups = lax.axis_size("gz") // 2
    out_field, grad_pre, to_before, to_after, *messages = forward(
        early, before, after, target, conv_big, conv_t, down_big, down_t, down_bias, fixed, channels, cell_total, groups
    )
    pairs = depth // 2
    shape = fields.shape

    got = [exchanged(message, "gz", 2 * far) for far, message in enumerate(messages) if far > 0]
    from_before = shifted(to_after, "gy", 1)
    from_after = shifted(to_before, "gy", -1)
    outer = ((0, pairs - 1), (0, 1, pairs - 1, pairs), (), (0, pairs), (1, pairs - 1))
    outer_core, low_open, high_open = spread(grad_pre, conv_t, fixed, shape, outer)
    packed = sum(got, messages[0])

    def plane(value, at):
        low = from_before[at, :channels, None].astype(f32)
        high = from_after[at, :channels, None].astype(f32)
        gap = jnp.zeros((channels, row_count - 2, col_count), f32)
        return (value + jnp.concatenate([low, gap, high], axis=1)).astype(bf16)

    from_below = shifted(plane(outer_core[3], depth + 1), "gz", 1)
    from_above = shifted(plane(outer_core[0], 0), "gz", -1)
    count = packed.shape[0] // 2
    core = lax.axis_index("gz") % 2
    own, small = packed[:, :big], beside(packed[:, big:], count)
    give = lax.dynamic_slice_in_dim(own, (1 - core) * count, count, 0)
    own = lax.dynamic_slice_in_dim(own, core * count, count, 0)
    packed = jnp.concatenate([own, small], axis=1) + exchanged(jnp.concatenate([give, small], axis=1), "gz", 1)

    packed, low_open = lax.optimization_barrier((packed, low_open))
    got = [exchanged(packed, "gy", far) for far in range(1, lax.axis_size("gy"))]
    inner = tuple(range(1, pairs - 1)), tuple(range(1, pairs)), (1, pairs - 1), tuple(range(1, pairs)), ()
    (sensitivity,) = spread(
        grad_pre, conv_t, fixed, shape, inner, (low_open, high_open),
        (outer_core, from_above, from_below, from_after, from_before),
    )
    conv, cbias, down, dbias, loss = call(
        last_kernel,
        (hidden, taps, big),
        [
            jax.ShapeDtypeStruct((hidden, taps), f32),
            jax.ShapeDtypeStruct((1, hidden), f32),
            jax.ShapeDtypeStruct((count, big), f32),
            jax.ShapeDtypeStruct((1, out_count), f32),
            jax.ShapeDtypeStruct((1, 1), f32),
        ],
        packed, *got,
        name="last",
    )
    return out_field, sensitivity, conv, cbias[0], down, dbias[0], loss[0, 0]


def solution(mesh):
    in_specs = (P(None, "gz", "gy", None), P(None, "gz", "gy", None), P(), P(), P(), P())
    out_specs = (
        P(None, "gz", "gy", None),
        P(None, "gz", "gy", None),
        P(),
        P(),
        P("gz", None),
        P(),
        P(),
    )
    return jax.shard_map(
        on_device, mesh=mesh, in_specs=in_specs, out_specs=out_specs, check_vma=False
    )
```

```python
import functools

import jax
import jax.numpy as jnp
import numpy as np
from jax import lax
from jax.experimental import pallas as pl
from jax.experimental.pallas import tpu as pltpu
from jax.sharding import PartitionSpec as P

gelu_scale = 0.7978845608028654
gelu_cubic = 0.044715
lanes = 128
bf16 = jnp.bfloat16
f32 = jnp.float32


def shifted(value, axis, by):
    count = lax.axis_size(axis)
    return lax.ppermute(value, axis, [(i, (i + by) % count) for i in range(count)])


def exchanged(value, axis, bit):
    count = lax.axis_size(axis)
    return lax.ppermute(value, axis, [(i, i ^ bit) for i in range(count)])


def column_merge(half_cols):
    merge = np.zeros((2 * half_cols, 2 * half_cols), np.float32)
    for par in range(2):
        for col in range(half_cols):
            merge[par * half_cols + col, (2 * col + par - 1) % (2 * half_cols)] = 1
    return merge


def row_spread(channels, row_count):
    pair_rows = row_count // 2 + 1
    core = np.zeros((pair_rows * 4 * channels, 2 * channels * row_count), np.float32)
    edge = np.zeros((8 * channels, 32), np.float32)
    for par_z in range(2):
        for ch in range(channels):
            for at in range(1, row_count + 1):
                target = ((at // 2 * 2 + par_z) * 2 + at % 2) * channels + ch
                core[target, (par_z * channels + ch) * row_count + at - 1] = 1
            edge[(par_z * 2) * channels + ch, par_z * 16 + ch] = 1
            edge[((2 + par_z) * 2 + 1) * channels + ch, par_z * 16 + 8 + ch] = 1
    return core, edge


def tap_spread(channels):
    spread = np.zeros((8, channels * 27, 64 * channels), np.float32)
    for cls in range(8):
        par_z, par_y, par_x = cls // 4, cls // 2 % 2, cls % 2
        for ch in range(channels):
            for off_z in range(3):
                for off_y in range(3):
                    for off_x in range(3):
                        at_z, at_y, at_x = par_z + off_z, par_y + off_y, par_x + off_x
                        place = (at_z // 2 * 2 + at_y // 2) * 2 + at_x // 2
                        place = ((place * 2 + at_x % 2) * 2 + at_z % 2) * 2 + at_y % 2
                        spread[cls, ch * 27 + 9 * off_z + 3 * off_y + off_x, place * channels + ch] = 1
    return spread


def class_order(hidden):
    order = np.zeros((8 * hidden, 8 * hidden), np.float32)
    for ch in range(hidden):
        for cls in range(8):
            order[ch * 8 + cls, cls * hidden + ch] = 1
    return order


def dot(a, b):
    return jnp.dot(a, b, preferred_element_type=f32)


def dot_rows(a, b):
    return lax.dot_general(a, b, (((1,), (1,)), ((), ())), preferred_element_type=f32)


def split_two(value):
    high = value.astype(bf16)
    return high, (value - high.astype(f32)).astype(bf16)


def split_three(value):
    high = value.astype(bf16)
    return (high,) + split_two(value - high.astype(f32))


def beside(value, count):
    while value.shape[0] > count:
        value = jnp.concatenate(jnp.split(value, 2, axis=0), axis=1)
    return value


def conv_rows(conv_ref, tap_ref):
    return jnp.concatenate([dot(conv_ref[...], tap_ref[cls]) for cls in range(8)], axis=0)


def row_of(ref, count):
    return jnp.transpose(jnp.broadcast_to(ref[...], (lanes, count)))


def fetched(pairs_of_refs, sems):
    copies = [pltpu.make_async_copy(*refs, sems.at[i]) for i, refs in enumerate(pairs_of_refs)]
    for copy in copies:
        copy.start()
    for copy in copies:
        copy.wait()


def rows_kernel(
    sizes, low_ref, high_ref, far_below_ref, far_above_ref, first_out, last_out, below_ref, above_ref, sems
):
    channels, depth = sizes
    fetched([(far_below_ref, below_ref), (far_above_ref, above_ref)], sems)
    for ref, at, out in ((low_ref, 0, first_out), (high_ref, -1, last_out)):
        for z in range(depth + 2):
            rows = []
            for ch in range(channels):
                if z == 0:
                    value = below_ref[ch]
                elif z == depth + 1:
                    value = above_ref[ch]
                else:
                    value = ref[ch, z - 1]
                value = value.astype(f32)
                rows.append(value[:1] if at == 0 else value[value.shape[0] - 1 :])
            rows.append(jnp.zeros((8 - channels, rows[0].shape[1]), f32))
            out[z] = jnp.concatenate(rows, axis=0).astype(bf16)


def prepare_kernel(
    sizes,
    field_ref,
    below_ref,
    above_ref,
    conv_weight_ref,
    conv_bias_ref,
    down_weight_ref,
    tap_ref,
    order_ref,
    col_ref,
    row_ref,
    split_ref,
    conv_ref,
    conv_t_ref,
    down_ref,
    down_t_ref,
):
    channels, pairs, half_rows, hidden = sizes
    group = 4 * channels
    conv = conv_rows(conv_weight_ref, tap_ref)
    conv_t_ref[...] = jnp.transpose(conv).astype(bf16)
    conv_ref[:, : 16 * group] = (0.5 * conv).astype(bf16)
    bias = 0.5 * row_of(conv_bias_ref, hidden)
    at = lax.broadcasted_iota(jnp.int32, bias.shape, 1)
    columns = jnp.zeros_like(bias)
    for k, piece in enumerate(split_three(bias)):
        columns = jnp.where(at == k, piece.astype(f32), columns)
    columns = jnp.concatenate([columns[:, :16]] * 8, axis=0)
    conv_ref[:, 16 * group :] = columns.astype(bf16)
    down = dot(down_weight_ref[...], order_ref[...])
    down_ref[...] = down.astype(bf16)
    down_t_ref[...] = jnp.transpose(down).astype(bf16)
    for slot in range(pairs + 1):
        lower = below_ref if slot == 0 else field_ref.at[:, 2 * slot - 1]
        upper = above_ref if slot == pairs else field_ref.at[:, 2 * slot]
        rows = [ref[ch] for ref in (lower, upper) for ch in range(channels)]
        rows = dot(row_ref[...], jnp.concatenate(rows, axis=0)).astype(bf16)
        rows = dot(rows, col_ref[...])
        for row in range(half_rows + 1):
            piece = rows[row * group : (row + 1) * group]
            split_ref[slot, :, row * lanes : (row + 1) * lanes] = shifts_of(piece).astype(bf16)


def shifts_of(piece):
    piece = jnp.concatenate([piece[:, :lanes], piece[:, lanes:]], axis=0)
    return jnp.concatenate([piece, pltpu.roll(piece, lanes - 1, 1)], axis=0)


def forward_kernel(
    sizes,
    early_ref,
    far_before_ref,
    far_after_ref,
    target_ref,
    conv_ref,
    conv_t_ref,
    down_ref,
    down_t_ref,
    down_bias_ref,
    far_tap_ref,
    far_order_ref,
    col_ref,
    edge_ref,
    merge_ref,
    edge_t_ref,
    out_ref,
    gpre_ref,
    to_before_ref,
    to_after_ref,
    *rest,
):
    channels, pairs, half_rows, hidden, out_count, tile, cell_total, groups = sizes
    message_refs = rest[:groups]
    (
    split_ref,
    gdown_t_ref,
    gconv_t_ref,
    gdb_ref,
    sq_ref,
    hid_ref,
    slope_ref,
    whole_ref,
    outer_ref,
    tap_ref,
    order_ref,
    sides_ref,
    before_ref,
    after_ref,
    split_sem,
    late_sem,
    ) = rest[groups:]
    group = 4 * channels
    cells = half_rows * lanes
    step = pl.program_id(0)

    def arrival(slot):
        return pltpu.make_async_copy(early_ref.at[slot], split_ref.at[slot], split_sem.at[slot])

    late = [
        pltpu.make_async_copy(far_tap_ref, tap_ref, late_sem.at[0]),
        pltpu.make_async_copy(far_order_ref, order_ref, late_sem.at[1]),
    ]

    def complete(slot):
        arrival(slot).wait()
        for side, row in enumerate((0, half_rows)):
            here = slice(row * lanes, (row + 1) * lanes)
            value = split_ref[slot, :, here].astype(f32) + sides_ref[slot, side]
            split_ref[slot, :, here] = value.astype(bf16)

    @pl.when(step == 0)
    def _():
        sides = [
            pltpu.make_async_copy(far_before_ref, before_ref, late_sem.at[2]),
            pltpu.make_async_copy(far_after_ref, after_ref, late_sem.at[3]),
        ]
        for copy in sides:
            copy.start()
        for slot in range(pairs + 1):
            arrival(slot).start()
        for copy in late:
            copy.start()
        gdown_t_ref[...] = jnp.zeros_like(gdown_t_ref)
        gconv_t_ref[...] = jnp.zeros_like(gconv_t_ref)
        gdb_ref[...] = jnp.zeros_like(gdb_ref)
        sq_ref[...] = jnp.zeros_like(sq_ref)
        width = 2 * lanes
        rows = []
        for copy in sides:
            copy.wait()
        for slot in range(pairs + 1):
            sides = [ref[2 * slot + par].astype(f32) for par in range(2) for ref in (before_ref, after_ref)]
            rows.append(jnp.concatenate(sides, axis=0).astype(bf16))
        rows = dot(edge_ref[...], jnp.concatenate(rows, axis=1)).astype(bf16)
        rows = [rows[:, slot * width : (slot + 1) * width] for slot in range(pairs + 1)]
        rows = dot(jnp.concatenate(rows, axis=0), col_ref[...])
        for slot in range(pairs + 1):
            for side in range(2):
                first = (2 * slot + side) * group
                sides_ref[slot, side] = shifts_of(rows[first : first + group])
        complete(0)

    complete(step + 1)

    ones = jnp.ones((16, tile), bf16)
    down_bias = row_of(down_bias_ref, out_count)
    down_bias = jnp.concatenate([down_bias] * (tile // lanes), axis=1)
    wanted = jnp.swapaxes(target_ref[:, 0].astype(f32), 0, 1)
    parts = cells // tile
    count = tile // lanes

    def window_of(part):
        start, stop = part * tile, (part + 1) * tile
        return jnp.concatenate(
            [
                split_ref[step + dz, :, start + dy * lanes : stop + dy * lanes]
                for dz in range(2)
                for dy in range(2)
            ]
            + [ones],
            axis=0,
        )

    outputs, diffs = {}, {}

    def activate(part, rows):
        pre = dot(conv_ref[rows], window_of(part))
        square = pre * pre
        tangent = jnp.tanh(pre * (square * (8.0 * gelu_scale * gelu_cubic) + 2.0 * gelu_scale))
        above = 1.0 + tangent
        bend = pre * (square * (12.0 * gelu_scale * gelu_cubic) + gelu_scale)
        hid_ref[part % 2, rows] = (pre * above).astype(bf16)
        slope_ref[part % 2, rows] = above * ((1.0 - tangent) * bend + 0.5)

    def compare(part):
        output = dot(down_ref[...], hid_ref[part % 2]) + down_bias
        first = part * count
        diff = output - jnp.concatenate([wanted[first + k] for k in range(count)], axis=1)
        outputs[part] = [output[:, k * lanes : (k + 1) * lanes] for k in range(count)]
        for k in range(count):
            piece = diff[:, k * lanes : (k + 1) * lanes]
            gdb_ref[...] += piece
            sq_ref[...] += piece * piece
        diffs[part] = diff.astype(bf16)

    def weigh_down(part):
        gdown_t_ref[...] += dot_rows(hid_ref[part % 2], diffs[part])

    def back(part, rows):
        value = dot(down_t_ref[rows], diffs[part]) * slope_ref[part % 2, rows]
        gpre_ref[0, rows, part * tile : (part + 1) * tile] = value.astype(bf16)

    def weigh_conv(part):
        gconv_t_ref[...] += dot_rows(window_of(part), gpre_ref[0, :, part * tile : (part + 1) * tile])

    big = 8 * hidden
    blocks = [slice(0, big)]
    for part in range(parts + 1):
        first = [functools.partial(activate, part, rows) for rows in blocks] if part < parts else []
        second = []
        if part > 0:
            done = part - 1
            second = [functools.partial(compare, done), functools.partial(weigh_down, done)]
            second += [functools.partial(back, done, rows) for rows in blocks]
            second += [functools.partial(weigh_conv, done)]
        for k in range(max(len(first), len(second))):
            if k < len(second):
                second[k]()
            if k < len(first):
                first[k]()
    for side, at in enumerate((0, cells - lanes)):
        outer_ref[side, step] = gpre_ref[0, :, at : at + lanes]
    outputs = [value for part in range(parts) for value in outputs[part]]
    out_ref[:, 0] = jnp.swapaxes(jnp.stack(outputs, axis=0), 0, 1).astype(bf16)

    @pl.when(step == pairs - 1)
    def _():
        taps = channels * 27
        for copy in late:
            copy.wait()
        folded = 0.0
        cb = jnp.zeros((hidden, 1), f32)
        gconv = jnp.transpose(gconv_t_ref[...])
        for cls in range(8):
            rows = gconv[cls * hidden : (cls + 1) * hidden]
            cb = cb + rows[:, 16 * group : 16 * group + 1]
            rows = jnp.concatenate(split_three(rows[:, : 16 * group]), axis=0)
            folded = folded + dot_rows(rows, tap_ref[cls])
        folded = folded[:hidden] + (folded[hidden : 2 * hidden] + folded[2 * hidden :])
        columns = [folded, cb]
        for ref, share in ((gdb_ref, 1.0), (sq_ref, 1.0 / out_count)):
            total = share * jnp.sum(ref[...], axis=1, keepdims=True)
            columns += [total[:hidden], total[hidden:]]
        columns.append(jnp.zeros((hidden, 2 * lanes - taps - 5), f32))
        small = jnp.concatenate(columns, axis=1) / cell_total
        pieces = jnp.concatenate(split_three(jnp.transpose(gdown_t_ref[...])), axis=0)
        pieces = dot_rows(pieces, order_ref[...])
        grad_down = pieces[:out_count] + (pieces[out_count : 2 * out_count] + pieces[2 * out_count :])
        rows = out_count // len(message_refs)
        small = beside(small, rows)
        here = lax.axis_index("gz") // 2
        whole_ref[...] = grad_down / cell_total
        for far, ref in enumerate(message_refs):
            first = pl.multiple_of((here ^ far) * rows, rows)
            ref[:, : 8 * hidden] = whole_ref[pl.ds(first, rows)]
            ref[:, 8 * hidden :] = small
        sides_of(channels, pairs, outer_ref, conv_t_ref, merge_ref, edge_t_ref, to_before_ref, to_after_ref)


def merged(piece, group):
    halves = [
        piece[par * group : (par + 1) * group]
        + pltpu.roll(piece[(2 + par) * group : (3 + par) * group], 1, 1)
        for par in range(2)
    ]
    return jnp.concatenate(halves, axis=1)


def sides_of(channels, pairs, outer_ref, conv_t_ref, merge_ref, edge_t_ref, before_ref, after_ref):
    group = 4 * channels
    span = 4 * group
    found = []
    for dy in range(2):
        weights = [conv_t_ref[(2 * dz + dy) * span : (2 * dz + dy + 1) * span] for dz in range(2)]
        values = [outer_ref[dy, pair] for pair in range(pairs)]
        found.append(dot(jnp.concatenate(weights, axis=0), jnp.concatenate(values, axis=1)))
    rows = []
    for slot in range(pairs + 1):
        outer = []
        for value in found:
            total = 0.0
            for dz in range(2):
                pair = slot - dz
                if 0 <= pair < pairs:
                    total = total + value[dz * span : (dz + 1) * span, pair * lanes : (pair + 1) * lanes]
            outer.append(merged(total, group))
        rows.append(jnp.concatenate(outer, axis=0))
    width = 2 * lanes
    sides = 0.0
    for value in split_two(jnp.concatenate(rows, axis=1)):
        value = dot(edge_t_ref[...], value).astype(bf16)
        value = [value[:, slot * width : (slot + 1) * width] for slot in range(pairs + 1)]
        sides = sides + dot(jnp.concatenate(value, axis=0), merge_ref[...])
    for at in range(2 * pairs + 2):
        before_ref[at] = sides[at * 16 : at * 16 + 8].astype(bf16)
        after_ref[at] = sides[at * 16 + 8 : at * 16 + 16].astype(bf16)


def spread_kernel(sizes, *refs):
    channels, depth, half_rows, tile, plan = sizes
    pairs, slots, taken, done, given = plan
    gpre_ref, conv_t_ref, merge_ref, row_t_ref = refs[:4]
    rest = refs[4:-1]
    spread_ref = refs[-1]
    if taken:
        rest, spread_ref = refs[4:-6], refs[-6]
        taken_refs = rest[: len(taken)]
        outer_ref, *far_refs, out_ref = rest[len(taken) :]
        near_refs, sems = refs[-5:-1], refs[-1]
        below_ref, above_ref, before_ref, after_ref = near_refs
    else:
        core_ref, *given_refs = rest
    group = 4 * channels
    span = 4 * group
    row_count = 2 * half_rows
    cells = half_rows * lanes
    step = pl.program_id(0)

    def spread_out(pair):
        for part in range(cells // tile):
            spread = dot(conv_t_ref[...], gpre_ref[0, :, part * tile : (part + 1) * tile])
            for dz in range(2):
                for dy in range(2):
                    first = (2 * dz + dy) * span
                    here = slice(part * tile + dy * lanes, (part + 1) * tile + dy * lanes)
                    spread_ref[slots.index(pair + dz), :, here] += spread[first : first + span]

    def lay_out(at, ch, value):
        z = at - 1
        out_ref[ch, z] = value
        out_ref[ch, z, 0:1] += after_ref[at, ch : ch + 1].astype(f32)
        out_ref[ch, z, row_count - 1 : row_count] += before_ref[at, ch : ch + 1].astype(f32)

    def finish(slot):
        rows = [
            merged(spread_ref[slots.index(slot), :, row * lanes : (row + 1) * lanes], group)
            for row in range(half_rows + 1)
        ]
        core = 0.0
        for value in split_two(jnp.concatenate(rows, axis=0)):
            core = core + dot(dot(row_t_ref[...], value).astype(bf16), merge_ref[...])
        for par in range(2):
            for ch in range(channels):
                first = (par * channels + ch) * row_count
                value = core[first : first + row_count]
                if taken:
                    lay_out(2 * slot + par, ch, value)
                else:
                    core_ref[2 * done.index(slot) + par, ch] = value

    for k, pair in enumerate(pairs):

        @pl.when(step == k)
        def _():
            if k == 0:
                for slot in slots:
                    if slot in taken:
                        spread_ref[slots.index(slot)] = taken_refs[taken.index(slot)][...]
                    else:
                        spread_ref[slots.index(slot)] = jnp.zeros(spread_ref.shape[1:], f32)
            if k == 0 and taken:
                fetched(list(zip(far_refs, near_refs, strict=True)), sems)
                for ch in range(channels):
                    lay_out(1, ch, outer_ref[1, ch] + above_ref[ch].astype(f32))
                    lay_out(depth, ch, outer_ref[2, ch] + below_ref[ch].astype(f32))
            for slot in done:
                if k > 0 and pairs[k - 1] in (slot - 1, slot) and not set(pairs[k:]) & {slot - 1, slot}:
                    finish(slot)
            spread_out(pair)
            if k == len(pairs) - 1:
                for slot in done:
                    if pair in (slot - 1, slot):
                        finish(slot)
                if not taken:
                    for slot, ref in zip(given, given_refs, strict=True):
                        ref[...] = spread_ref[slots.index(slot)]


def last_kernel(sizes, *refs):
    hidden, taps, big, parts = sizes
    conv_out, cbias_out, down_out, dbias_out, loss_out, here_ref, sems = refs[parts:]
    fetched([(ref, here_ref.at[i]) for i, ref in enumerate(refs[:parts])], sems)
    total = here_ref[0]
    for i in range(1, parts):
        total = total + here_ref[i]
    down_out[...] = total[:, :big]
    small = total[:, big:]
    while small.shape[0] < hidden:
        small = jnp.concatenate(jnp.split(small, 2, axis=1), axis=0)
    conv_out[...] = small[:, :taps]
    turned = jnp.transpose(small[:, lanes:])
    at = taps - lanes
    cbias_out[...] = turned[at : at + 1]
    dbias_out[...] = jnp.concatenate([turned[at + 1 : at + 2], turned[at + 2 : at + 3]], axis=1)
    loss_out[...] = jnp.sum(turned[at + 3 : at + 4] + turned[at + 4 : at + 5], axis=1, keepdims=True)


def call(kernel, sizes, out_shape, *args, grid=None, in_specs=None, out_specs=None, scratch=(), flops=0, vmem=16, name):
    if grid is None:
        grid = (1,)
        in_specs = [whole(a.shape) for a in args]
        out_specs = [whole(o.shape) for o in out_shape]
    return pl.pallas_call(
        functools.partial(kernel, sizes),
        out_shape=out_shape,
        in_specs=in_specs,
        out_specs=out_specs,
        scratch_shapes=scratch,
        compiler_params=pltpu.CompilerParams(vmem_limit_bytes=vmem * 1024 * 1024),
        cost_estimate=pl.CostEstimate(
            flops=flops,
            bytes_accessed=sum(a.size * a.dtype.itemsize for a in (*args, *out_shape)),
            transcendentals=0,
        ),
        name=name,
        grid=grid,
    )(*args)


def whole(shape):
    return pl.BlockSpec(tuple(shape), lambda z: (0,) * len(shape))


def constants(channels, row_count, half_cols, hidden):
    core, edge = row_spread(channels, row_count)
    names = {
        "col": column_merge(half_cols).T,
        "merge": column_merge(half_cols),
        "row": core,
        "row_t": core.T,
        "edge": edge,
        "edge_t": edge.T,
        "tap": tap_spread(channels),
        "order": class_order(hidden),
    }
    return {name: jnp.asarray(value, bf16) for name, value in names.items()}


def outer_rows(fields, below, above):
    channels, depth, row_count, col_count = fields.shape
    out = jax.ShapeDtypeStruct((depth + 2, 8, col_count), fields.dtype)
    block = (channels, depth, 16, col_count)
    beside = pl.BlockSpec(memory_space=pl.ANY)
    return call(
        rows_kernel,
        (channels, depth),
        [out, out],
        fields, fields, below, above,
        grid=(1,),
        in_specs=[
            pl.BlockSpec(block, lambda z: (0, 0, 0, 0)),
            pl.BlockSpec(block, lambda z: (0, 0, row_count // 16 - 1, 0)),
            beside,
            beside,
        ],
        out_specs=[whole(out.shape)] * 2,
        scratch=[pltpu.VMEM(below.shape, bf16), pltpu.VMEM(above.shape, bf16), pltpu.SemaphoreType.DMA((2,))],
        name="rows",
    )


def prepare(fields, below, above, conv_weight, conv_bias, down_weight, fixed):
    channels, depth, row_count, _ = fields.shape
    hidden, out_count = conv_weight.shape[0], down_weight.shape[0]
    pairs, half_rows = depth // 2, row_count // 2
    big, win = 8 * hidden, 64 * channels
    return call(
        prepare_kernel,
        (channels, pairs, half_rows, hidden),
        [
            jax.ShapeDtypeStruct((pairs + 1, 16 * channels, (half_rows + 1) * lanes), bf16),
            jax.ShapeDtypeStruct((big, win + 16), bf16),
            jax.ShapeDtypeStruct((win, big), bf16),
            jax.ShapeDtypeStruct((out_count, big), bf16),
            jax.ShapeDtypeStruct((big, out_count), bf16),
        ],
        fields, below, above, conv_weight, conv_bias[None], down_weight,
        fixed["tap"], fixed["order"], fixed["col"], fixed["row"],
        flops=2 * fields.size * row_count * channels * 4,
        name="prepare",
    )


def forward(early, before, after, target, conv, conv_t, down, down_t, down_bias, fixed, channels, cell_total, groups):
    out_count, pairs, half_rows, half_cols = target.shape
    win, big = conv_t.shape
    hidden = big // 8
    cells = half_rows * half_cols
    args = (
        early, before, after, target, conv, conv_t, down, down_t, down_bias[None],
        fixed["tap"], fixed["order"], fixed["col"], fixed["edge"], fixed["merge"], fixed["edge_t"],
    )
    slab = pl.BlockSpec((out_count, 1, half_rows, half_cols), lambda z: (0, z, 0, 0))
    rows = out_count // groups
    message = jax.ShapeDtypeStruct((rows, big + 2 * lanes * hidden // rows), f32)
    in_specs = [whole(a.shape) for a in args]
    for i in (0, 9, 10):
        in_specs[i] = pl.BlockSpec(memory_space=pl.ANY)
    for i in (1, 2):
        in_specs[i] = pl.BlockSpec(memory_space=pl.ANY)
    in_specs[3] = slab
    return call(
        forward_kernel,
        (channels, pairs, half_rows, hidden, out_count, forward_tile, cell_total, groups),
        [
            jax.ShapeDtypeStruct(target.shape, bf16),
            jax.ShapeDtypeStruct((pairs, big, cells), bf16),
            jax.ShapeDtypeStruct(before.shape, bf16),
            jax.ShapeDtypeStruct(after.shape, bf16),
        ]
        + [message] * groups,
        *args,
        grid=(pairs,),
        in_specs=in_specs,
        out_specs=[
            slab,
            pl.BlockSpec((1, big, cells), lambda z: (z, 0, 0)),
            whole(before.shape),
            whole(after.shape),
        ]
        + [whole(message.shape)] * groups,
        scratch=[
            pltpu.VMEM(early.shape, bf16),
            pltpu.VMEM((big, out_count), f32),
            pltpu.VMEM((win + 16, big), f32),
            pltpu.VMEM((out_count, lanes), f32),
            pltpu.VMEM((out_count, lanes), f32),
            pltpu.VMEM((2, big, forward_tile), bf16),
            pltpu.VMEM((2, big, forward_tile), f32),
            pltpu.VMEM((out_count, big), f32),
            pltpu.VMEM((2, pairs, big, lanes), bf16),
            pltpu.VMEM(fixed["tap"].shape, bf16),
            pltpu.VMEM(fixed["order"].shape, bf16),
            pltpu.VMEM((pairs + 1, 2, 16 * channels, lanes), f32),
            pltpu.VMEM(before.shape, bf16),
            pltpu.VMEM(after.shape, bf16),
            pltpu.SemaphoreType.DMA((pairs + 1,)),
            pltpu.SemaphoreType.DMA((4,)),
        ],
        flops=4 * pairs * cells * big * (win + out_count),
        vmem=40,
        name="forward",
    )


def spread(grad_pre, conv_t, fixed, shape, plan, taken=(), beside=()):
    channels, depth, row_count, col_count = shape
    _, big, cells = grad_pre.shape
    pairs, slots, _, done, given = plan
    open_shape = (16 * channels, cells + lanes)
    args = (grad_pre, conv_t, fixed["merge"], fixed["row_t"], *taken, *beside)
    if taken:
        outs = [jax.ShapeDtypeStruct(shape, f32)]
    else:
        outs = [jax.ShapeDtypeStruct((2 * len(done), channels, row_count, col_count), f32)]
    outs += [jax.ShapeDtypeStruct(open_shape, f32)] * len(given)
    first = pairs[0]
    stride = pairs[1] - first if len(pairs) > 1 else 1
    return call(
        spread_kernel,
        (channels, depth, row_count // 2, spread_tile, plan),
        outs,
        *args,
        grid=(len(pairs),),
        in_specs=[pl.BlockSpec((1, big, cells), lambda z: (first + stride * z, 0, 0))]
        + [whole(a.shape) for a in args[1 : len(args) - len(beside[1:])]]
        + [pl.BlockSpec(memory_space=pl.ANY) for _ in beside[1:]],
        out_specs=[whole(o.shape) for o in outs],
        scratch=[pltpu.VMEM((len(slots), *open_shape), f32)]
        + [pltpu.VMEM(a.shape, a.dtype) for a in beside[1:]]
        + ([pltpu.SemaphoreType.DMA((len(beside) - 1,))] if beside else []),
        flops=2 * len(pairs) * cells * big * conv_t.shape[0],
        vmem=32,
        name="spread",
    )


forward_tile = 1024
spread_tile = 1024


def on_device(fields, target, conv_weight, conv_bias, down_weight, down_bias):
    channels, depth, row_count, col_count = fields.shape
    hidden = conv_weight.shape[0]
    out_count = down_weight.shape[0]
    taps = channels * 27
    big = 8 * hidden
    cell_total = fields.size // channels // 8 * lax.axis_size("gz") * lax.axis_size("gy")
    fixed = constants(channels, row_count, col_count // 2, hidden)

    below = shifted(fields[:, depth - 1], "gz", 1)
    above = shifted(fields[:, 0], "gz", -1)
    first_rows, last_rows = outer_rows(fields, below, above)
    before = shifted(last_rows, "gy", 1)
    after = shifted(first_rows, "gy", -1)
    early, conv_big, conv_t, down_big, down_t = prepare(
        fields, below, above, conv_weight, conv_bias, down_weight, fixed
    )
    groups = lax.axis_size("gz") // 2
    out_field, grad_pre, to_before, to_after, *messages = forward(
        early, before, after, target, conv_big, conv_t, down_big, down_t, down_bias, fixed, channels, cell_total, groups
    )
    pairs = depth // 2
    shape = fields.shape

    got = [exchanged(message, "gz", 2 * far) for far, message in enumerate(messages) if far > 0]
    from_before = shifted(to_after, "gy", 1)
    from_after = shifted(to_before, "gy", -1)
    outer = ((0, pairs - 1), (0, 1, pairs - 1, pairs), (), (0, pairs), (1, pairs - 1))
    outer_core, low_open, high_open = spread(grad_pre, conv_t, fixed, shape, outer)
    packed = sum(got, messages[0])

    def plane(value, at):
        low = from_before[at, :channels, None].astype(f32)
        high = from_after[at, :channels, None].astype(f32)
        gap = jnp.zeros((channels, row_count - 2, col_count), f32)
        return (value + jnp.concatenate([low, gap, high], axis=1)).astype(bf16)

    from_below = shifted(plane(outer_core[3], depth + 1), "gz", 1)
    from_above = shifted(plane(outer_core[0], 0), "gz", -1)
    count = packed.shape[0] // 2
    core = lax.axis_index("gz") % 2
    own, small = packed[:, :big], beside(packed[:, big:], count)
    give = lax.dynamic_slice_in_dim(own, (1 - core) * count, count, 0)
    own = lax.dynamic_slice_in_dim(own, core * count, count, 0)
    packed = jnp.concatenate([own, small], axis=1) + exchanged(jnp.concatenate([give, small], axis=1), "gz", 1)

    packed, low_open = lax.optimization_barrier((packed, low_open))
    got = [exchanged(packed, "gy", far) for far in range(1, lax.axis_size("gy"))]
    inner = tuple(range(1, pairs - 1)), tuple(range(1, pairs)), (1, pairs - 1), tuple(range(1, pairs)), ()
    (sensitivity,) = spread(
        grad_pre, conv_t, fixed, shape, inner, (low_open, high_open),
        (outer_core, from_above, from_below, from_after, from_before),
    )
    conv, cbias, down, dbias, loss = call(
        last_kernel,
        (hidden, taps, big, 1 + len(got)),
        [
            jax.ShapeDtypeStruct((hidden, taps), f32),
            jax.ShapeDtypeStruct((1, hidden), f32),
            jax.ShapeDtypeStruct((count, big), f32),
            jax.ShapeDtypeStruct((1, out_count), f32),
            jax.ShapeDtypeStruct((1, 1), f32),
        ],
        packed, *got,
        grid=(1,),
        in_specs=[pl.BlockSpec(memory_space=pl.ANY)] * (1 + len(got)),
        out_specs=[pl.BlockSpec(memory_space=pltpu.VMEM)] * 5,
        scratch=[pltpu.VMEM((1 + len(got), *packed.shape), f32), pltpu.SemaphoreType.DMA((1 + len(got),))],
        name="last",
    )
    return out_field, sensitivity, conv, cbias[0], down, dbias[0], loss[0, 0]


def solution(mesh):
    in_specs = (P(None, "gz", "gy", None), P(None, "gz", "gy", None), P(), P(), P(), P())
    out_specs = (
        P(None, "gz", "gy", None),
        P(None, "gz", "gy", None),
        P(),
        P(),
        P("gz", None),
        P(),
        P(),
    )
    return jax.shard_map(
        on_device, mesh=mesh, in_specs=in_specs, out_specs=out_specs, check_vma=False
    )
```

```python
import functools

import jax
import jax.numpy as jnp
import numpy as np
from jax import lax
from jax.experimental import pallas as pl
from jax.experimental.pallas import tpu as pltpu
from jax.sharding import PartitionSpec as P

gelu_scale = 0.7978845608028654
gelu_cubic = 0.044715
lanes = 128
bf16 = jnp.bfloat16
f32 = jnp.float32


def shifted(value, axis, by):
    count = lax.axis_size(axis)
    return lax.ppermute(value, axis, [(i, (i + by) % count) for i in range(count)])


def exchanged(value, axis, bit):
    count = lax.axis_size(axis)
    return lax.ppermute(value, axis, [(i, i ^ bit) for i in range(count)])


def column_merge(half_cols):
    merge = np.zeros((2 * half_cols, 2 * half_cols), np.float32)
    for par in range(2):
        for col in range(half_cols):
            merge[par * half_cols + col, (2 * col + par - 1) % (2 * half_cols)] = 1
    return merge


def row_spread(channels, row_count):
    pair_rows = row_count // 2 + 1
    core = np.zeros((pair_rows * 4 * channels, 2 * channels * row_count), np.float32)
    edge = np.zeros((8 * channels, 32), np.float32)
    for par_z in range(2):
        for ch in range(channels):
            for at in range(1, row_count + 1):
                target = ((at // 2 * 2 + par_z) * 2 + at % 2) * channels + ch
                core[target, (par_z * channels + ch) * row_count + at - 1] = 1
            edge[(par_z * 2) * channels + ch, par_z * 16 + ch] = 1
            edge[((2 + par_z) * 2 + 1) * channels + ch, par_z * 16 + 8 + ch] = 1
    return core, edge


def tap_spread(channels):
    spread = np.zeros((8, channels * 27, 64 * channels), np.float32)
    for cls in range(8):
        par_z, par_y, par_x = cls // 4, cls // 2 % 2, cls % 2
        for ch in range(channels):
            for off_z in range(3):
                for off_y in range(3):
                    for off_x in range(3):
                        at_z, at_y, at_x = par_z + off_z, par_y + off_y, par_x + off_x
                        place = (at_z // 2 * 2 + at_y // 2) * 2 + at_x // 2
                        place = ((place * 2 + at_x % 2) * 2 + at_z % 2) * 2 + at_y % 2
                        spread[cls, ch * 27 + 9 * off_z + 3 * off_y + off_x, place * channels + ch] = 1
    return spread


def class_order(hidden):
    order = np.zeros((8 * hidden, 8 * hidden), np.float32)
    for ch in range(hidden):
        for cls in range(8):
            order[ch * 8 + cls, cls * hidden + ch] = 1
    return order


def dot(a, b):
    return jnp.dot(a, b, preferred_element_type=f32)


def dot_rows(a, b):
    return lax.dot_general(a, b, (((1,), (1,)), ((), ())), preferred_element_type=f32)


def split_two(value):
    high = value.astype(bf16)
    return high, (value - high.astype(f32)).astype(bf16)


def split_three(value):
    high = value.astype(bf16)
    return (high,) + split_two(value - high.astype(f32))


def beside(value, count):
    while value.shape[0] > count:
        value = jnp.concatenate(jnp.split(value, 2, axis=0), axis=1)
    return value


def conv_rows(conv_ref, tap_ref):
    return jnp.concatenate([dot(conv_ref[...], tap_ref[cls]) for cls in range(8)], axis=0)


def row_of(ref, count):
    return jnp.transpose(jnp.broadcast_to(ref[...], (lanes, count)))


def fetched(pairs_of_refs, sems):
    copies = [pltpu.make_async_copy(*refs, sems.at[i]) for i, refs in enumerate(pairs_of_refs)]
    for copy in copies:
        copy.start()
    for copy in copies:
        copy.wait()


def rows_kernel(
    sizes, low_ref, high_ref, far_below_ref, far_above_ref, first_out, last_out, below_ref, above_ref, sems
):
    channels, depth = sizes
    fetched([(far_below_ref, below_ref), (far_above_ref, above_ref)], sems)
    for ref, at, out in ((low_ref, 0, first_out), (high_ref, -1, last_out)):
        for z in range(depth + 2):
            rows = []
            for ch in range(channels):
                if z == 0:
                    value = below_ref[ch]
                elif z == depth + 1:
                    value = above_ref[ch]
                else:
                    value = ref[ch, z - 1]
                value = value.astype(f32)
                rows.append(value[:1] if at == 0 else value[value.shape[0] - 1 :])
            rows.append(jnp.zeros((8 - channels, rows[0].shape[1]), f32))
            out[z] = jnp.concatenate(rows, axis=0).astype(bf16)


def prepare_kernel(
    sizes,
    field_ref,
    below_ref,
    above_ref,
    conv_weight_ref,
    conv_bias_ref,
    down_weight_ref,
    tap_ref,
    order_ref,
    col_ref,
    row_ref,
    split_ref,
    conv_ref,
    conv_t_ref,
    down_ref,
    down_t_ref,
):
    channels, pairs, half_rows, hidden = sizes
    group = 4 * channels
    conv = conv_rows(conv_weight_ref, tap_ref)
    conv_t_ref[...] = jnp.transpose(conv).astype(bf16)
    conv_ref[:, : 16 * group] = (0.5 * conv).astype(bf16)
    bias = 0.5 * row_of(conv_bias_ref, hidden)
    at = lax.broadcasted_iota(jnp.int32, bias.shape, 1)
    columns = jnp.zeros_like(bias)
    for k, piece in enumerate(split_three(bias)):
        columns = jnp.where(at == k, piece.astype(f32), columns)
    columns = jnp.concatenate([columns[:, :16]] * 8, axis=0)
    conv_ref[:, 16 * group :] = columns.astype(bf16)
    down = dot(down_weight_ref[...], order_ref[...])
    down_ref[...] = down.astype(bf16)
    down_t_ref[...] = jnp.transpose(down).astype(bf16)
    for slot in range(pairs + 1):
        lower = below_ref if slot == 0 else field_ref.at[:, 2 * slot - 1]
        upper = above_ref if slot == pairs else field_ref.at[:, 2 * slot]
        rows = [ref[ch] for ref in (lower, upper) for ch in range(channels)]
        rows = dot(row_ref[...], jnp.concatenate(rows, axis=0)).astype(bf16)
        rows = dot(rows, col_ref[...])
        for row in range(half_rows + 1):
            piece = rows[row * group : (row + 1) * group]
            split_ref[slot, :, row * lanes : (row + 1) * lanes] = shifts_of(piece).astype(bf16)


def shifts_of(piece):
    piece = jnp.concatenate([piece[:, :lanes], piece[:, lanes:]], axis=0)
    return jnp.concatenate([piece, pltpu.roll(piece, lanes - 1, 1)], axis=0)


def forward_kernel(
    sizes,
    early_ref,
    far_before_ref,
    far_after_ref,
    target_ref,
    conv_ref,
    conv_t_ref,
    down_ref,
    down_t_ref,
    down_bias_ref,
    far_tap_ref,
    far_order_ref,
    col_ref,
    edge_ref,
    merge_ref,
    edge_t_ref,
    out_ref,
    gpre_ref,
    to_before_ref,
    to_after_ref,
    *rest,
):
    channels, pairs, half_rows, hidden, out_count, tile, cell_total, groups = sizes
    message_refs = rest[:groups]
    (
    split_ref,
    gdown_t_ref,
    gconv_t_ref,
    gdb_ref,
    sq_ref,
    hid_ref,
    slope_ref,
    whole_ref,
    outer_ref,
    tap_ref,
    order_ref,
    sides_ref,
    before_ref,
    after_ref,
    split_sem,
    late_sem,
    ) = rest[groups:]
    group = 4 * channels
    cells = half_rows * lanes
    step = pl.program_id(0)

    def arrival(slot):
        return pltpu.make_async_copy(early_ref.at[slot], split_ref.at[slot], split_sem.at[slot])

    late = [
        pltpu.make_async_copy(far_tap_ref, tap_ref, late_sem.at[0]),
        pltpu.make_async_copy(far_order_ref, order_ref, late_sem.at[1]),
    ]

    def complete(slot):
        arrival(slot).wait()
        for side, row in enumerate((0, half_rows)):
            here = slice(row * lanes, (row + 1) * lanes)
            value = split_ref[slot, :, here].astype(f32) + sides_ref[slot, side]
            split_ref[slot, :, here] = value.astype(bf16)

    @pl.when(step == 0)
    def _():
        sides = [
            pltpu.make_async_copy(far_before_ref, before_ref, late_sem.at[2]),
            pltpu.make_async_copy(far_after_ref, after_ref, late_sem.at[3]),
        ]
        for copy in sides:
            copy.start()
        for slot in range(pairs + 1):
            arrival(slot).start()
        for copy in late:
            copy.start()
        gdown_t_ref[...] = jnp.zeros_like(gdown_t_ref)
        gconv_t_ref[...] = jnp.zeros_like(gconv_t_ref)
        gdb_ref[...] = jnp.zeros_like(gdb_ref)
        sq_ref[...] = jnp.zeros_like(sq_ref)
        width = 2 * lanes
        rows = []
        for copy in sides:
            copy.wait()
        for slot in range(pairs + 1):
            sides = [ref[2 * slot + par].astype(f32) for par in range(2) for ref in (before_ref, after_ref)]
            rows.append(jnp.concatenate(sides, axis=0).astype(bf16))
        rows = dot(edge_ref[...], jnp.concatenate(rows, axis=1)).astype(bf16)
        rows = [rows[:, slot * width : (slot + 1) * width] for slot in range(pairs + 1)]
        rows = dot(jnp.concatenate(rows, axis=0), col_ref[...])
        for slot in range(pairs + 1):
            for side in range(2):
                first = (2 * slot + side) * group
                sides_ref[slot, side] = shifts_of(rows[first : first + group])
        complete(0)

    complete(step + 1)

    ones = jnp.ones((16, tile), bf16)
    down_bias = row_of(down_bias_ref, out_count)
    down_bias = jnp.concatenate([down_bias] * (tile // lanes), axis=1)
    wanted = jnp.swapaxes(target_ref[:, 0].astype(f32), 0, 1)
    parts = cells // tile
    count = tile // lanes

    def window_of(part):
        start, stop = part * tile, (part + 1) * tile
        return jnp.concatenate(
            [
                split_ref[step + dz, :, start + dy * lanes : stop + dy * lanes]
                for dz in range(2)
                for dy in range(2)
            ]
            + [ones],
            axis=0,
        )

    outputs, diffs = {}, {}

    def activate(part, rows):
        pre = dot(conv_ref[rows], window_of(part))
        square = pre * pre
        tangent = jnp.tanh(pre * (square * (8.0 * gelu_scale * gelu_cubic) + 2.0 * gelu_scale))
        above = 1.0 + tangent
        bend = pre * (square * (12.0 * gelu_scale * gelu_cubic) + gelu_scale)
        hid_ref[part % 2, rows] = (pre * above).astype(bf16)
        slope_ref[part % 2, rows] = above * ((1.0 - tangent) * bend + 0.5)

    def compare(part):
        output = dot(down_ref[...], hid_ref[part % 2]) + down_bias
        first = part * count
        diff = output - jnp.concatenate([wanted[first + k] for k in range(count)], axis=1)
        outputs[part] = [output[:, k * lanes : (k + 1) * lanes] for k in range(count)]
        for k in range(count):
            piece = diff[:, k * lanes : (k + 1) * lanes]
            gdb_ref[...] += piece
            sq_ref[...] += piece * piece
        diffs[part] = diff.astype(bf16)

    def weigh_down(part):
        gdown_t_ref[...] += dot_rows(hid_ref[part % 2], diffs[part])

    def back(part, rows):
        value = dot(down_t_ref[rows], diffs[part]) * slope_ref[part % 2, rows]
        gpre_ref[0, rows, part * tile : (part + 1) * tile] = value.astype(bf16)

    def weigh_conv(part):
        gconv_t_ref[...] += dot_rows(window_of(part), gpre_ref[0, :, part * tile : (part + 1) * tile])

    big = 8 * hidden
    blocks = [slice(0, big)]
    for part in range(parts + 1):
        first = [functools.partial(activate, part, rows) for rows in blocks] if part < parts else []
        second = []
        if part > 0:
            done = part - 1
            second = [functools.partial(compare, done), functools.partial(weigh_down, done)]
            second += [functools.partial(back, done, rows) for rows in blocks]
            second += [functools.partial(weigh_conv, done)]
        for k in range(max(len(first), len(second))):
            if k < len(second):
                second[k]()
            if k < len(first):
                first[k]()
    for side, at in enumerate((0, cells - lanes)):
        outer_ref[side, step] = gpre_ref[0, :, at : at + lanes]
    outputs = [value for part in range(parts) for value in outputs[part]]
    out_ref[:, 0] = jnp.swapaxes(jnp.stack(outputs, axis=0), 0, 1).astype(bf16)

    @pl.when(step == pairs - 1)
    def _():
        taps = channels * 27
        for copy in late:
            copy.wait()
        folded = 0.0
        cb = jnp.zeros((hidden, 1), f32)
        gconv = jnp.transpose(gconv_t_ref[...])
        for cls in range(8):
            rows = gconv[cls * hidden : (cls + 1) * hidden]
            cb = cb + rows[:, 16 * group : 16 * group + 1]
            rows = jnp.concatenate(split_three(rows[:, : 16 * group]), axis=0)
            folded = folded + dot_rows(rows, tap_ref[cls])
        folded = folded[:hidden] + (folded[hidden : 2 * hidden] + folded[2 * hidden :])
        columns = [folded, cb]
        for ref, share in ((gdb_ref, 1.0), (sq_ref, 1.0 / out_count)):
            total = share * jnp.sum(ref[...], axis=1, keepdims=True)
            columns += [total[:hidden], total[hidden:]]
        columns.append(jnp.zeros((hidden, 2 * lanes - taps - 5), f32))
        small = jnp.concatenate(columns, axis=1) / cell_total
        pieces = jnp.concatenate(split_three(jnp.transpose(gdown_t_ref[...])), axis=0)
        pieces = dot_rows(pieces, order_ref[...])
        grad_down = pieces[:out_count] + (pieces[out_count : 2 * out_count] + pieces[2 * out_count :])
        rows = out_count // len(message_refs)
        small = beside(small, rows)
        here = lax.axis_index("gz") // 2
        whole_ref[...] = grad_down / cell_total
        for far, ref in enumerate(message_refs):
            first = pl.multiple_of((here ^ far) * rows, rows)
            ref[:, : 8 * hidden] = whole_ref[pl.ds(first, rows)]
            ref[:, 8 * hidden :] = small
        sides_of(channels, pairs, outer_ref, conv_t_ref, merge_ref, edge_t_ref, to_before_ref, to_after_ref)


def merged(piece, group):
    halves = [
        piece[par * group : (par + 1) * group]
        + pltpu.roll(piece[(2 + par) * group : (3 + par) * group], 1, 1)
        for par in range(2)
    ]
    return jnp.concatenate(halves, axis=1)


def sides_of(channels, pairs, outer_ref, conv_t_ref, merge_ref, edge_t_ref, before_ref, after_ref):
    group = 4 * channels
    span = 4 * group
    found = []
    for dy in range(2):
        weights = [conv_t_ref[(2 * dz + dy) * span : (2 * dz + dy + 1) * span] for dz in range(2)]
        values = [outer_ref[dy, pair] for pair in range(pairs)]
        found.append(dot(jnp.concatenate(weights, axis=0), jnp.concatenate(values, axis=1)))
    rows = []
    for slot in range(pairs + 1):
        outer = []
        for value in found:
            total = 0.0
            for dz in range(2):
                pair = slot - dz
                if 0 <= pair < pairs:
                    total = total + value[dz * span : (dz + 1) * span, pair * lanes : (pair + 1) * lanes]
            outer.append(merged(total, group))
        rows.append(jnp.concatenate(outer, axis=0))
    width = 2 * lanes
    sides = 0.0
    for value in split_two(jnp.concatenate(rows, axis=1)):
        value = dot(edge_t_ref[...], value).astype(bf16)
        value = [value[:, slot * width : (slot + 1) * width] for slot in range(pairs + 1)]
        sides = sides + dot(jnp.concatenate(value, axis=0), merge_ref[...])
    for at in range(2 * pairs + 2):
        before_ref[at] = sides[at * 16 : at * 16 + 8].astype(bf16)
        after_ref[at] = sides[at * 16 + 8 : at * 16 + 16].astype(bf16)


def spread_kernel(sizes, *refs):
    channels, depth, half_rows, tile, plan = sizes
    pairs, slots, taken, done, given = plan
    gpre_ref, conv_t_ref, merge_ref, row_t_ref = refs[:4]
    rest = refs[4:-1]
    spread_ref = refs[-1]
    if taken:
        rest, spread_ref = refs[4:-6], refs[-6]
        taken_refs = rest[: len(taken)]
        outer_ref, *far_refs, out_ref = rest[len(taken) :]
        near_refs, sems = refs[-5:-1], refs[-1]
        below_ref, above_ref, before_ref, after_ref = near_refs
    else:
        core_ref, *given_refs = rest
    group = 4 * channels
    span = 4 * group
    row_count = 2 * half_rows
    cells = half_rows * lanes
    step = pl.program_id(0)

    def spread_out(pair):
        for part in range(cells // tile):
            spread = dot(conv_t_ref[...], gpre_ref[0, :, part * tile : (part + 1) * tile])
            for dz in range(2):
                for dy in range(2):
                    first = (2 * dz + dy) * span
                    here = slice(part * tile + dy * lanes, (part + 1) * tile + dy * lanes)
                    spread_ref[slots.index(pair + dz), :, here] += spread[first : first + span]

    def lay_out(at, ch, value):
        z = at - 1
        out_ref[ch, z] = value
        out_ref[ch, z, 0:1] += after_ref[at, ch : ch + 1].astype(f32)
        out_ref[ch, z, row_count - 1 : row_count] += before_ref[at, ch : ch + 1].astype(f32)

    def finish(slot):
        rows = [
            merged(spread_ref[slots.index(slot), :, row * lanes : (row + 1) * lanes], group)
            for row in range(half_rows + 1)
        ]
        core = 0.0
        for value in split_two(jnp.concatenate(rows, axis=0)):
            core = core + dot(dot(row_t_ref[...], value).astype(bf16), merge_ref[...])
        for par in range(2):
            for ch in range(channels):
                first = (par * channels + ch) * row_count
                value = core[first : first + row_count]
                if taken:
                    lay_out(2 * slot + par, ch, value)
                else:
                    core_ref[2 * done.index(slot) + par, ch] = value

    for k, pair in enumerate(pairs):

        @pl.when(step == k)
        def _():
            if k == 0:
                for slot in slots:
                    if slot in taken:
                        spread_ref[slots.index(slot)] = taken_refs[taken.index(slot)][...]
                    else:
                        spread_ref[slots.index(slot)] = jnp.zeros(spread_ref.shape[1:], f32)
            if k == 0 and taken:
                fetched(list(zip(far_refs, near_refs, strict=True)), sems)
                for ch in range(channels):
                    lay_out(1, ch, outer_ref[1, ch] + above_ref[ch].astype(f32))
                    lay_out(depth, ch, outer_ref[2, ch] + below_ref[ch].astype(f32))
            for slot in done:
                if k > 0 and pairs[k - 1] in (slot - 1, slot) and not set(pairs[k:]) & {slot - 1, slot}:
                    finish(slot)
            spread_out(pair)
            if k == len(pairs) - 1:
                for slot in done:
                    if pair in (slot - 1, slot):
                        finish(slot)
                if not taken:
                    for slot, ref in zip(given, given_refs, strict=True):
                        ref[...] = spread_ref[slots.index(slot)]


def last_kernel(sizes, *refs):
    hidden, taps, big, parts = sizes
    conv_out, cbias_out, down_out, dbias_out, loss_out, here_ref, sems = refs[parts:]
    fetched([(ref, here_ref.at[i]) for i, ref in enumerate(refs[:parts])], sems)
    total = here_ref[0]
    for i in range(1, parts):
        total = total + here_ref[i]
    down_out[...] = total[:, :big]
    small = total[:, big:]
    while small.shape[0] < hidden:
        small = jnp.concatenate(jnp.split(small, 2, axis=1), axis=0)
    conv_out[...] = small[:, :taps]
    turned = jnp.transpose(small[:, lanes:])
    at = taps - lanes
    cbias_out[...] = turned[at : at + 1]
    dbias_out[...] = jnp.concatenate([turned[at + 1 : at + 2], turned[at + 2 : at + 3]], axis=1)
    loss_out[...] = jnp.sum(turned[at + 3 : at + 4] + turned[at + 4 : at + 5], axis=1, keepdims=True)


def call(kernel, sizes, out_shape, *args, grid=None, in_specs=None, out_specs=None, scratch=(), flops=0, vmem=16, name):
    if grid is None:
        grid = (1,)
        in_specs = [whole(a.shape) for a in args]
        out_specs = [whole(o.shape) for o in out_shape]
    return pl.pallas_call(
        functools.partial(kernel, sizes),
        out_shape=out_shape,
        in_specs=in_specs,
        out_specs=out_specs,
        scratch_shapes=scratch,
        compiler_params=pltpu.CompilerParams(vmem_limit_bytes=vmem * 1024 * 1024),
        cost_estimate=pl.CostEstimate(
            flops=flops,
            bytes_accessed=sum(a.size * a.dtype.itemsize for a in (*args, *out_shape)),
            transcendentals=0,
        ),
        name=name,
        grid=grid,
    )(*args)


def whole(shape):
    return pl.BlockSpec(tuple(shape), lambda z: (0,) * len(shape))


def constants(channels, row_count, half_cols, hidden):
    core, edge = row_spread(channels, row_count)
    names = {
        "col": column_merge(half_cols).T,
        "merge": column_merge(half_cols),
        "row": core,
        "row_t": core.T,
        "edge": edge,
        "edge_t": edge.T,
        "tap": tap_spread(channels),
        "order": class_order(hidden),
    }
    return {name: jnp.asarray(value, bf16) for name, value in names.items()}


def outer_rows(fields, below, above):
    channels, depth, row_count, col_count = fields.shape
    out = jax.ShapeDtypeStruct((depth + 2, 8, col_count), fields.dtype)
    block = (channels, depth, 16, col_count)
    beside = pl.BlockSpec(memory_space=pl.ANY)
    return call(
        rows_kernel,
        (channels, depth),
        [out, out],
        fields, fields, below, above,
        grid=(1,),
        in_specs=[
            pl.BlockSpec(block, lambda z: (0, 0, 0, 0)),
            pl.BlockSpec(block, lambda z: (0, 0, row_count // 16 - 1, 0)),
            beside,
            beside,
        ],
        out_specs=[whole(out.shape)] * 2,
        scratch=[pltpu.VMEM(below.shape, bf16), pltpu.VMEM(above.shape, bf16), pltpu.SemaphoreType.DMA((2,))],
        name="rows",
    )


def prepare(fields, below, above, conv_weight, conv_bias, down_weight, fixed):
    channels, depth, row_count, _ = fields.shape
    hidden, out_count = conv_weight.shape[0], down_weight.shape[0]
    pairs, half_rows = depth // 2, row_count // 2
    big, win = 8 * hidden, 64 * channels
    return call(
        prepare_kernel,
        (channels, pairs, half_rows, hidden),
        [
            jax.ShapeDtypeStruct((pairs + 1, 16 * channels, (half_rows + 1) * lanes), bf16),
            jax.ShapeDtypeStruct((big, win + 16), bf16),
            jax.ShapeDtypeStruct((win, big), bf16),
            jax.ShapeDtypeStruct((out_count, big), bf16),
            jax.ShapeDtypeStruct((big, out_count), bf16),
        ],
        fields, below, above, conv_weight, conv_bias[None], down_weight,
        fixed["tap"], fixed["order"], fixed["col"], fixed["row"],
        flops=2 * fields.size * row_count * channels * 4,
        name="prepare",
    )


def forward(early, before, after, target, conv, conv_t, down, down_t, down_bias, fixed, channels, cell_total, groups):
    out_count, pairs, half_rows, half_cols = target.shape
    win, big = conv_t.shape
    hidden = big // 8
    cells = half_rows * half_cols
    args = (
        early, before, after, target, conv, conv_t, down, down_t, down_bias[None],
        fixed["tap"], fixed["order"], fixed["col"], fixed["edge"], fixed["merge"], fixed["edge_t"],
    )
    slab = pl.BlockSpec((out_count, 1, half_rows, half_cols), lambda z: (0, z, 0, 0))
    rows = out_count // groups
    message = jax.ShapeDtypeStruct((rows, big + 2 * lanes * hidden // rows), f32)
    in_specs = [whole(a.shape) for a in args]
    for i in (0, 9, 10):
        in_specs[i] = pl.BlockSpec(memory_space=pl.ANY)
    for i in (1, 2):
        in_specs[i] = pl.BlockSpec(memory_space=pl.ANY)
    in_specs[3] = slab
    return call(
        forward_kernel,
        (channels, pairs, half_rows, hidden, out_count, forward_tile, cell_total, groups),
        [
            jax.ShapeDtypeStruct(target.shape, bf16),
            jax.ShapeDtypeStruct((pairs, big, cells), bf16),
            jax.ShapeDtypeStruct(before.shape, bf16),
            jax.ShapeDtypeStruct(after.shape, bf16),
        ]
        + [message] * groups,
        *args,
        grid=(pairs,),
        in_specs=in_specs,
        out_specs=[
            slab,
            pl.BlockSpec((1, big, cells), lambda z: (z, 0, 0)),
            whole(before.shape),
            whole(after.shape),
        ]
        + [whole(message.shape)] * groups,
        scratch=[
            pltpu.VMEM(early.shape, bf16),
            pltpu.VMEM((big, out_count), f32),
            pltpu.VMEM((win + 16, big), f32),
            pltpu.VMEM((out_count, lanes), f32),
            pltpu.VMEM((out_count, lanes), f32),
            pltpu.VMEM((2, big, forward_tile), bf16),
            pltpu.VMEM((2, big, forward_tile), f32),
            pltpu.VMEM((out_count, big), f32),
            pltpu.VMEM((2, pairs, big, lanes), bf16),
            pltpu.VMEM(fixed["tap"].shape, bf16),
            pltpu.VMEM(fixed["order"].shape, bf16),
            pltpu.VMEM((pairs + 1, 2, 16 * channels, lanes), f32),
            pltpu.VMEM(before.shape, bf16),
            pltpu.VMEM(after.shape, bf16),
            pltpu.SemaphoreType.DMA((pairs + 1,)),
            pltpu.SemaphoreType.DMA((4,)),
        ],
        flops=4 * pairs * cells * big * (win + out_count),
        vmem=36,
        name="forward",
    )


def spread(grad_pre, conv_t, fixed, shape, plan, taken=(), beside=()):
    channels, depth, row_count, col_count = shape
    _, big, cells = grad_pre.shape
    pairs, slots, _, done, given = plan
    open_shape = (16 * channels, cells + lanes)
    args = (grad_pre, conv_t, fixed["merge"], fixed["row_t"], *taken, *beside)
    if taken:
        outs = [jax.ShapeDtypeStruct(shape, f32)]
    else:
        outs = [jax.ShapeDtypeStruct((2 * len(done), channels, row_count, col_count), f32)]
    outs += [jax.ShapeDtypeStruct(open_shape, f32)] * len(given)
    first = pairs[0]
    stride = pairs[1] - first if len(pairs) > 1 else 1
    return call(
        spread_kernel,
        (channels, depth, row_count // 2, spread_tile, plan),
        outs,
        *args,
        grid=(len(pairs),),
        in_specs=[pl.BlockSpec((1, big, cells), lambda z: (first + stride * z, 0, 0))]
        + [whole(a.shape) for a in args[1 : len(args) - len(beside[1:])]]
        + [pl.BlockSpec(memory_space=pl.ANY) for _ in beside[1:]],
        out_specs=[whole(o.shape) for o in outs],
        scratch=[pltpu.VMEM((len(slots), *open_shape), f32)]
        + [pltpu.VMEM(a.shape, a.dtype) for a in beside[1:]]
        + ([pltpu.SemaphoreType.DMA((len(beside) - 1,))] if beside else []),
        flops=2 * len(pairs) * cells * big * conv_t.shape[0],
        vmem=20,
        name="spread",
    )


forward_tile = 1024
spread_tile = 1024


def on_device(fields, target, conv_weight, conv_bias, down_weight, down_bias):
    channels, depth, row_count, col_count = fields.shape
    hidden = conv_weight.shape[0]
    out_count = down_weight.shape[0]
    taps = channels * 27
    big = 8 * hidden
    cell_total = fields.size // channels // 8 * lax.axis_size("gz") * lax.axis_size("gy")
    fixed = constants(channels, row_count, col_count // 2, hidden)

    below = shifted(fields[:, depth - 1], "gz", 1)
    above = shifted(fields[:, 0], "gz", -1)
    first_rows, last_rows = outer_rows(fields, below, above)
    before = shifted(last_rows, "gy", 1)
    after = shifted(first_rows, "gy", -1)
    early, conv_big, conv_t, down_big, down_t = prepare(
        fields, below, above, conv_weight, conv_bias, down_weight, fixed
    )
    groups = lax.axis_size("gz") // 2
    out_field, grad_pre, to_before, to_after, *messages = forward(
        early, before, after, target, conv_big, conv_t, down_big, down_t, down_bias, fixed, channels, cell_total, groups
    )
    pairs = depth // 2
    shape = fields.shape

    got = [exchanged(message, "gz", 2 * far) for far, message in enumerate(messages) if far > 0]
    from_before = shifted(to_after, "gy", 1)
    from_after = shifted(to_before, "gy", -1)
    outer = ((0, pairs - 1), (0, 1, pairs - 1, pairs), (), (0, pairs), (1, pairs - 1))
    outer_core, low_open, high_open = spread(grad_pre, conv_t, fixed, shape, outer)
    packed = sum(got, messages[0])

    def plane(value, at):
        low = from_before[at, :channels, None].astype(f32)
        high = from_after[at, :channels, None].astype(f32)
        gap = jnp.zeros((channels, row_count - 2, col_count), f32)
        return (value + jnp.concatenate([low, gap, high], axis=1)).astype(bf16)

    from_below = shifted(plane(outer_core[3], depth + 1), "gz", 1)
    from_above = shifted(plane(outer_core[0], 0), "gz", -1)
    count = packed.shape[0] // 2
    core = lax.axis_index("gz") % 2
    own, small = packed[:, :big], beside(packed[:, big:], count)
    give = lax.dynamic_slice_in_dim(own, (1 - core) * count, count, 0)
    own = lax.dynamic_slice_in_dim(own, core * count, count, 0)
    packed = jnp.concatenate([own, small], axis=1) + exchanged(jnp.concatenate([give, small], axis=1), "gz", 1)

    packed, low_open = lax.optimization_barrier((packed, low_open))
    got = [exchanged(packed, "gy", far) for far in range(1, lax.axis_size("gy"))]
    inner = tuple(range(1, pairs - 1)), tuple(range(1, pairs)), (1, pairs - 1), tuple(range(1, pairs)), ()
    (sensitivity,) = spread(
        grad_pre, conv_t, fixed, shape, inner, (low_open, high_open),
        (outer_core, from_above, from_below, from_after, from_before),
    )
    conv, cbias, down, dbias, loss = call(
        last_kernel,
        (hidden, taps, big, 1 + len(got)),
        [
            jax.ShapeDtypeStruct((hidden, taps), f32),
            jax.ShapeDtypeStruct((1, hidden), f32),
            jax.ShapeDtypeStruct((count, big), f32),
            jax.ShapeDtypeStruct((1, out_count), f32),
            jax.ShapeDtypeStruct((1, 1), f32),
        ],
        packed, *got,
        grid=(1,),
        in_specs=[pl.BlockSpec(memory_space=pl.ANY)] * (1 + len(got)),
        out_specs=[pl.BlockSpec(memory_space=pltpu.VMEM)] * 5,
        scratch=[pltpu.VMEM((1 + len(got), *packed.shape), f32), pltpu.SemaphoreType.DMA((1 + len(got),))],
        name="last",
    )
    return out_field, sensitivity, conv, cbias[0], down, dbias[0], loss[0, 0]


def solution(mesh):
    in_specs = (P(None, "gz", "gy", None), P(None, "gz", "gy", None), P(), P(), P(), P())
    out_specs = (
        P(None, "gz", "gy", None),
        P(None, "gz", "gy", None),
        P(),
        P(),
        P("gz", None),
        P(),
        P(),
    )
    return jax.shard_map(
        on_device, mesh=mesh, in_specs=in_specs, out_specs=out_specs, check_vma=False
    )
```

```python
import functools

import jax
import jax.numpy as jnp
import numpy as np
from jax import lax
from jax.experimental import pallas as pl
from jax.experimental.pallas import tpu as pltpu
from jax.sharding import PartitionSpec as P

gelu_scale = 0.7978845608028654
gelu_cubic = 0.044715
lanes = 128
bf16 = jnp.bfloat16
f32 = jnp.float32


def shifted(value, axis, by):
    count = lax.axis_size(axis)
    return lax.ppermute(value, axis, [(i, (i + by) % count) for i in range(count)])


def exchanged(value, axis, bit):
    count = lax.axis_size(axis)
    return lax.ppermute(value, axis, [(i, i ^ bit) for i in range(count)])


def column_merge(half_cols):
    merge = np.zeros((2 * half_cols, 2 * half_cols), np.float32)
    for par in range(2):
        for col in range(half_cols):
            merge[par * half_cols + col, (2 * col + par - 1) % (2 * half_cols)] = 1
    return merge


def row_spread(channels, row_count):
    pair_rows = row_count // 2 + 1
    core = np.zeros((pair_rows * 4 * channels, 2 * channels * row_count), np.float32)
    edge = np.zeros((8 * channels, 32), np.float32)
    for par_z in range(2):
        for ch in range(channels):
            for at in range(1, row_count + 1):
                target = ((at // 2 * 2 + par_z) * 2 + at % 2) * channels + ch
                core[target, (par_z * channels + ch) * row_count + at - 1] = 1
            edge[(par_z * 2) * channels + ch, par_z * 16 + ch] = 1
            edge[((2 + par_z) * 2 + 1) * channels + ch, par_z * 16 + 8 + ch] = 1
    return core, edge


def tap_spread(channels):
    spread = np.zeros((8, channels * 27, 64 * channels), np.float32)
    for cls in range(8):
        par_z, par_y, par_x = cls // 4, cls // 2 % 2, cls % 2
        for ch in range(channels):
            for off_z in range(3):
                for off_y in range(3):
                    for off_x in range(3):
                        at_z, at_y, at_x = par_z + off_z, par_y + off_y, par_x + off_x
                        place = (at_z // 2 * 2 + at_y // 2) * 2 + at_x // 2
                        place = ((place * 2 + at_x % 2) * 2 + at_z % 2) * 2 + at_y % 2
                        spread[cls, ch * 27 + 9 * off_z + 3 * off_y + off_x, place * channels + ch] = 1
    return spread


def class_order(hidden):
    order = np.zeros((8 * hidden, 8 * hidden), np.float32)
    for ch in range(hidden):
        for cls in range(8):
            order[ch * 8 + cls, cls * hidden + ch] = 1
    return order


def dot(a, b):
    return jnp.dot(a, b, preferred_element_type=f32)


def dot_rows(a, b):
    return lax.dot_general(a, b, (((1,), (1,)), ((), ())), preferred_element_type=f32)


def split_two(value):
    high = value.astype(bf16)
    return high, (value - high.astype(f32)).astype(bf16)


def split_three(value):
    high = value.astype(bf16)
    return (high,) + split_two(value - high.astype(f32))


def beside(value, count):
    while value.shape[0] > count:
        value = jnp.concatenate(jnp.split(value, 2, axis=0), axis=1)
    return value


def conv_rows(conv_ref, tap_ref):
    return jnp.concatenate([dot(conv_ref[...], tap_ref[cls]) for cls in range(8)], axis=0)


def row_of(ref, count):
    return jnp.transpose(jnp.broadcast_to(ref[...], (lanes, count)))


def fetched(pairs_of_refs, sems):
    copies = [pltpu.make_async_copy(*refs, sems.at[i]) for i, refs in enumerate(pairs_of_refs)]
    for copy in copies:
        copy.start()
    for copy in copies:
        copy.wait()


def rows_kernel(sizes, low_ref, high_ref, first_out, last_out):
    channels, depth = sizes
    for ref, at, out in ((low_ref, 0, first_out), (high_ref, 15, last_out)):
        for z in range(depth):
            rows = [ref[ch, z].astype(f32)[at : at + 1] for ch in range(channels)]
            rows.append(jnp.zeros((8 - channels, rows[0].shape[1]), f32))
            out[z] = jnp.concatenate(rows, axis=0).astype(bf16)


def more_rows_kernel(sizes, *refs):
    channels, depth = sizes
    first_out, last_out, first_ref, last_ref, below_ref, above_ref, sems = refs[4:]
    fetched(list(zip(refs[:4], (first_ref, last_ref, below_ref, above_ref), strict=True)), sems)
    count = below_ref.shape[1]
    for ref, at, out in ((first_ref, 0, first_out), (last_ref, count - 1, last_out)):
        out[1 : depth + 1] = ref[...]
        for z, plane_ref in ((0, below_ref), (depth + 1, above_ref)):
            rows = [plane_ref[ch].astype(f32)[at : at + 1] for ch in range(channels)]
            rows.append(jnp.zeros((8 - channels, rows[0].shape[1]), f32))
            out[z] = jnp.concatenate(rows, axis=0).astype(bf16)


def prepare_kernel(
    sizes,
    field_ref,
    below_ref,
    above_ref,
    conv_weight_ref,
    conv_bias_ref,
    down_weight_ref,
    tap_ref,
    order_ref,
    col_ref,
    row_ref,
    split_ref,
    conv_ref,
    conv_t_ref,
    down_ref,
    down_t_ref,
):
    channels, pairs, half_rows, hidden = sizes
    group = 4 * channels
    conv = conv_rows(conv_weight_ref, tap_ref)
    conv_t_ref[...] = jnp.transpose(conv).astype(bf16)
    conv_ref[:, : 16 * group] = (0.5 * conv).astype(bf16)
    bias = 0.5 * row_of(conv_bias_ref, hidden)
    at = lax.broadcasted_iota(jnp.int32, bias.shape, 1)
    columns = jnp.zeros_like(bias)
    for k, piece in enumerate(split_three(bias)):
        columns = jnp.where(at == k, piece.astype(f32), columns)
    columns = jnp.concatenate([columns[:, :16]] * 8, axis=0)
    conv_ref[:, 16 * group :] = columns.astype(bf16)
    down = dot(down_weight_ref[...], order_ref[...])
    down_ref[...] = down.astype(bf16)
    down_t_ref[...] = jnp.transpose(down).astype(bf16)
    for slot in range(pairs + 1):
        lower = below_ref if slot == 0 else field_ref.at[:, 2 * slot - 1]
        upper = above_ref if slot == pairs else field_ref.at[:, 2 * slot]
        rows = [ref[ch] for ref in (lower, upper) for ch in range(channels)]
        rows = dot(row_ref[...], jnp.concatenate(rows, axis=0)).astype(bf16)
        rows = dot(rows, col_ref[...])
        for row in range(half_rows + 1):
            piece = rows[row * group : (row + 1) * group]
            split_ref[slot, :, row * lanes : (row + 1) * lanes] = shifts_of(piece).astype(bf16)


def shifts_of(piece):
    piece = jnp.concatenate([piece[:, :lanes], piece[:, lanes:]], axis=0)
    return jnp.concatenate([piece, pltpu.roll(piece, lanes - 1, 1)], axis=0)


def forward_kernel(
    sizes,
    early_ref,
    far_before_ref,
    far_after_ref,
    target_ref,
    conv_ref,
    conv_t_ref,
    down_ref,
    down_t_ref,
    down_bias_ref,
    far_tap_ref,
    far_order_ref,
    col_ref,
    edge_ref,
    merge_ref,
    edge_t_ref,
    out_ref,
    gpre_ref,
    to_before_ref,
    to_after_ref,
    *rest,
):
    channels, pairs, half_rows, hidden, out_count, tile, cell_total, groups = sizes
    message_refs = rest[:groups]
    (
    split_ref,
    gdown_t_ref,
    gconv_t_ref,
    gdb_ref,
    sq_ref,
    hid_ref,
    slope_ref,
    whole_ref,
    outer_ref,
    tap_ref,
    order_ref,
    sides_ref,
    before_ref,
    after_ref,
    split_sem,
    late_sem,
    ) = rest[groups:]
    group = 4 * channels
    cells = half_rows * lanes
    step = pl.program_id(0)

    def arrival(slot):
        return pltpu.make_async_copy(early_ref.at[slot], split_ref.at[slot], split_sem.at[slot])

    late = [
        pltpu.make_async_copy(far_tap_ref, tap_ref, late_sem.at[0]),
        pltpu.make_async_copy(far_order_ref, order_ref, late_sem.at[1]),
    ]

    def complete(slot):
        arrival(slot).wait()
        for side, row in enumerate((0, half_rows)):
            here = slice(row * lanes, (row + 1) * lanes)
            value = split_ref[slot, :, here].astype(f32) + sides_ref[slot, side]
            split_ref[slot, :, here] = value.astype(bf16)

    @pl.when(step == 0)
    def _():
        sides = [
            pltpu.make_async_copy(far_before_ref, before_ref, late_sem.at[2]),
            pltpu.make_async_copy(far_after_ref, after_ref, late_sem.at[3]),
        ]
        for copy in sides:
            copy.start()
        for slot in range(pairs + 1):
            arrival(slot).start()
        for copy in late:
            copy.start()
        gdown_t_ref[...] = jnp.zeros_like(gdown_t_ref)
        gconv_t_ref[...] = jnp.zeros_like(gconv_t_ref)
        gdb_ref[...] = jnp.zeros_like(gdb_ref)
        sq_ref[...] = jnp.zeros_like(sq_ref)
        width = 2 * lanes
        rows = []
        for copy in sides:
            copy.wait()
        for slot in range(pairs + 1):
            sides = [ref[2 * slot + par].astype(f32) for par in range(2) for ref in (before_ref, after_ref)]
            rows.append(jnp.concatenate(sides, axis=0).astype(bf16))
        rows = dot(edge_ref[...], jnp.concatenate(rows, axis=1)).astype(bf16)
        rows = [rows[:, slot * width : (slot + 1) * width] for slot in range(pairs + 1)]
        rows = dot(jnp.concatenate(rows, axis=0), col_ref[...])
        for slot in range(pairs + 1):
            for side in range(2):
                first = (2 * slot + side) * group
                sides_ref[slot, side] = shifts_of(rows[first : first + group])
        complete(0)

    complete(step + 1)

    ones = jnp.ones((16, tile), bf16)
    down_bias = row_of(down_bias_ref, out_count)
    down_bias = jnp.concatenate([down_bias] * (tile // lanes), axis=1)
    wanted = jnp.swapaxes(target_ref[:, 0].astype(f32), 0, 1)
    parts = cells // tile
    count = tile // lanes

    def window_of(part):
        start, stop = part * tile, (part + 1) * tile
        return jnp.concatenate(
            [
                split_ref[step + dz, :, start + dy * lanes : stop + dy * lanes]
                for dz in range(2)
                for dy in range(2)
            ]
            + [ones],
            axis=0,
        )

    outputs, diffs = {}, {}

    def activate(part, rows):
        pre = dot(conv_ref[rows], window_of(part))
        square = pre * pre
        tangent = jnp.tanh(pre * (square * (8.0 * gelu_scale * gelu_cubic) + 2.0 * gelu_scale))
        above = 1.0 + tangent
        bend = pre * (square * (12.0 * gelu_scale * gelu_cubic) + gelu_scale)
        hid_ref[part % 2, rows] = (pre * above).astype(bf16)
        slope_ref[part % 2, rows] = above * ((1.0 - tangent) * bend + 0.5)

    def compare(part):
        output = dot(down_ref[...], hid_ref[part % 2]) + down_bias
        first = part * count
        diff = output - jnp.concatenate([wanted[first + k] for k in range(count)], axis=1)
        outputs[part] = [output[:, k * lanes : (k + 1) * lanes] for k in range(count)]
        for k in range(count):
            piece = diff[:, k * lanes : (k + 1) * lanes]
            gdb_ref[...] += piece
            sq_ref[...] += piece * piece
        diffs[part] = diff.astype(bf16)

    def weigh_down(part):
        gdown_t_ref[...] += dot_rows(hid_ref[part % 2], diffs[part])

    def back(part, rows):
        value = dot(down_t_ref[rows], diffs[part]) * slope_ref[part % 2, rows]
        gpre_ref[0, rows, part * tile : (part + 1) * tile] = value.astype(bf16)

    def weigh_conv(part):
        gconv_t_ref[...] += dot_rows(window_of(part), gpre_ref[0, :, part * tile : (part + 1) * tile])

    big = 8 * hidden
    blocks = [slice(0, big)]
    for part in range(parts + 1):
        first = [functools.partial(activate, part, rows) for rows in blocks] if part < parts else []
        second = []
        if part > 0:
            done = part - 1
            second = [functools.partial(compare, done), functools.partial(weigh_down, done)]
            second += [functools.partial(back, done, rows) for rows in blocks]
            second += [functools.partial(weigh_conv, done)]
        for k in range(max(len(first), len(second))):
            if k < len(second):
                second[k]()
            if k < len(first):
                first[k]()
    for side, at in enumerate((0, cells - lanes)):
        outer_ref[side, step] = gpre_ref[0, :, at : at + lanes]
    outputs = [value for part in range(parts) for value in outputs[part]]
    out_ref[:, 0] = jnp.swapaxes(jnp.stack(outputs, axis=0), 0, 1).astype(bf16)

    @pl.when(step == pairs - 1)
    def _():
        taps = channels * 27
        for copy in late:
            copy.wait()
        folded = 0.0
        cb = jnp.zeros((hidden, 1), f32)
        gconv = jnp.transpose(gconv_t_ref[...])
        for cls in range(8):
            rows = gconv[cls * hidden : (cls + 1) * hidden]
            cb = cb + rows[:, 16 * group : 16 * group + 1]
            rows = jnp.concatenate(split_three(rows[:, : 16 * group]), axis=0)
            folded = folded + dot_rows(rows, tap_ref[cls])
        folded = folded[:hidden] + (folded[hidden : 2 * hidden] + folded[2 * hidden :])
        columns = [folded, cb]
        for ref, share in ((gdb_ref, 1.0), (sq_ref, 1.0 / out_count)):
            total = share * jnp.sum(ref[...], axis=1, keepdims=True)
            columns += [total[:hidden], total[hidden:]]
        columns.append(jnp.zeros((hidden, 2 * lanes - taps - 5), f32))
        small = jnp.concatenate(columns, axis=1) / cell_total
        pieces = jnp.concatenate(split_three(jnp.transpose(gdown_t_ref[...])), axis=0)
        pieces = dot_rows(pieces, order_ref[...])
        grad_down = pieces[:out_count] + (pieces[out_count : 2 * out_count] + pieces[2 * out_count :])
        rows = out_count // len(message_refs)
        small = beside(small, rows)
        here = lax.axis_index("gz") // 2
        whole_ref[...] = grad_down / cell_total
        for far, ref in enumerate(message_refs):
            first = pl.multiple_of((here ^ far) * rows, rows)
            ref[:, : 8 * hidden] = whole_ref[pl.ds(first, rows)]
            ref[:, 8 * hidden :] = small
        sides_of(channels, pairs, outer_ref, conv_t_ref, merge_ref, edge_t_ref, to_before_ref, to_after_ref)


def merged(piece, group):
    halves = [
        piece[par * group : (par + 1) * group]
        + pltpu.roll(piece[(2 + par) * group : (3 + par) * group], 1, 1)
        for par in range(2)
    ]
    return jnp.concatenate(halves, axis=1)


def sides_of(channels, pairs, outer_ref, conv_t_ref, merge_ref, edge_t_ref, before_ref, after_ref):
    group = 4 * channels
    span = 4 * group
    found = []
    for dy in range(2):
        weights = [conv_t_ref[(2 * dz + dy) * span : (2 * dz + dy + 1) * span] for dz in range(2)]
        values = [outer_ref[dy, pair] for pair in range(pairs)]
        found.append(dot(jnp.concatenate(weights, axis=0), jnp.concatenate(values, axis=1)))
    rows = []
    for slot in range(pairs + 1):
        outer = []
        for value in found:
            total = 0.0
            for dz in range(2):
                pair = slot - dz
                if 0 <= pair < pairs:
                    total = total + value[dz * span : (dz + 1) * span, pair * lanes : (pair + 1) * lanes]
            outer.append(merged(total, group))
        rows.append(jnp.concatenate(outer, axis=0))
    width = 2 * lanes
    sides = 0.0
    for value in split_two(jnp.concatenate(rows, axis=1)):
        value = dot(edge_t_ref[...], value).astype(bf16)
        value = [value[:, slot * width : (slot + 1) * width] for slot in range(pairs + 1)]
        sides = sides + dot(jnp.concatenate(value, axis=0), merge_ref[...])
    for at in range(2 * pairs + 2):
        before_ref[at] = sides[at * 16 : at * 16 + 8].astype(bf16)
        after_ref[at] = sides[at * 16 + 8 : at * 16 + 16].astype(bf16)


def spread_kernel(sizes, *refs):
    channels, depth, half_rows, tile, plan = sizes
    pairs, slots, taken, done, given = plan
    gpre_ref, conv_t_ref, merge_ref, row_t_ref = refs[:4]
    rest = refs[4:-1]
    spread_ref = refs[-1]
    if taken:
        rest, spread_ref = refs[4:-6], refs[-6]
        taken_refs = rest[: len(taken)]
        outer_ref, *far_refs, out_ref = rest[len(taken) :]
        near_refs, sems = refs[-5:-1], refs[-1]
        below_ref, above_ref, before_ref, after_ref = near_refs
    else:
        core_ref, *given_refs = rest
    group = 4 * channels
    span = 4 * group
    row_count = 2 * half_rows
    cells = half_rows * lanes
    step = pl.program_id(0)

    def spread_out(pair):
        for part in range(cells // tile):
            spread = dot(conv_t_ref[...], gpre_ref[0, :, part * tile : (part + 1) * tile])
            for dz in range(2):
                for dy in range(2):
                    first = (2 * dz + dy) * span
                    here = slice(part * tile + dy * lanes, (part + 1) * tile + dy * lanes)
                    spread_ref[slots.index(pair + dz), :, here] += spread[first : first + span]

    def lay_out(at, ch, value):
        z = at - 1
        out_ref[ch, z] = value
        out_ref[ch, z, 0:1] += after_ref[at, ch : ch + 1].astype(f32)
        out_ref[ch, z, row_count - 1 : row_count] += before_ref[at, ch : ch + 1].astype(f32)

    def finish(slot):
        rows = [
            merged(spread_ref[slots.index(slot), :, row * lanes : (row + 1) * lanes], group)
            for row in range(half_rows + 1)
        ]
        core = 0.0
        for value in split_two(jnp.concatenate(rows, axis=0)):
            core = core + dot(dot(row_t_ref[...], value).astype(bf16), merge_ref[...])
        for par in range(2):
            for ch in range(channels):
                first = (par * channels + ch) * row_count
                value = core[first : first + row_count]
                if taken:
                    lay_out(2 * slot + par, ch, value)
                else:
                    core_ref[2 * done.index(slot) + par, ch] = value

    for k, pair in enumerate(pairs):

        @pl.when(step == k)
        def _():
            if k == 0:
                for slot in slots:
                    if slot in taken:
                        spread_ref[slots.index(slot)] = taken_refs[taken.index(slot)][...]
                    else:
                        spread_ref[slots.index(slot)] = jnp.zeros(spread_ref.shape[1:], f32)
            if k == 0 and taken:
                fetched(list(zip(far_refs, near_refs, strict=True)), sems)
                for ch in range(channels):
                    lay_out(1, ch, outer_ref[1, ch] + above_ref[ch].astype(f32))
                    lay_out(depth, ch, outer_ref[2, ch] + below_ref[ch].astype(f32))
            for slot in done:
                if k > 0 and pairs[k - 1] in (slot - 1, slot) and not set(pairs[k:]) & {slot - 1, slot}:
                    finish(slot)
            spread_out(pair)
            if k == len(pairs) - 1:
                for slot in done:
                    if pair in (slot - 1, slot):
                        finish(slot)
                if not taken:
                    for slot, ref in zip(given, given_refs, strict=True):
                        ref[...] = spread_ref[slots.index(slot)]


def last_kernel(sizes, *refs):
    hidden, taps, big, parts = sizes
    conv_out, cbias_out, down_out, dbias_out, loss_out, here_ref, sems = refs[parts:]
    fetched([(ref, here_ref.at[i]) for i, ref in enumerate(refs[:parts])], sems)
    total = here_ref[0]
    for i in range(1, parts):
        total = total + here_ref[i]
    down_out[...] = total[:, :big]
    small = total[:, big:]
    while small.shape[0] < hidden:
        small = jnp.concatenate(jnp.split(small, 2, axis=1), axis=0)
    conv_out[...] = small[:, :taps]
    turned = jnp.transpose(small[:, lanes:])
    at = taps - lanes
    cbias_out[...] = turned[at : at + 1]
    dbias_out[...] = jnp.concatenate([turned[at + 1 : at + 2], turned[at + 2 : at + 3]], axis=1)
    loss_out[...] = jnp.sum(turned[at + 3 : at + 4] + turned[at + 4 : at + 5], axis=1, keepdims=True)


def call(kernel, sizes, out_shape, *args, grid=None, in_specs=None, out_specs=None, scratch=(), flops=0, vmem=16, name):
    if grid is None:
        grid = (1,)
        in_specs = [whole(a.shape) for a in args]
        out_specs = [whole(o.shape) for o in out_shape]
    return pl.pallas_call(
        functools.partial(kernel, sizes),
        out_shape=out_shape,
        in_specs=in_specs,
        out_specs=out_specs,
        scratch_shapes=scratch,
        compiler_params=pltpu.CompilerParams(vmem_limit_bytes=vmem * 1024 * 1024),
        cost_estimate=pl.CostEstimate(
            flops=flops,
            bytes_accessed=sum(a.size * a.dtype.itemsize for a in (*args, *out_shape)),
            transcendentals=0,
        ),
        name=name,
        grid=grid,
    )(*args)


def whole(shape):
    return pl.BlockSpec(tuple(shape), lambda z: (0,) * len(shape))


def constants(channels, row_count, half_cols, hidden):
    core, edge = row_spread(channels, row_count)
    names = {
        "col": column_merge(half_cols).T,
        "merge": column_merge(half_cols),
        "row": core,
        "row_t": core.T,
        "edge": edge,
        "edge_t": edge.T,
        "tap": tap_spread(channels),
        "order": class_order(hidden),
    }
    return {name: jnp.asarray(value, bf16) for name, value in names.items()}


def outer_rows(fields):
    channels, depth, row_count, col_count = fields.shape
    out = jax.ShapeDtypeStruct((depth, 8, col_count), fields.dtype)
    block = (channels, depth, 16, col_count)
    return call(
        rows_kernel,
        (channels, depth),
        [out, out],
        fields, fields,
        grid=(1,),
        in_specs=[
            pl.BlockSpec(block, lambda z: (0, 0, 0, 0)),
            pl.BlockSpec(block, lambda z: (0, 0, row_count // 16 - 1, 0)),
        ],
        out_specs=[whole(out.shape)] * 2,
        name="rows",
    )


def more_rows(first_rows, last_rows, below, above):
    depth, _, col_count = first_rows.shape
    out = jax.ShapeDtypeStruct((depth + 2, 8, col_count), first_rows.dtype)
    args = (first_rows, last_rows, below, above)
    return call(
        more_rows_kernel,
        (below.shape[0], depth),
        [out, out],
        *args,
        grid=(1,),
        in_specs=[pl.BlockSpec(memory_space=pl.ANY)] * 4,
        out_specs=[whole(out.shape)] * 2,
        scratch=[pltpu.VMEM(a.shape, a.dtype) for a in args] + [pltpu.SemaphoreType.DMA((4,))],
        name="more_rows",
    )


def prepare(fields, below, above, conv_weight, conv_bias, down_weight, fixed):
    channels, depth, row_count, _ = fields.shape
    hidden, out_count = conv_weight.shape[0], down_weight.shape[0]
    pairs, half_rows = depth // 2, row_count // 2
    big, win = 8 * hidden, 64 * channels
    return call(
        prepare_kernel,
        (channels, pairs, half_rows, hidden),
        [
            jax.ShapeDtypeStruct((pairs + 1, 16 * channels, (half_rows + 1) * lanes), bf16),
            jax.ShapeDtypeStruct((big, win + 16), bf16),
            jax.ShapeDtypeStruct((win, big), bf16),
            jax.ShapeDtypeStruct((out_count, big), bf16),
            jax.ShapeDtypeStruct((big, out_count), bf16),
        ],
        fields, below, above, conv_weight, conv_bias[None], down_weight,
        fixed["tap"], fixed["order"], fixed["col"], fixed["row"],
        flops=2 * fields.size * row_count * channels * 4,
        name="prepare",
    )


def forward(early, before, after, target, conv, conv_t, down, down_t, down_bias, fixed, channels, cell_total, groups):
    out_count, pairs, half_rows, half_cols = target.shape
    win, big = conv_t.shape
    hidden = big // 8
    cells = half_rows * half_cols
    args = (
        early, before, after, target, conv, conv_t, down, down_t, down_bias[None],
        fixed["tap"], fixed["order"], fixed["col"], fixed["edge"], fixed["merge"], fixed["edge_t"],
    )
    slab = pl.BlockSpec((out_count, 1, half_rows, half_cols), lambda z: (0, z, 0, 0))
    rows = out_count // groups
    message = jax.ShapeDtypeStruct((rows, big + 2 * lanes * hidden // rows), f32)
    in_specs = [whole(a.shape) for a in args]
    for i in (0, 9, 10):
        in_specs[i] = pl.BlockSpec(memory_space=pl.ANY)
    for i in (1, 2):
        in_specs[i] = pl.BlockSpec(memory_space=pl.ANY)
    in_specs[3] = slab
    return call(
        forward_kernel,
        (channels, pairs, half_rows, hidden, out_count, forward_tile, cell_total, groups),
        [
            jax.ShapeDtypeStruct(target.shape, bf16),
            jax.ShapeDtypeStruct((pairs, big, cells), bf16),
            jax.ShapeDtypeStruct(before.shape, bf16),
            jax.ShapeDtypeStruct(after.shape, bf16),
        ]
        + [message] * groups,
        *args,
        grid=(pairs,),
        in_specs=in_specs,
        out_specs=[
            slab,
            pl.BlockSpec((1, big, cells), lambda z: (z, 0, 0)),
            whole(before.shape),
            whole(after.shape),
        ]
        + [whole(message.shape)] * groups,
        scratch=[
            pltpu.VMEM(early.shape, bf16),
            pltpu.VMEM((big, out_count), f32),
            pltpu.VMEM((win + 16, big), f32),
            pltpu.VMEM((out_count, lanes), f32),
            pltpu.VMEM((out_count, lanes), f32),
            pltpu.VMEM((2, big, forward_tile), bf16),
            pltpu.VMEM((2, big, forward_tile), f32),
            pltpu.VMEM((out_count, big), f32),
            pltpu.VMEM((2, pairs, big, lanes), bf16),
            pltpu.VMEM(fixed["tap"].shape, bf16),
            pltpu.VMEM(fixed["order"].shape, bf16),
            pltpu.VMEM((pairs + 1, 2, 16 * channels, lanes), f32),
            pltpu.VMEM(before.shape, bf16),
            pltpu.VMEM(after.shape, bf16),
            pltpu.SemaphoreType.DMA((pairs + 1,)),
            pltpu.SemaphoreType.DMA((4,)),
        ],
        flops=4 * pairs * cells * big * (win + out_count),
        vmem=36,
        name="forward",
    )


def spread(grad_pre, conv_t, fixed, shape, plan, taken=(), beside=()):
    channels, depth, row_count, col_count = shape
    _, big, cells = grad_pre.shape
    pairs, slots, _, done, given = plan
    open_shape = (16 * channels, cells + lanes)
    args = (grad_pre, conv_t, fixed["merge"], fixed["row_t"], *taken, *beside)
    if taken:
        outs = [jax.ShapeDtypeStruct(shape, f32)]
    else:
        outs = [jax.ShapeDtypeStruct((2 * len(done), channels, row_count, col_count), f32)]
    outs += [jax.ShapeDtypeStruct(open_shape, f32)] * len(given)
    first = pairs[0]
    stride = pairs[1] - first if len(pairs) > 1 else 1
    return call(
        spread_kernel,
        (channels, depth, row_count // 2, spread_tile, plan),
        outs,
        *args,
        grid=(len(pairs),),
        in_specs=[pl.BlockSpec((1, big, cells), lambda z: (first + stride * z, 0, 0))]
        + [whole(a.shape) for a in args[1 : len(args) - len(beside[1:])]]
        + [pl.BlockSpec(memory_space=pl.ANY) for _ in beside[1:]],
        out_specs=[whole(o.shape) for o in outs],
        scratch=[pltpu.VMEM((len(slots), *open_shape), f32)]
        + [pltpu.VMEM(a.shape, a.dtype) for a in beside[1:]]
        + ([pltpu.SemaphoreType.DMA((len(beside) - 1,))] if beside else []),
        flops=2 * len(pairs) * cells * big * conv_t.shape[0],
        vmem=20,
        name="spread",
    )


forward_tile = 1024
spread_tile = 1024


def on_device(fields, target, conv_weight, conv_bias, down_weight, down_bias):
    channels, depth, row_count, col_count = fields.shape
    hidden = conv_weight.shape[0]
    out_count = down_weight.shape[0]
    taps = channels * 27
    big = 8 * hidden
    cell_total = fields.size // channels // 8 * lax.axis_size("gz") * lax.axis_size("gy")
    fixed = constants(channels, row_count, col_count // 2, hidden)

    below = shifted(fields[:, depth - 1], "gz", 1)
    above = shifted(fields[:, 0], "gz", -1)
    first_rows, last_rows = more_rows(*outer_rows(fields), below, above)
    before = shifted(last_rows, "gy", 1)
    after = shifted(first_rows, "gy", -1)
    early, conv_big, conv_t, down_big, down_t = prepare(
        fields, below, above, conv_weight, conv_bias, down_weight, fixed
    )
    groups = lax.axis_size("gz") // 2
    out_field, grad_pre, to_before, to_after, *messages = forward(
        early, before, after, target, conv_big, conv_t, down_big, down_t, down_bias, fixed, channels, cell_total, groups
    )
    pairs = depth // 2
    shape = fields.shape

    from_before = shifted(to_after, "gy", 1)
    from_after = shifted(to_before, "gy", -1)
    got = [exchanged(message, "gz", 2 * far) for far, message in enumerate(messages) if far > 0]
    from_before, from_after, *got = lax.optimization_barrier((from_before, from_after, *got))
    outer = ((0, pairs - 1), (0, 1, pairs - 1, pairs), (), (0, pairs), (1, pairs - 1))
    outer_core, low_open, high_open = spread(grad_pre, conv_t, fixed, shape, outer)
    packed = sum(got, messages[0])

    def plane(value, at):
        low = from_before[at, :channels, None].astype(f32)
        high = from_after[at, :channels, None].astype(f32)
        gap = jnp.zeros((channels, row_count - 2, col_count), f32)
        return (value + jnp.concatenate([low, gap, high], axis=1)).astype(bf16)

    from_below = shifted(plane(outer_core[3], depth + 1), "gz", 1)
    from_above = shifted(plane(outer_core[0], 0), "gz", -1)
    count = packed.shape[0] // 2
    core = lax.axis_index("gz") % 2
    own, small = packed[:, :big], beside(packed[:, big:], count)
    give = lax.dynamic_slice_in_dim(own, (1 - core) * count, count, 0)
    own = lax.dynamic_slice_in_dim(own, core * count, count, 0)
    packed = jnp.concatenate([own, small], axis=1) + exchanged(jnp.concatenate([give, small], axis=1), "gz", 1)

    packed, low_open = lax.optimization_barrier((packed, low_open))
    got = [exchanged(packed, "gy", far) for far in range(1, lax.axis_size("gy"))]
    inner = tuple(range(1, pairs - 1)), tuple(range(1, pairs)), (1, pairs - 1), tuple(range(1, pairs)), ()
    (sensitivity,) = spread(
        grad_pre, conv_t, fixed, shape, inner, (low_open, high_open),
        (outer_core, from_above, from_below, from_after, from_before),
    )
    conv, cbias, down, dbias, loss = call(
        last_kernel,
        (hidden, taps, big, 1 + len(got)),
        [
            jax.ShapeDtypeStruct((hidden, taps), f32),
            jax.ShapeDtypeStruct((1, hidden), f32),
            jax.ShapeDtypeStruct((count, big), f32),
            jax.ShapeDtypeStruct((1, out_count), f32),
            jax.ShapeDtypeStruct((1, 1), f32),
        ],
        packed, *got,
        grid=(1,),
        in_specs=[pl.BlockSpec(memory_space=pl.ANY)] * (1 + len(got)),
        out_specs=[pl.BlockSpec(memory_space=pltpu.VMEM)] * 5,
        scratch=[pltpu.VMEM((1 + len(got), *packed.shape), f32), pltpu.SemaphoreType.DMA((1 + len(got),))],
        name="last",
    )
    return out_field, sensitivity, conv, cbias[0], down, dbias[0], loss[0, 0]


def solution(mesh):
    in_specs = (P(None, "gz", "gy", None), P(None, "gz", "gy", None), P(), P(), P(), P())
    out_specs = (
        P(None, "gz", "gy", None),
        P(None, "gz", "gy", None),
        P(),
        P(),
        P("gz", None),
        P(),
        P(),
    )
    return jax.shard_map(
        on_device, mesh=mesh, in_specs=in_specs, out_specs=out_specs, check_vma=False
    )
```

```python
import functools

import jax
import jax.numpy as jnp
import numpy as np
from jax import lax
from jax.experimental import pallas as pl
from jax.experimental.pallas import tpu as pltpu
from jax.sharding import PartitionSpec as P

gelu_scale = 0.7978845608028654
gelu_cubic = 0.044715
lanes = 128
bf16 = jnp.bfloat16
f32 = jnp.float32


def shifted(value, axis, by):
    count = lax.axis_size(axis)
    return lax.ppermute(value, axis, [(i, (i + by) % count) for i in range(count)])


def exchanged(value, axis, bit):
    count = lax.axis_size(axis)
    return lax.ppermute(value, axis, [(i, i ^ bit) for i in range(count)])


def merge_table(width, turned=False):
    place = lax.broadcasted_iota(jnp.int32, (width, width), 1 if turned else 0)
    found = lax.broadcasted_iota(jnp.int32, (width, width), 0 if turned else 1)
    half = width // 2
    at = jnp.where(place < half, 2 * place - 1, 2 * (place - half))
    at = jnp.where(at < 0, width - 1, at)
    return jnp.where(found == at, 1.0, 0.0).astype(bf16)


def row_spread(channels, row_count):
    pair_rows = row_count // 2 + 1
    core = np.zeros((pair_rows * 4 * channels, 2 * channels * row_count), np.float32)
    edge = np.zeros((8 * channels, 32), np.float32)
    for par_z in range(2):
        for ch in range(channels):
            for at in range(1, row_count + 1):
                target = ((at // 2 * 2 + par_z) * 2 + at % 2) * channels + ch
                core[target, (par_z * channels + ch) * row_count + at - 1] = 1
            edge[(par_z * 2) * channels + ch, par_z * 16 + ch] = 1
            edge[((2 + par_z) * 2 + 1) * channels + ch, par_z * 16 + 8 + ch] = 1
    return core, edge


def tap_spread(channels):
    spread = np.zeros((8, channels * 27, 64 * channels), np.float32)
    for cls in range(8):
        par_z, par_y, par_x = cls // 4, cls // 2 % 2, cls % 2
        for ch in range(channels):
            for off_z in range(3):
                for off_y in range(3):
                    for off_x in range(3):
                        at_z, at_y, at_x = par_z + off_z, par_y + off_y, par_x + off_x
                        place = (at_z // 2 * 2 + at_y // 2) * 2 + at_x // 2
                        place = ((place * 2 + at_x % 2) * 2 + at_z % 2) * 2 + at_y % 2
                        spread[cls, ch * 27 + 9 * off_z + 3 * off_y + off_x, place * channels + ch] = 1
    return spread


def class_order(hidden):
    order = np.zeros((8 * hidden, 8 * hidden), np.float32)
    for ch in range(hidden):
        for cls in range(8):
            order[ch * 8 + cls, cls * hidden + ch] = 1
    return order


def dot(a, b):
    return jnp.dot(a, b, preferred_element_type=f32)


def dot_rows(a, b):
    return lax.dot_general(a, b, (((1,), (1,)), ((), ())), preferred_element_type=f32)


def split_two(value):
    high = value.astype(bf16)
    return high, (value - high.astype(f32)).astype(bf16)


def split_three(value):
    high = value.astype(bf16)
    return (high,) + split_two(value - high.astype(f32))


def beside(value, count):
    while value.shape[0] > count:
        value = jnp.concatenate(jnp.split(value, 2, axis=0), axis=1)
    return value


def conv_rows(conv_ref, tap_ref):
    return jnp.concatenate([dot(conv_ref[...], tap_ref[cls]) for cls in range(8)], axis=0)


def row_of(ref, count):
    return jnp.transpose(jnp.broadcast_to(ref[...], (lanes, count)))


def fetched(pairs_of_refs, sems):
    copies = [pltpu.make_async_copy(*refs, sems.at[i]) for i, refs in enumerate(pairs_of_refs)]
    for copy in copies:
        copy.start()
    for copy in copies:
        copy.wait()


def rows_kernel(sizes, low_ref, high_ref, first_out, last_out):
    channels, depth = sizes
    for ref, at, out in ((low_ref, 0, first_out), (high_ref, 15, last_out)):
        for z in range(depth):
            rows = [ref[ch, z].astype(f32)[at : at + 1] for ch in range(channels)]
            rows.append(jnp.zeros((8 - channels, rows[0].shape[1]), f32))
            out[z] = jnp.concatenate(rows, axis=0).astype(bf16)


def more_rows_kernel(sizes, *refs):
    channels, depth = sizes
    first_out, last_out, first_ref, last_ref, below_ref, above_ref, sems = refs[4:]
    fetched(list(zip(refs[:4], (first_ref, last_ref, below_ref, above_ref), strict=True)), sems)
    count = below_ref.shape[1]
    for ref, at, out in ((first_ref, 0, first_out), (last_ref, count - 1, last_out)):
        out[1 : depth + 1] = ref[...]
        for z, plane_ref in ((0, below_ref), (depth + 1, above_ref)):
            rows = [plane_ref[ch].astype(f32)[at : at + 1] for ch in range(channels)]
            rows.append(jnp.zeros((8 - channels, rows[0].shape[1]), f32))
            out[z] = jnp.concatenate(rows, axis=0).astype(bf16)


def prepare_kernel(
    sizes,
    field_ref,
    below_ref,
    above_ref,
    conv_weight_ref,
    conv_bias_ref,
    down_weight_ref,
    tap_ref,
    order_ref,
    row_ref,
    split_ref,
    conv_ref,
    conv_t_ref,
    down_ref,
    down_t_ref,
):
    channels, pairs, half_rows, hidden = sizes
    group = 4 * channels
    conv = conv_rows(conv_weight_ref, tap_ref)
    conv_t_ref[...] = jnp.transpose(conv).astype(bf16)
    conv_ref[:, : 16 * group] = (0.5 * conv).astype(bf16)
    bias = 0.5 * row_of(conv_bias_ref, hidden)
    at = lax.broadcasted_iota(jnp.int32, bias.shape, 1)
    columns = jnp.zeros_like(bias)
    for k, piece in enumerate(split_three(bias)):
        columns = jnp.where(at == k, piece.astype(f32), columns)
    columns = jnp.concatenate([columns[:, :16]] * 8, axis=0)
    conv_ref[:, 16 * group :] = columns.astype(bf16)
    down = dot(down_weight_ref[...], order_ref[...])
    down_ref[...] = down.astype(bf16)
    down_t_ref[...] = jnp.transpose(down).astype(bf16)
    for slot in range(pairs + 1):
        lower = below_ref if slot == 0 else field_ref.at[:, 2 * slot - 1]
        upper = above_ref if slot == pairs else field_ref.at[:, 2 * slot]
        rows = [ref[ch] for ref in (lower, upper) for ch in range(channels)]
        rows = dot(row_ref[...], jnp.concatenate(rows, axis=0)).astype(bf16)
        rows = dot(rows, merge_table(2 * lanes, turned=True))
        for row in range(half_rows + 1):
            piece = rows[row * group : (row + 1) * group]
            split_ref[slot, :, row * lanes : (row + 1) * lanes] = shifts_of(piece).astype(bf16)


def shifts_of(piece):
    piece = jnp.concatenate([piece[:, :lanes], piece[:, lanes:]], axis=0)
    return jnp.concatenate([piece, pltpu.roll(piece, lanes - 1, 1)], axis=0)


def forward_kernel(
    sizes,
    early_ref,
    far_before_ref,
    far_after_ref,
    target_ref,
    conv_ref,
    conv_t_ref,
    down_ref,
    down_t_ref,
    down_bias_ref,
    far_tap_ref,
    far_order_ref,
    edge_ref,
    edge_t_ref,
    out_ref,
    gpre_ref,
    to_before_ref,
    to_after_ref,
    *rest,
):
    channels, pairs, half_rows, hidden, out_count, tile, cell_total, groups = sizes
    message_refs = rest[:groups]
    (
    split_ref,
    gdown_t_ref,
    gconv_t_ref,
    gdb_ref,
    sq_ref,
    hid_ref,
    slope_ref,
    whole_ref,
    outer_ref,
    tap_ref,
    order_ref,
    sides_ref,
    before_ref,
    after_ref,
    split_sem,
    late_sem,
    ) = rest[groups:]
    group = 4 * channels
    cells = half_rows * lanes
    step = pl.program_id(0)

    def arrival(slot):
        return pltpu.make_async_copy(early_ref.at[slot], split_ref.at[slot], split_sem.at[slot])

    late = [
        pltpu.make_async_copy(far_tap_ref, tap_ref, late_sem.at[0]),
        pltpu.make_async_copy(far_order_ref, order_ref, late_sem.at[1]),
    ]

    def complete(slot):
        arrival(slot).wait()
        for side, row in enumerate((0, half_rows)):
            here = slice(row * lanes, (row + 1) * lanes)
            value = split_ref[slot, :, here].astype(f32) + sides_ref[slot, side]
            split_ref[slot, :, here] = value.astype(bf16)

    @pl.when(step == 0)
    def _():
        sides = [
            pltpu.make_async_copy(far_before_ref, before_ref, late_sem.at[2]),
            pltpu.make_async_copy(far_after_ref, after_ref, late_sem.at[3]),
        ]
        for copy in sides:
            copy.start()
        for slot in range(pairs + 1):
            arrival(slot).start()
        for copy in late:
            copy.start()
        gdown_t_ref[...] = jnp.zeros_like(gdown_t_ref)
        gconv_t_ref[...] = jnp.zeros_like(gconv_t_ref)
        gdb_ref[...] = jnp.zeros_like(gdb_ref)
        sq_ref[...] = jnp.zeros_like(sq_ref)
        width = 2 * lanes
        rows = []
        for copy in sides:
            copy.wait()
        for slot in range(pairs + 1):
            sides = [ref[2 * slot + par].astype(f32) for par in range(2) for ref in (before_ref, after_ref)]
            rows.append(jnp.concatenate(sides, axis=0).astype(bf16))
        rows = dot(edge_ref[...], jnp.concatenate(rows, axis=1)).astype(bf16)
        rows = [rows[:, slot * width : (slot + 1) * width] for slot in range(pairs + 1)]
        rows = dot(jnp.concatenate(rows, axis=0), merge_table(2 * lanes, turned=True))
        for slot in range(pairs + 1):
            for side in range(2):
                first = (2 * slot + side) * group
                sides_ref[slot, side] = shifts_of(rows[first : first + group])
        complete(0)

    complete(step + 1)

    ones = jnp.ones((16, tile), bf16)
    down_bias = row_of(down_bias_ref, out_count)
    down_bias = jnp.concatenate([down_bias] * (tile // lanes), axis=1)
    wanted = jnp.swapaxes(target_ref[:, 0].astype(f32), 0, 1)
    parts = cells // tile
    count = tile // lanes

    def window_of(part):
        start, stop = part * tile, (part + 1) * tile
        return jnp.concatenate(
            [
                split_ref[step + dz, :, start + dy * lanes : stop + dy * lanes]
                for dz in range(2)
                for dy in range(2)
            ]
            + [ones],
            axis=0,
        )

    outputs, diffs = {}, {}

    def activate(part, rows):
        pre = dot(conv_ref[rows], window_of(part))
        square = pre * pre
        tangent = jnp.tanh(pre * (square * (8.0 * gelu_scale * gelu_cubic) + 2.0 * gelu_scale))
        above = 1.0 + tangent
        bend = pre * (square * (12.0 * gelu_scale * gelu_cubic) + gelu_scale)
        hid_ref[part % 2, rows] = (pre * above).astype(bf16)
        slope_ref[part % 2, rows] = above * ((1.0 - tangent) * bend + 0.5)

    def compare(part):
        output = dot(down_ref[...], hid_ref[part % 2]) + down_bias
        first = part * count
        diff = output - jnp.concatenate([wanted[first + k] for k in range(count)], axis=1)
        outputs[part] = [output[:, k * lanes : (k + 1) * lanes] for k in range(count)]
        for k in range(count):
            piece = diff[:, k * lanes : (k + 1) * lanes]
            gdb_ref[...] += piece
            sq_ref[...] += piece * piece
        diffs[part] = diff.astype(bf16)

    def weigh_down(part):
        gdown_t_ref[...] += dot_rows(hid_ref[part % 2], diffs[part])

    def back(part, rows):
        value = dot(down_t_ref[rows], diffs[part]) * slope_ref[part % 2, rows]
        gpre_ref[0, rows, part * tile : (part + 1) * tile] = value.astype(bf16)

    def weigh_conv(part):
        gconv_t_ref[...] += dot_rows(window_of(part), gpre_ref[0, :, part * tile : (part + 1) * tile])

    big = 8 * hidden
    blocks = [slice(0, big)]
    for part in range(parts + 1):
        first = [functools.partial(activate, part, rows) for rows in blocks] if part < parts else []
        second = []
        if part > 0:
            done = part - 1
            second = [functools.partial(compare, done), functools.partial(weigh_down, done)]
            second += [functools.partial(back, done, rows) for rows in blocks]
            second += [functools.partial(weigh_conv, done)]
        for k in range(max(len(first), len(second))):
            if k < len(second):
                second[k]()
            if k < len(first):
                first[k]()
    for side, at in enumerate((0, cells - lanes)):
        outer_ref[side, step] = gpre_ref[0, :, at : at + lanes]
    outputs = [value for part in range(parts) for value in outputs[part]]
    out_ref[:, 0] = jnp.swapaxes(jnp.stack(outputs, axis=0), 0, 1).astype(bf16)

    @pl.when(step == pairs - 1)
    def _():
        taps = channels * 27
        for copy in late:
            copy.wait()
        folded = 0.0
        cb = jnp.zeros((hidden, 1), f32)
        gconv = jnp.transpose(gconv_t_ref[...])
        for cls in range(8):
            rows = gconv[cls * hidden : (cls + 1) * hidden]
            cb = cb + rows[:, 16 * group : 16 * group + 1]
            rows = jnp.concatenate(split_three(rows[:, : 16 * group]), axis=0)
            folded = folded + dot_rows(rows, tap_ref[cls])
        folded = folded[:hidden] + (folded[hidden : 2 * hidden] + folded[2 * hidden :])
        columns = [folded, cb]
        for ref, share in ((gdb_ref, 1.0), (sq_ref, 1.0 / out_count)):
            total = share * jnp.sum(ref[...], axis=1, keepdims=True)
            columns += [total[:hidden], total[hidden:]]
        columns.append(jnp.zeros((hidden, 2 * lanes - taps - 5), f32))
        small = jnp.concatenate(columns, axis=1) / cell_total
        pieces = jnp.concatenate(split_three(jnp.transpose(gdown_t_ref[...])), axis=0)
        pieces = dot_rows(pieces, order_ref[...])
        grad_down = pieces[:out_count] + (pieces[out_count : 2 * out_count] + pieces[2 * out_count :])
        rows = out_count // len(message_refs)
        small = beside(small, rows)
        here = lax.axis_index("gz") // 2
        whole_ref[...] = grad_down / cell_total
        for far, ref in enumerate(message_refs):
            first = pl.multiple_of((here ^ far) * rows, rows)
            ref[:, : 8 * hidden] = whole_ref[pl.ds(first, rows)]
            ref[:, 8 * hidden :] = small
        sides_of(channels, pairs, outer_ref, conv_t_ref, edge_t_ref, to_before_ref, to_after_ref)


def merged(piece, group):
    halves = [
        piece[par * group : (par + 1) * group]
        + pltpu.roll(piece[(2 + par) * group : (3 + par) * group], 1, 1)
        for par in range(2)
    ]
    return jnp.concatenate(halves, axis=1)


def sides_of(channels, pairs, outer_ref, conv_t_ref, edge_t_ref, before_ref, after_ref):
    group = 4 * channels
    span = 4 * group
    found = []
    for dy in range(2):
        weights = [conv_t_ref[(2 * dz + dy) * span : (2 * dz + dy + 1) * span] for dz in range(2)]
        values = [outer_ref[dy, pair] for pair in range(pairs)]
        found.append(dot(jnp.concatenate(weights, axis=0), jnp.concatenate(values, axis=1)))
    rows = []
    for slot in range(pairs + 1):
        outer = []
        for value in found:
            total = 0.0
            for dz in range(2):
                pair = slot - dz
                if 0 <= pair < pairs:
                    total = total + value[dz * span : (dz + 1) * span, pair * lanes : (pair + 1) * lanes]
            outer.append(merged(total, group))
        rows.append(jnp.concatenate(outer, axis=0))
    width = 2 * lanes
    sides = 0.0
    for value in split_two(jnp.concatenate(rows, axis=1)):
        value = dot(edge_t_ref[...], value).astype(bf16)
        value = [value[:, slot * width : (slot + 1) * width] for slot in range(pairs + 1)]
        sides = sides + dot(jnp.concatenate(value, axis=0), merge_table(2 * lanes))
    for at in range(2 * pairs + 2):
        before_ref[at] = sides[at * 16 : at * 16 + 8].astype(bf16)
        after_ref[at] = sides[at * 16 + 8 : at * 16 + 16].astype(bf16)


def spread_kernel(sizes, *refs):
    channels, depth, half_rows, tile, plan = sizes
    pairs, slots, taken, done, given = plan
    gpre_ref, conv_t_ref, row_t_ref = refs[:3]
    rest = refs[3:-1]
    spread_ref = refs[-1]
    if taken:
        rest, spread_ref = refs[3:-6], refs[-6]
        taken_refs = rest[: len(taken)]
        outer_ref, *far_refs, out_ref = rest[len(taken) :]
        near_refs, sems = refs[-5:-1], refs[-1]
        below_ref, above_ref, before_ref, after_ref = near_refs
    else:
        core_ref, *given_refs = rest
    group = 4 * channels
    span = 4 * group
    row_count = 2 * half_rows
    cells = half_rows * lanes
    step = pl.program_id(0)

    def spread_out(pair):
        for part in range(cells // tile):
            spread = dot(conv_t_ref[...], gpre_ref[0, :, part * tile : (part + 1) * tile])
            for dz in range(2):
                for dy in range(2):
                    first = (2 * dz + dy) * span
                    here = slice(part * tile + dy * lanes, (part + 1) * tile + dy * lanes)
                    spread_ref[slots.index(pair + dz), :, here] += spread[first : first + span]

    def lay_out(at, ch, value):
        z = at - 1
        out_ref[ch, z] = value
        out_ref[ch, z, 0:1] += after_ref[at, ch : ch + 1].astype(f32)
        out_ref[ch, z, row_count - 1 : row_count] += before_ref[at, ch : ch + 1].astype(f32)

    def finish(slot):
        rows = [
            merged(spread_ref[slots.index(slot), :, row * lanes : (row + 1) * lanes], group)
            for row in range(half_rows + 1)
        ]
        core = 0.0
        for value in split_two(jnp.concatenate(rows, axis=0)):
            core = core + dot(dot(row_t_ref[...], value).astype(bf16), merge_table(2 * lanes))
        for par in range(2):
            for ch in range(channels):
                first = (par * channels + ch) * row_count
                value = core[first : first + row_count]
                if taken:
                    lay_out(2 * slot + par, ch, value)
                else:
                    core_ref[2 * done.index(slot) + par, ch] = value

    for k, pair in enumerate(pairs):

        @pl.when(step == k)
        def _():
            if k == 0:
                for slot in slots:
                    if slot in taken:
                        spread_ref[slots.index(slot)] = taken_refs[taken.index(slot)][...]
                    else:
                        spread_ref[slots.index(slot)] = jnp.zeros(spread_ref.shape[1:], f32)
            if k == 0 and taken:
                fetched(list(zip(far_refs, near_refs, strict=True)), sems)
                for ch in range(channels):
                    lay_out(1, ch, outer_ref[1, ch] + above_ref[ch].astype(f32))
                    lay_out(depth, ch, outer_ref[2, ch] + below_ref[ch].astype(f32))
            for slot in done:
                if k > 0 and pairs[k - 1] in (slot - 1, slot) and not set(pairs[k:]) & {slot - 1, slot}:
                    finish(slot)
            spread_out(pair)
            if k == len(pairs) - 1:
                for slot in done:
                    if pair in (slot - 1, slot):
                        finish(slot)
                if not taken:
                    for slot, ref in zip(given, given_refs, strict=True):
                        ref[...] = spread_ref[slots.index(slot)]


def last_kernel(sizes, *refs):
    hidden, taps, big, parts = sizes
    conv_out, cbias_out, down_out, dbias_out, loss_out, here_ref, sems = refs[parts:]
    fetched([(ref, here_ref.at[i]) for i, ref in enumerate(refs[:parts])], sems)
    total = here_ref[0]
    for i in range(1, parts):
        total = total + here_ref[i]
    down_out[...] = total[:, :big]
    small = total[:, big:]
    while small.shape[0] < hidden:
        small = jnp.concatenate(jnp.split(small, 2, axis=1), axis=0)
    conv_out[...] = small[:, :taps]
    turned = jnp.transpose(small[:, lanes:])
    at = taps - lanes
    cbias_out[...] = turned[at : at + 1]
    dbias_out[...] = jnp.concatenate([turned[at + 1 : at + 2], turned[at + 2 : at + 3]], axis=1)
    loss_out[...] = jnp.sum(turned[at + 3 : at + 4] + turned[at + 4 : at + 5], axis=1, keepdims=True)


def call(kernel, sizes, out_shape, *args, grid=None, in_specs=None, out_specs=None, scratch=(), flops=0, vmem=16, name):
    if grid is None:
        grid = (1,)
        in_specs = [whole(a.shape) for a in args]
        out_specs = [whole(o.shape) for o in out_shape]
    return pl.pallas_call(
        functools.partial(kernel, sizes),
        out_shape=out_shape,
        in_specs=in_specs,
        out_specs=out_specs,
        scratch_shapes=scratch,
        compiler_params=pltpu.CompilerParams(vmem_limit_bytes=vmem * 1024 * 1024),
        cost_estimate=pl.CostEstimate(
            flops=flops,
            bytes_accessed=sum(a.size * a.dtype.itemsize for a in (*args, *out_shape)),
            transcendentals=0,
        ),
        name=name,
        grid=grid,
    )(*args)


def whole(shape):
    return pl.BlockSpec(tuple(shape), lambda z: (0,) * len(shape))


def constants(channels, row_count, hidden):
    core, edge = row_spread(channels, row_count)
    names = {
        "row": core,
        "row_t": core.T,
        "edge": edge,
        "edge_t": edge.T,
        "tap": tap_spread(channels),
        "order": class_order(hidden),
    }
    return {name: jnp.asarray(value, bf16) for name, value in names.items()}


def outer_rows(fields):
    channels, depth, row_count, col_count = fields.shape
    out = jax.ShapeDtypeStruct((depth, 8, col_count), fields.dtype)
    block = (channels, depth, 16, col_count)
    return call(
        rows_kernel,
        (channels, depth),
        [out, out],
        fields, fields,
        grid=(1,),
        in_specs=[
            pl.BlockSpec(block, lambda z: (0, 0, 0, 0)),
            pl.BlockSpec(block, lambda z: (0, 0, row_count // 16 - 1, 0)),
        ],
        out_specs=[whole(out.shape)] * 2,
        name="rows",
    )


def more_rows(first_rows, last_rows, below, above):
    depth, _, col_count = first_rows.shape
    out = jax.ShapeDtypeStruct((depth + 2, 8, col_count), first_rows.dtype)
    args = (first_rows, last_rows, below, above)
    return call(
        more_rows_kernel,
        (below.shape[0], depth),
        [out, out],
        *args,
        grid=(1,),
        in_specs=[pl.BlockSpec(memory_space=pl.ANY)] * 4,
        out_specs=[whole(out.shape)] * 2,
        scratch=[pltpu.VMEM(a.shape, a.dtype) for a in args] + [pltpu.SemaphoreType.DMA((4,))],
        name="more_rows",
    )


def prepare(fields, below, above, conv_weight, conv_bias, down_weight, fixed):
    channels, depth, row_count, _ = fields.shape
    hidden, out_count = conv_weight.shape[0], down_weight.shape[0]
    pairs, half_rows = depth // 2, row_count // 2
    big, win = 8 * hidden, 64 * channels
    return call(
        prepare_kernel,
        (channels, pairs, half_rows, hidden),
        [
            jax.ShapeDtypeStruct((pairs + 1, 16 * channels, (half_rows + 1) * lanes), bf16),
            jax.ShapeDtypeStruct((big, win + 16), bf16),
            jax.ShapeDtypeStruct((win, big), bf16),
            jax.ShapeDtypeStruct((out_count, big), bf16),
            jax.ShapeDtypeStruct((big, out_count), bf16),
        ],
        fields, below, above, conv_weight, conv_bias[None], down_weight,
        fixed["tap"], fixed["order"], fixed["row"],
        flops=2 * fields.size * row_count * channels * 4,
        name="prepare",
    )


def forward(early, before, after, target, conv, conv_t, down, down_t, down_bias, fixed, channels, cell_total, groups):
    out_count, pairs, half_rows, half_cols = target.shape
    win, big = conv_t.shape
    hidden = big // 8
    cells = half_rows * half_cols
    args = (
        early, before, after, target, conv, conv_t, down, down_t, down_bias[None],
        fixed["tap"], fixed["order"], fixed["edge"], fixed["edge_t"],
    )
    slab = pl.BlockSpec((out_count, 1, half_rows, half_cols), lambda z: (0, z, 0, 0))
    rows = out_count // groups
    message = jax.ShapeDtypeStruct((rows, big + 2 * lanes * hidden // rows), f32)
    in_specs = [whole(a.shape) for a in args]
    for i in (0, 9, 10):
        in_specs[i] = pl.BlockSpec(memory_space=pl.ANY)
    for i in (1, 2):
        in_specs[i] = pl.BlockSpec(memory_space=pl.ANY)
    in_specs[3] = slab
    return call(
        forward_kernel,
        (channels, pairs, half_rows, hidden, out_count, forward_tile, cell_total, groups),
        [
            jax.ShapeDtypeStruct(target.shape, bf16),
            jax.ShapeDtypeStruct((pairs, big, cells), bf16),
            jax.ShapeDtypeStruct(before.shape, bf16),
            jax.ShapeDtypeStruct(after.shape, bf16),
        ]
        + [message] * groups,
        *args,
        grid=(pairs,),
        in_specs=in_specs,
        out_specs=[
            slab,
            pl.BlockSpec((1, big, cells), lambda z: (z, 0, 0)),
            whole(before.shape),
            whole(after.shape),
        ]
        + [whole(message.shape)] * groups,
        scratch=[
            pltpu.VMEM(early.shape, bf16),
            pltpu.VMEM((big, out_count), f32),
            pltpu.VMEM((win + 16, big), f32),
            pltpu.VMEM((out_count, lanes), f32),
            pltpu.VMEM((out_count, lanes), f32),
            pltpu.VMEM((2, big, forward_tile), bf16),
            pltpu.VMEM((2, big, forward_tile), f32),
            pltpu.VMEM((out_count, big), f32),
            pltpu.VMEM((2, pairs, big, lanes), bf16),
            pltpu.VMEM(fixed["tap"].shape, bf16),
            pltpu.VMEM(fixed["order"].shape, bf16),
            pltpu.VMEM((pairs + 1, 2, 16 * channels, lanes), f32),
            pltpu.VMEM(before.shape, bf16),
            pltpu.VMEM(after.shape, bf16),
            pltpu.SemaphoreType.DMA((pairs + 1,)),
            pltpu.SemaphoreType.DMA((4,)),
        ],
        flops=4 * pairs * cells * big * (win + out_count),
        vmem=36,
        name="forward",
    )


def spread(grad_pre, conv_t, fixed, shape, plan, taken=(), beside=()):
    channels, depth, row_count, col_count = shape
    _, big, cells = grad_pre.shape
    pairs, slots, _, done, given = plan
    open_shape = (16 * channels, cells + lanes)
    args = (grad_pre, conv_t, fixed["row_t"], *taken, *beside)
    if taken:
        outs = [jax.ShapeDtypeStruct(shape, f32)]
    else:
        outs = [jax.ShapeDtypeStruct((2 * len(done), channels, row_count, col_count), f32)]
    outs += [jax.ShapeDtypeStruct(open_shape, f32)] * len(given)
    first = pairs[0]
    stride = pairs[1] - first if len(pairs) > 1 else 1
    return call(
        spread_kernel,
        (channels, depth, row_count // 2, spread_tile, plan),
        outs,
        *args,
        grid=(len(pairs),),
        in_specs=[pl.BlockSpec((1, big, cells), lambda z: (first + stride * z, 0, 0))]
        + [whole(a.shape) for a in args[1 : len(args) - len(beside[1:])]]
        + [pl.BlockSpec(memory_space=pl.ANY) for _ in beside[1:]],
        out_specs=[whole(o.shape) for o in outs],
        scratch=[pltpu.VMEM((len(slots), *open_shape), f32)]
        + [pltpu.VMEM(a.shape, a.dtype) for a in beside[1:]]
        + ([pltpu.SemaphoreType.DMA((len(beside) - 1,))] if beside else []),
        flops=2 * len(pairs) * cells * big * conv_t.shape[0],
        vmem=20,
        name="spread",
    )


forward_tile = 1024
spread_tile = 1024


def on_device(fields, target, conv_weight, conv_bias, down_weight, down_bias):
    channels, depth, row_count, col_count = fields.shape
    hidden = conv_weight.shape[0]
    out_count = down_weight.shape[0]
    taps = channels * 27
    big = 8 * hidden
    cell_total = fields.size // channels // 8 * lax.axis_size("gz") * lax.axis_size("gy")
    fixed = constants(channels, row_count, hidden)

    below = shifted(fields[:, depth - 1], "gz", 1)
    above = shifted(fields[:, 0], "gz", -1)
    first_rows, last_rows = more_rows(*outer_rows(fields), below, above)
    before = shifted(last_rows, "gy", 1)
    after = shifted(first_rows, "gy", -1)
    early, conv_big, conv_t, down_big, down_t = prepare(
        fields, below, above, conv_weight, conv_bias, down_weight, fixed
    )
    groups = lax.axis_size("gz") // 2
    out_field, grad_pre, to_before, to_after, *messages = forward(
        early, before, after, target, conv_big, conv_t, down_big, down_t, down_bias, fixed, channels, cell_total, groups
    )
    pairs = depth // 2
    shape = fields.shape

    got = [exchanged(message, "gz", 2 * far) for far, message in enumerate(messages) if far > 0]
    from_before = shifted(to_after, "gy", 1)
    from_after = shifted(to_before, "gy", -1)
    outer = ((0, pairs - 1), (0, 1, pairs - 1, pairs), (), (0, pairs), (1, pairs - 1))
    outer_core, low_open, high_open = spread(grad_pre, conv_t, fixed, shape, outer)
    packed = sum(got, messages[0])

    def plane(value, at):
        low = from_before[at, :channels, None].astype(f32)
        high = from_after[at, :channels, None].astype(f32)
        gap = jnp.zeros((channels, row_count - 2, col_count), f32)
        return (value + jnp.concatenate([low, gap, high], axis=1)).astype(bf16)

    from_below = shifted(plane(outer_core[3], depth + 1), "gz", 1)
    from_above = shifted(plane(outer_core[0], 0), "gz", -1)
    count = packed.shape[0] // 2
    core = lax.axis_index("gz") % 2
    own, small = packed[:, :big], beside(packed[:, big:], count)
    give = lax.dynamic_slice_in_dim(own, (1 - core) * count, count, 0)
    own = lax.dynamic_slice_in_dim(own, core * count, count, 0)
    packed = jnp.concatenate([own, small], axis=1) + exchanged(jnp.concatenate([give, small], axis=1), "gz", 1)

    packed, low_open = lax.optimization_barrier((packed, low_open))
    got = [exchanged(packed, "gy", far) for far in range(1, lax.axis_size("gy"))]
    inner = tuple(range(1, pairs - 1)), tuple(range(1, pairs)), (1, pairs - 1), tuple(range(1, pairs)), ()
    (sensitivity,) = spread(
        grad_pre, conv_t, fixed, shape, inner, (low_open, high_open),
        (outer_core, from_above, from_below, from_after, from_before),
    )
    conv, cbias, down, dbias, loss = call(
        last_kernel,
        (hidden, taps, big, 1 + len(got)),
        [
            jax.ShapeDtypeStruct((hidden, taps), f32),
            jax.ShapeDtypeStruct((1, hidden), f32),
            jax.ShapeDtypeStruct((count, big), f32),
            jax.ShapeDtypeStruct((1, out_count), f32),
            jax.ShapeDtypeStruct((1, 1), f32),
        ],
        packed, *got,
        grid=(1,),
        in_specs=[pl.BlockSpec(memory_space=pl.ANY)] * (1 + len(got)),
        out_specs=[pl.BlockSpec(memory_space=pltpu.VMEM)] * 5,
        scratch=[pltpu.VMEM((1 + len(got), *packed.shape), f32), pltpu.SemaphoreType.DMA((1 + len(got),))],
        name="last",
    )
    return out_field, sensitivity, conv, cbias[0], down, dbias[0], loss[0, 0]


def solution(mesh):
    in_specs = (P(None, "gz", "gy", None), P(None, "gz", "gy", None), P(), P(), P(), P())
    out_specs = (
        P(None, "gz", "gy", None),
        P(None, "gz", "gy", None),
        P(),
        P(),
        P("gz", None),
        P(),
        P(),
    )
    return jax.shard_map(
        on_device, mesh=mesh, in_specs=in_specs, out_specs=out_specs, check_vma=False
    )
```

```python
import functools

import jax
import jax.numpy as jnp
import numpy as np
from jax import lax
from jax.experimental import pallas as pl
from jax.experimental.pallas import tpu as pltpu
from jax.sharding import PartitionSpec as P

gelu_scale = 0.7978845608028654
gelu_cubic = 0.044715
lanes = 128
bf16 = jnp.bfloat16
f32 = jnp.float32


def shifted(value, axis, by):
    count = lax.axis_size(axis)
    return lax.ppermute(value, axis, [(i, (i + by) % count) for i in range(count)])


def exchanged(value, axis, bit):
    count = lax.axis_size(axis)
    return lax.ppermute(value, axis, [(i, i ^ bit) for i in range(count)])


def merge_table(width, turned=False):
    place = lax.broadcasted_iota(jnp.int32, (width, width), 1 if turned else 0)
    found = lax.broadcasted_iota(jnp.int32, (width, width), 0 if turned else 1)
    half = width // 2
    at = jnp.where(place < half, 2 * place - 1, 2 * (place - half))
    at = jnp.where(at < 0, width - 1, at)
    return jnp.where(found == at, 1.0, 0.0).astype(bf16)


def row_spread(channels, row_count):
    pair_rows = row_count // 2 + 1
    core = np.zeros((pair_rows * 4 * channels, 2 * channels * row_count), np.float32)
    edge = np.zeros((8 * channels, 32), np.float32)
    for par_z in range(2):
        for ch in range(channels):
            for at in range(1, row_count + 1):
                target = ((at // 2 * 2 + par_z) * 2 + at % 2) * channels + ch
                core[target, (par_z * channels + ch) * row_count + at - 1] = 1
            edge[(par_z * 2) * channels + ch, par_z * 16 + ch] = 1
            edge[((2 + par_z) * 2 + 1) * channels + ch, par_z * 16 + 8 + ch] = 1
    return core, edge


def tap_spread(channels):
    spread = np.zeros((8, channels * 27, 64 * channels), np.float32)
    for cls in range(8):
        par_z, par_y, par_x = cls // 4, cls // 2 % 2, cls % 2
        for ch in range(channels):
            for off_z in range(3):
                for off_y in range(3):
                    for off_x in range(3):
                        at_z, at_y, at_x = par_z + off_z, par_y + off_y, par_x + off_x
                        place = (at_z // 2 * 2 + at_y // 2) * 2 + at_x // 2
                        place = ((place * 2 + at_x % 2) * 2 + at_z % 2) * 2 + at_y % 2
                        spread[cls, ch * 27 + 9 * off_z + 3 * off_y + off_x, place * channels + ch] = 1
    return spread


def class_order(hidden):
    order = np.zeros((8 * hidden, 8 * hidden), np.float32)
    for ch in range(hidden):
        for cls in range(8):
            order[ch * 8 + cls, cls * hidden + ch] = 1
    return order


def dot(a, b):
    return jnp.dot(a, b, preferred_element_type=f32)


def dot_rows(a, b):
    return lax.dot_general(a, b, (((1,), (1,)), ((), ())), preferred_element_type=f32)


def split_two(value):
    high = value.astype(bf16)
    return high, (value - high.astype(f32)).astype(bf16)


def split_three(value):
    high = value.astype(bf16)
    return (high,) + split_two(value - high.astype(f32))


def beside(value, count):
    while value.shape[0] > count:
        value = jnp.concatenate(jnp.split(value, 2, axis=0), axis=1)
    return value


def conv_rows(conv_ref, tap_ref):
    return jnp.concatenate([dot(conv_ref[...], tap_ref[cls]) for cls in range(8)], axis=0)


def row_of(ref, count):
    return jnp.transpose(jnp.broadcast_to(ref[...], (lanes, count)))


def fetched(pairs_of_refs, sems):
    copies = [pltpu.make_async_copy(*refs, sems.at[i]) for i, refs in enumerate(pairs_of_refs)]
    for copy in copies:
        copy.start()
    for copy in copies:
        copy.wait()


def rows_kernel(sizes, low_ref, high_ref, first_out, last_out):
    channels, depth = sizes
    for ref, at, out in ((low_ref, 0, first_out), (high_ref, 15, last_out)):
        for z in range(depth):
            rows = [ref[ch, z].astype(f32)[at : at + 1] for ch in range(channels)]
            rows.append(jnp.zeros((8 - channels, rows[0].shape[1]), f32))
            out[z] = jnp.concatenate(rows, axis=0).astype(bf16)


def more_rows_kernel(sizes, *refs):
    channels, depth = sizes
    first_out, last_out, first_ref, last_ref, below_ref, above_ref, sems = refs[4:]
    fetched(list(zip(refs[:4], (first_ref, last_ref, below_ref, above_ref), strict=True)), sems)
    count = below_ref.shape[1]
    for ref, at, out in ((first_ref, 0, first_out), (last_ref, count - 1, last_out)):
        out[1 : depth + 1] = ref[...]
        for z, plane_ref in ((0, below_ref), (depth + 1, above_ref)):
            rows = [plane_ref[ch].astype(f32)[at : at + 1] for ch in range(channels)]
            rows.append(jnp.zeros((8 - channels, rows[0].shape[1]), f32))
            out[z] = jnp.concatenate(rows, axis=0).astype(bf16)


def prepare_kernel(
    sizes,
    field_ref,
    below_ref,
    above_ref,
    conv_weight_ref,
    conv_bias_ref,
    down_weight_ref,
    tap_ref,
    order_ref,
    row_ref,
    split_ref,
    conv_ref,
    conv_t_ref,
    down_ref,
    down_t_ref,
):
    channels, pairs, half_rows, hidden = sizes
    group = 4 * channels
    conv = conv_rows(conv_weight_ref, tap_ref)
    conv_t_ref[...] = jnp.transpose(conv).astype(bf16)
    conv_ref[:, : 16 * group] = (0.5 * conv).astype(bf16)
    bias = 0.5 * row_of(conv_bias_ref, hidden)
    at = lax.broadcasted_iota(jnp.int32, bias.shape, 1)
    columns = jnp.zeros_like(bias)
    for k, piece in enumerate(split_three(bias)):
        columns = jnp.where(at == k, piece.astype(f32), columns)
    columns = jnp.concatenate([columns[:, :16]] * 8, axis=0)
    conv_ref[:, 16 * group :] = columns.astype(bf16)
    down = dot(down_weight_ref[...], order_ref[...])
    down_ref[...] = down.astype(bf16)
    down_t_ref[...] = jnp.transpose(down).astype(bf16)
    for slot in range(pairs + 1):
        lower = below_ref if slot == 0 else field_ref.at[:, 2 * slot - 1]
        upper = above_ref if slot == pairs else field_ref.at[:, 2 * slot]
        rows = [ref[ch] for ref in (lower, upper) for ch in range(channels)]
        rows = dot(row_ref[...], jnp.concatenate(rows, axis=0)).astype(bf16)
        rows = dot(rows, merge_table(2 * lanes, turned=True))
        for row in range(half_rows + 1):
            piece = rows[row * group : (row + 1) * group]
            split_ref[slot, :, row * lanes : (row + 1) * lanes] = shifts_of(piece).astype(bf16)


def shifts_of(piece):
    piece = jnp.concatenate([piece[:, :lanes], piece[:, lanes:]], axis=0)
    return jnp.concatenate([piece, pltpu.roll(piece, lanes - 1, 1)], axis=0)


def forward_kernel(
    sizes,
    early_ref,
    far_before_ref,
    far_after_ref,
    target_ref,
    conv_ref,
    conv_t_ref,
    down_ref,
    down_t_ref,
    down_bias_ref,
    far_tap_ref,
    far_order_ref,
    edge_ref,
    edge_t_ref,
    out_ref,
    gpre_ref,
    to_before_ref,
    to_after_ref,
    *rest,
):
    channels, pairs, half_rows, hidden, out_count, tile, cell_total, groups = sizes
    message_refs = rest[:groups]
    (
    split_ref,
    gdown_t_ref,
    gconv_t_ref,
    gdb_ref,
    sq_ref,
    hid_ref,
    slope_ref,
    whole_ref,
    outer_ref,
    tap_ref,
    order_ref,
    sides_ref,
    before_ref,
    after_ref,
    split_sem,
    late_sem,
    ) = rest[groups:]
    group = 4 * channels
    cells = half_rows * lanes
    step = pl.program_id(0)

    def arrival(slot):
        return pltpu.make_async_copy(early_ref.at[slot], split_ref.at[slot], split_sem.at[slot])

    late = [
        pltpu.make_async_copy(far_tap_ref, tap_ref, late_sem.at[0]),
        pltpu.make_async_copy(far_order_ref, order_ref, late_sem.at[1]),
    ]

    def complete(slot):
        arrival(slot).wait()
        for side, row in enumerate((0, half_rows)):
            here = slice(row * lanes, (row + 1) * lanes)
            value = split_ref[slot, :, here].astype(f32) + sides_ref[slot, side]
            split_ref[slot, :, here] = value.astype(bf16)

    @pl.when(step == 0)
    def _():
        sides = [
            pltpu.make_async_copy(far_before_ref, before_ref, late_sem.at[2]),
            pltpu.make_async_copy(far_after_ref, after_ref, late_sem.at[3]),
        ]
        for copy in sides:
            copy.start()
        for slot in range(pairs + 1):
            arrival(slot).start()
        for copy in late:
            copy.start()
        gdown_t_ref[...] = jnp.zeros_like(gdown_t_ref)
        gconv_t_ref[...] = jnp.zeros_like(gconv_t_ref)
        gdb_ref[...] = jnp.zeros_like(gdb_ref)
        sq_ref[...] = jnp.zeros_like(sq_ref)
        width = 2 * lanes
        rows = []
        for copy in sides:
            copy.wait()
        for slot in range(pairs + 1):
            sides = [ref[2 * slot + par].astype(f32) for par in range(2) for ref in (before_ref, after_ref)]
            rows.append(jnp.concatenate(sides, axis=0).astype(bf16))
        rows = dot(edge_ref[...], jnp.concatenate(rows, axis=1)).astype(bf16)
        rows = [rows[:, slot * width : (slot + 1) * width] for slot in range(pairs + 1)]
        rows = dot(jnp.concatenate(rows, axis=0), merge_table(2 * lanes, turned=True))
        for slot in range(pairs + 1):
            for side in range(2):
                first = (2 * slot + side) * group
                sides_ref[slot, side] = shifts_of(rows[first : first + group])
        complete(0)

    complete(step + 1)

    ones = jnp.ones((16, tile), bf16)
    down_bias = row_of(down_bias_ref, out_count)
    down_bias = jnp.concatenate([down_bias] * (tile // lanes), axis=1)
    wanted = jnp.swapaxes(target_ref[:, 0].astype(f32), 0, 1)
    parts = cells // tile
    count = tile // lanes

    def window_of(part):
        start, stop = part * tile, (part + 1) * tile
        return jnp.concatenate(
            [
                split_ref[step + dz, :, start + dy * lanes : stop + dy * lanes]
                for dz in range(2)
                for dy in range(2)
            ]
            + [ones],
            axis=0,
        )

    outputs, diffs = {}, {}

    def activate(part, rows):
        pre = dot(conv_ref[rows], window_of(part))
        square = pre * pre
        tangent = jnp.tanh(pre * (square * (8.0 * gelu_scale * gelu_cubic) + 2.0 * gelu_scale))
        above = 1.0 + tangent
        bend = pre * (square * (12.0 * gelu_scale * gelu_cubic) + gelu_scale)
        hid_ref[part % 2, rows] = (pre * above).astype(bf16)
        slope_ref[part % 2, rows] = above * ((1.0 - tangent) * bend + 0.5)

    def compare(part):
        output = dot(down_ref[...], hid_ref[part % 2]) + down_bias
        first = part * count
        diff = output - jnp.concatenate([wanted[first + k] for k in range(count)], axis=1)
        outputs[part] = [output[:, k * lanes : (k + 1) * lanes] for k in range(count)]
        for k in range(count):
            piece = diff[:, k * lanes : (k + 1) * lanes]
            gdb_ref[...] += piece
            sq_ref[...] += piece * piece
        diffs[part] = diff.astype(bf16)

    def weigh_down(part):
        gdown_t_ref[...] += dot_rows(hid_ref[part % 2], diffs[part])

    def back(part, rows):
        value = dot(down_t_ref[rows], diffs[part]) * slope_ref[part % 2, rows]
        gpre_ref[0, rows, part * tile : (part + 1) * tile] = value.astype(bf16)

    def weigh_conv(part):
        gconv_t_ref[...] += dot_rows(window_of(part), gpre_ref[0, :, part * tile : (part + 1) * tile])

    big = 8 * hidden
    blocks = [slice(0, big)]
    for part in range(parts + 1):
        first = [functools.partial(activate, part, rows) for rows in blocks] if part < parts else []
        second = []
        if part > 0:
            done = part - 1
            second = [functools.partial(compare, done), functools.partial(weigh_down, done)]
            second += [functools.partial(back, done, rows) for rows in blocks]
            second += [functools.partial(weigh_conv, done)]
        for k in range(max(len(first), len(second))):
            if k < len(second):
                second[k]()
            if k < len(first):
                first[k]()
    for side, at in enumerate((0, cells - lanes)):
        outer_ref[side, step] = gpre_ref[0, :, at : at + lanes]
    outputs = [value for part in range(parts) for value in outputs[part]]
    out_ref[:, 0] = jnp.swapaxes(jnp.stack(outputs, axis=0), 0, 1).astype(bf16)

    @pl.when(step == pairs - 1)
    def _():
        taps = channels * 27
        for copy in late:
            copy.wait()
        folded = 0.0
        cb = jnp.zeros((hidden, 1), f32)
        gconv = jnp.transpose(gconv_t_ref[...])
        for cls in range(8):
            rows = gconv[cls * hidden : (cls + 1) * hidden]
            cb = cb + rows[:, 16 * group : 16 * group + 1]
            rows = jnp.concatenate(split_three(rows[:, : 16 * group]), axis=0)
            folded = folded + dot_rows(rows, tap_ref[cls])
        folded = folded[:hidden] + (folded[hidden : 2 * hidden] + folded[2 * hidden :])
        columns = [folded, cb]
        for ref, share in ((gdb_ref, 1.0), (sq_ref, 1.0 / out_count)):
            total = share * jnp.sum(ref[...], axis=1, keepdims=True)
            columns += [total[:hidden], total[hidden:]]
        columns.append(jnp.zeros((hidden, 2 * lanes - taps - 5), f32))
        small = jnp.concatenate(columns, axis=1) / cell_total
        pieces = jnp.concatenate(split_three(jnp.transpose(gdown_t_ref[...])), axis=0)
        pieces = dot_rows(pieces, order_ref[...])
        grad_down = pieces[:out_count] + (pieces[out_count : 2 * out_count] + pieces[2 * out_count :])
        rows = out_count // len(message_refs)
        small = beside(small, rows)
        here = lax.axis_index("gz") // 2
        whole_ref[...] = grad_down / cell_total
        for far, ref in enumerate(message_refs):
            first = pl.multiple_of((here ^ far) * rows, rows)
            ref[:, : 8 * hidden] = whole_ref[pl.ds(first, rows)]
            ref[:, 8 * hidden :] = small
        sides_of(channels, pairs, outer_ref, conv_t_ref, edge_t_ref, to_before_ref, to_after_ref)


def merged(piece, group):
    halves = [
        piece[par * group : (par + 1) * group]
        + pltpu.roll(piece[(2 + par) * group : (3 + par) * group], 1, 1)
        for par in range(2)
    ]
    return jnp.concatenate(halves, axis=1)


def sides_of(channels, pairs, outer_ref, conv_t_ref, edge_t_ref, before_ref, after_ref):
    group = 4 * channels
    span = 4 * group
    found = []
    for dy in range(2):
        weights = [conv_t_ref[(2 * dz + dy) * span : (2 * dz + dy + 1) * span] for dz in range(2)]
        values = [outer_ref[dy, pair] for pair in range(pairs)]
        found.append(dot(jnp.concatenate(weights, axis=0), jnp.concatenate(values, axis=1)))
    rows = []
    for slot in range(pairs + 1):
        outer = []
        for value in found:
            total = 0.0
            for dz in range(2):
                pair = slot - dz
                if 0 <= pair < pairs:
                    total = total + value[dz * span : (dz + 1) * span, pair * lanes : (pair + 1) * lanes]
            outer.append(merged(total, group))
        rows.append(jnp.concatenate(outer, axis=0))
    width = 2 * lanes
    sides = 0.0
    for value in split_two(jnp.concatenate(rows, axis=1)):
        value = dot(edge_t_ref[...], value).astype(bf16)
        value = [value[:, slot * width : (slot + 1) * width] for slot in range(pairs + 1)]
        sides = sides + dot(jnp.concatenate(value, axis=0), merge_table(2 * lanes))
    for at in range(2 * pairs + 2):
        before_ref[at] = sides[at * 16 : at * 16 + 8].astype(bf16)
        after_ref[at] = sides[at * 16 + 8 : at * 16 + 16].astype(bf16)


def spread_kernel(sizes, *refs):
    channels, depth, half_rows, tile, plan = sizes
    pairs, slots, taken, done, given = plan
    gpre_ref, conv_t_ref, row_t_ref = refs[:3]
    rest = refs[3:-1]
    spread_ref = refs[-1]
    if taken:
        rest, spread_ref = refs[3:-6], refs[-6]
        taken_refs = rest[: len(taken)]
        outer_ref, *far_refs, out_ref = rest[len(taken) :]
        near_refs, sems = refs[-5:-1], refs[-1]
        below_ref, above_ref, before_ref, after_ref = near_refs
    else:
        core_ref, *given_refs = rest
    group = 4 * channels
    span = 4 * group
    row_count = 2 * half_rows
    cells = half_rows * lanes
    step = pl.program_id(0)

    def spread_out(pair):
        for part in range(cells // tile):
            spread = dot(conv_t_ref[...], gpre_ref[0, :, part * tile : (part + 1) * tile])
            for dz in range(2):
                for dy in range(2):
                    first = (2 * dz + dy) * span
                    here = slice(part * tile + dy * lanes, (part + 1) * tile + dy * lanes)
                    spread_ref[slots.index(pair + dz), :, here] += spread[first : first + span]

    def lay_out(at, ch, value):
        z = at - 1
        out_ref[ch, z] = value
        out_ref[ch, z, 0:1] += after_ref[at, ch : ch + 1].astype(f32)
        out_ref[ch, z, row_count - 1 : row_count] += before_ref[at, ch : ch + 1].astype(f32)

    def finish(slot):
        rows = [
            merged(spread_ref[slots.index(slot), :, row * lanes : (row + 1) * lanes], group)
            for row in range(half_rows + 1)
        ]
        core = 0.0
        for value in split_two(jnp.concatenate(rows, axis=0)):
            core = core + dot(dot(row_t_ref[...], value).astype(bf16), merge_table(2 * lanes))
        for par in range(2):
            for ch in range(channels):
                first = (par * channels + ch) * row_count
                value = core[first : first + row_count]
                if taken:
                    lay_out(2 * slot + par, ch, value)
                else:
                    core_ref[2 * done.index(slot) + par, ch] = value

    for k, pair in enumerate(pairs):

        @pl.when(step == k)
        def _():
            if k == 0:
                for slot in slots:
                    if slot in taken:
                        spread_ref[slots.index(slot)] = taken_refs[taken.index(slot)][...]
                    else:
                        spread_ref[slots.index(slot)] = jnp.zeros(spread_ref.shape[1:], f32)
            if k == 0 and taken:
                fetched(list(zip(far_refs, near_refs, strict=True)), sems)
                for ch in range(channels):
                    lay_out(1, ch, outer_ref[1, ch] + above_ref[ch].astype(f32))
                    lay_out(2, ch, outer_ref[2, ch])
                    lay_out(3, ch, outer_ref[3, ch])
                    lay_out(depth, ch, outer_ref[4, ch] + below_ref[ch].astype(f32))
            for slot in done:
                if k > 0 and pairs[k - 1] in (slot - 1, slot) and not set(pairs[k:]) & {slot - 1, slot}:
                    finish(slot)
            spread_out(pair)
            if k == len(pairs) - 1:
                for slot in done:
                    if pair in (slot - 1, slot):
                        finish(slot)
                if not taken:
                    for slot, ref in zip(given, given_refs, strict=True):
                        ref[...] = spread_ref[slots.index(slot)]


def last_kernel(sizes, *refs):
    hidden, taps, big, parts = sizes
    conv_out, cbias_out, down_out, dbias_out, loss_out, here_ref, sems = refs[parts:]
    fetched([(ref, here_ref.at[i]) for i, ref in enumerate(refs[:parts])], sems)
    total = here_ref[0]
    for i in range(1, parts):
        total = total + here_ref[i]
    down_out[...] = total[:, :big]
    small = total[:, big:]
    while small.shape[0] < hidden:
        small = jnp.concatenate(jnp.split(small, 2, axis=1), axis=0)
    conv_out[...] = small[:, :taps]
    turned = jnp.transpose(small[:, lanes:])
    at = taps - lanes
    cbias_out[...] = turned[at : at + 1]
    dbias_out[...] = jnp.concatenate([turned[at + 1 : at + 2], turned[at + 2 : at + 3]], axis=1)
    loss_out[...] = jnp.sum(turned[at + 3 : at + 4] + turned[at + 4 : at + 5], axis=1, keepdims=True)


def call(kernel, sizes, out_shape, *args, grid=None, in_specs=None, out_specs=None, scratch=(), flops=0, vmem=16, name):
    if grid is None:
        grid = (1,)
        in_specs = [whole(a.shape) for a in args]
        out_specs = [whole(o.shape) for o in out_shape]
    return pl.pallas_call(
        functools.partial(kernel, sizes),
        out_shape=out_shape,
        in_specs=in_specs,
        out_specs=out_specs,
        scratch_shapes=scratch,
        compiler_params=pltpu.CompilerParams(vmem_limit_bytes=vmem * 1024 * 1024),
        cost_estimate=pl.CostEstimate(
            flops=flops,
            bytes_accessed=sum(a.size * a.dtype.itemsize for a in (*args, *out_shape)),
            transcendentals=0,
        ),
        name=name,
        grid=grid,
    )(*args)


def whole(shape):
    return pl.BlockSpec(tuple(shape), lambda z: (0,) * len(shape))


def constants(channels, row_count, hidden):
    core, edge = row_spread(channels, row_count)
    names = {
        "row": core,
        "row_t": core.T,
        "edge": edge,
        "edge_t": edge.T,
        "tap": tap_spread(channels),
        "order": class_order(hidden),
    }
    return {name: jnp.asarray(value, bf16) for name, value in names.items()}


def outer_rows(fields):
    channels, depth, row_count, col_count = fields.shape
    out = jax.ShapeDtypeStruct((depth, 8, col_count), fields.dtype)
    block = (channels, depth, 16, col_count)
    return call(
        rows_kernel,
        (channels, depth),
        [out, out],
        fields, fields,
        grid=(1,),
        in_specs=[
            pl.BlockSpec(block, lambda z: (0, 0, 0, 0)),
            pl.BlockSpec(block, lambda z: (0, 0, row_count // 16 - 1, 0)),
        ],
        out_specs=[whole(out.shape)] * 2,
        name="rows",
    )


def more_rows(first_rows, last_rows, below, above):
    depth, _, col_count = first_rows.shape
    out = jax.ShapeDtypeStruct((depth + 2, 8, col_count), first_rows.dtype)
    args = (first_rows, last_rows, below, above)
    return call(
        more_rows_kernel,
        (below.shape[0], depth),
        [out, out],
        *args,
        grid=(1,),
        in_specs=[pl.BlockSpec(memory_space=pl.ANY)] * 4,
        out_specs=[whole(out.shape)] * 2,
        scratch=[pltpu.VMEM(a.shape, a.dtype) for a in args] + [pltpu.SemaphoreType.DMA((4,))],
        name="more_rows",
    )


def prepare(fields, below, above, conv_weight, conv_bias, down_weight, fixed):
    channels, depth, row_count, _ = fields.shape
    hidden, out_count = conv_weight.shape[0], down_weight.shape[0]
    pairs, half_rows = depth // 2, row_count // 2
    big, win = 8 * hidden, 64 * channels
    return call(
        prepare_kernel,
        (channels, pairs, half_rows, hidden),
        [
            jax.ShapeDtypeStruct((pairs + 1, 16 * channels, (half_rows + 1) * lanes), bf16),
            jax.ShapeDtypeStruct((big, win + 16), bf16),
            jax.ShapeDtypeStruct((win, big), bf16),
            jax.ShapeDtypeStruct((out_count, big), bf16),
            jax.ShapeDtypeStruct((big, out_count), bf16),
        ],
        fields, below, above, conv_weight, conv_bias[None], down_weight,
        fixed["tap"], fixed["order"], fixed["row"],
        flops=2 * fields.size * row_count * channels * 4,
        name="prepare",
    )


def forward(early, before, after, target, conv, conv_t, down, down_t, down_bias, fixed, channels, cell_total, groups):
    out_count, pairs, half_rows, half_cols = target.shape
    win, big = conv_t.shape
    hidden = big // 8
    cells = half_rows * half_cols
    args = (
        early, before, after, target, conv, conv_t, down, down_t, down_bias[None],
        fixed["tap"], fixed["order"], fixed["edge"], fixed["edge_t"],
    )
    slab = pl.BlockSpec((out_count, 1, half_rows, half_cols), lambda z: (0, z, 0, 0))
    rows = out_count // groups
    message = jax.ShapeDtypeStruct((rows, big + 2 * lanes * hidden // rows), f32)
    in_specs = [whole(a.shape) for a in args]
    for i in (0, 9, 10):
        in_specs[i] = pl.BlockSpec(memory_space=pl.ANY)
    for i in (1, 2):
        in_specs[i] = pl.BlockSpec(memory_space=pl.ANY)
    in_specs[3] = slab
    return call(
        forward_kernel,
        (channels, pairs, half_rows, hidden, out_count, forward_tile, cell_total, groups),
        [
            jax.ShapeDtypeStruct(target.shape, bf16),
            jax.ShapeDtypeStruct((pairs, big, cells), bf16),
            jax.ShapeDtypeStruct(before.shape, bf16),
            jax.ShapeDtypeStruct(after.shape, bf16),
        ]
        + [message] * groups,
        *args,
        grid=(pairs,),
        in_specs=in_specs,
        out_specs=[
            slab,
            pl.BlockSpec((1, big, cells), lambda z: (z, 0, 0)),
            whole(before.shape),
            whole(after.shape),
        ]
        + [whole(message.shape)] * groups,
        scratch=[
            pltpu.VMEM(early.shape, bf16),
            pltpu.VMEM((big, out_count), f32),
            pltpu.VMEM((win + 16, big), f32),
            pltpu.VMEM((out_count, lanes), f32),
            pltpu.VMEM((out_count, lanes), f32),
            pltpu.VMEM((2, big, forward_tile), bf16),
            pltpu.VMEM((2, big, forward_tile), f32),
            pltpu.VMEM((out_count, big), f32),
            pltpu.VMEM((2, pairs, big, lanes), bf16),
            pltpu.VMEM(fixed["tap"].shape, bf16),
            pltpu.VMEM(fixed["order"].shape, bf16),
            pltpu.VMEM((pairs + 1, 2, 16 * channels, lanes), f32),
            pltpu.VMEM(before.shape, bf16),
            pltpu.VMEM(after.shape, bf16),
            pltpu.SemaphoreType.DMA((pairs + 1,)),
            pltpu.SemaphoreType.DMA((4,)),
        ],
        flops=4 * pairs * cells * big * (win + out_count),
        vmem=36,
        name="forward",
    )


def spread(grad_pre, conv_t, fixed, shape, plan, taken=(), beside=()):
    channels, depth, row_count, col_count = shape
    _, big, cells = grad_pre.shape
    pairs, slots, _, done, given = plan
    open_shape = (16 * channels, cells + lanes)
    args = (grad_pre, conv_t, fixed["row_t"], *taken, *beside)
    if taken:
        outs = [jax.ShapeDtypeStruct(shape, f32)]
    else:
        outs = [jax.ShapeDtypeStruct((2 * len(done), channels, row_count, col_count), f32)]
    outs += [jax.ShapeDtypeStruct(open_shape, f32)] * len(given)

    def block_of(z):
        at = pairs[0]
        for k, pair in enumerate(pairs[1:]):
            at = jnp.where(z == k + 1, pair, at)
        return at, 0, 0

    return call(
        spread_kernel,
        (channels, depth, row_count // 2, spread_tile, plan),
        outs,
        *args,
        grid=(len(pairs),),
        in_specs=[pl.BlockSpec((1, big, cells), block_of)]
        + [whole(a.shape) for a in args[1 : len(args) - len(beside[1:])]]
        + [pl.BlockSpec(memory_space=pl.ANY) for _ in beside[1:]],
        out_specs=[whole(o.shape) for o in outs],
        scratch=[pltpu.VMEM((len(slots), *open_shape), f32)]
        + [pltpu.VMEM(a.shape, a.dtype) for a in beside[1:]]
        + ([pltpu.SemaphoreType.DMA((len(beside) - 1,))] if beside else []),
        flops=2 * len(pairs) * cells * big * conv_t.shape[0],
        vmem=20,
        name="spread",
    )


forward_tile = 1024
spread_tile = 1024


def on_device(fields, target, conv_weight, conv_bias, down_weight, down_bias):
    channels, depth, row_count, col_count = fields.shape
    hidden = conv_weight.shape[0]
    out_count = down_weight.shape[0]
    taps = channels * 27
    big = 8 * hidden
    cell_total = fields.size // channels // 8 * lax.axis_size("gz") * lax.axis_size("gy")
    fixed = constants(channels, row_count, hidden)

    below = shifted(fields[:, depth - 1], "gz", 1)
    above = shifted(fields[:, 0], "gz", -1)
    first_rows, last_rows = more_rows(*outer_rows(fields), below, above)
    before = shifted(last_rows, "gy", 1)
    after = shifted(first_rows, "gy", -1)
    early, conv_big, conv_t, down_big, down_t = prepare(
        fields, below, above, conv_weight, conv_bias, down_weight, fixed
    )
    groups = lax.axis_size("gz") // 2
    out_field, grad_pre, to_before, to_after, *messages = forward(
        early, before, after, target, conv_big, conv_t, down_big, down_t, down_bias, fixed, channels, cell_total, groups
    )
    pairs = depth // 2
    shape = fields.shape

    got = [exchanged(message, "gz", 2 * far) for far, message in enumerate(messages) if far > 0]
    from_before = shifted(to_after, "gy", 1)
    from_after = shifted(to_before, "gy", -1)
    outer = ((0, pairs - 1, 1), (0, 1, 2, pairs - 1, pairs), (), (0, 1, pairs), (2, pairs - 1))
    outer_core, low_open, high_open = spread(grad_pre, conv_t, fixed, shape, outer)
    packed = sum(got, messages[0])

    def plane(value, at):
        low = from_before[at, :channels, None].astype(f32)
        high = from_after[at, :channels, None].astype(f32)
        gap = jnp.zeros((channels, row_count - 2, col_count), f32)
        return (value + jnp.concatenate([low, gap, high], axis=1)).astype(bf16)

    from_below = shifted(plane(outer_core[5], depth + 1), "gz", 1)
    from_above = shifted(plane(outer_core[0], 0), "gz", -1)
    count = packed.shape[0] // 2
    core = lax.axis_index("gz") % 2
    own, small = packed[:, :big], beside(packed[:, big:], count)
    give = lax.dynamic_slice_in_dim(own, (1 - core) * count, count, 0)
    own = lax.dynamic_slice_in_dim(own, core * count, count, 0)
    packed = jnp.concatenate([own, small], axis=1) + exchanged(jnp.concatenate([give, small], axis=1), "gz", 1)

    packed, low_open = lax.optimization_barrier((packed, low_open))
    got = [exchanged(packed, "gy", far) for far in range(1, lax.axis_size("gy"))]
    inner = tuple(range(2, pairs - 1)), tuple(range(2, pairs)), (2, pairs - 1), tuple(range(2, pairs)), ()
    (sensitivity,) = spread(
        grad_pre, conv_t, fixed, shape, inner, (low_open, high_open),
        (outer_core, from_above, from_below, from_after, from_before),
    )
    conv, cbias, down, dbias, loss = call(
        last_kernel,
        (hidden, taps, big, 1 + len(got)),
        [
            jax.ShapeDtypeStruct((hidden, taps), f32),
            jax.ShapeDtypeStruct((1, hidden), f32),
            jax.ShapeDtypeStruct((count, big), f32),
            jax.ShapeDtypeStruct((1, out_count), f32),
            jax.ShapeDtypeStruct((1, 1), f32),
        ],
        packed, *got,
        grid=(1,),
        in_specs=[pl.BlockSpec(memory_space=pl.ANY)] * (1 + len(got)),
        out_specs=[pl.BlockSpec(memory_space=pltpu.VMEM)] * 5,
        scratch=[pltpu.VMEM((1 + len(got), *packed.shape), f32), pltpu.SemaphoreType.DMA((1 + len(got),))],
        name="last",
    )
    return out_field, sensitivity, conv, cbias[0], down, dbias[0], loss[0, 0]


def solution(mesh):
    in_specs = (P(None, "gz", "gy", None), P(None, "gz", "gy", None), P(), P(), P(), P())
    out_specs = (
        P(None, "gz", "gy", None),
        P(None, "gz", "gy", None),
        P(),
        P(),
        P("gz", None),
        P(),
        P(),
    )
    return jax.shard_map(
        on_device, mesh=mesh, in_specs=in_specs, out_specs=out_specs, check_vma=False
    )
```
